128 devices in a mesh: item: 32 (over z, x, core), dim: 4 (over y).
Axes of the slice: x: 4, y: 4, z: 4, core: 2. Of those that a mesh axis runs over, the one named last changes fastest.
Arguments:
- embeddings: float32 [131072, 512], P('item', 'dim'), as said below
- cand_index: int32 [3, 1024], P(None, 'item'), may hold values from 0 to 4095
- cand_count: int32 [3, 32], replicated, may hold values from 1 to 32, 512 in all within a row
Outputs:
- weights: float32 [3, 131072], P(None, ('item', 'dim'))
The draws below stay inside these ranges and needn't reach their ends.
Inputs may be any that keep to these rules, and one draw needn't show every extreme that they name: `cand_index`: row numbers within one index of item's own 4096 rows; unused slots also hold such numbers. `cand_count`: in every round the counts add up to 512 and the largest is exactly 32. `embeddings`: finite values.
All inputs are finite; a program needn't handle non-finite values.
Results may differ from the reference program's by a relative error of at most 0.00018.
Values sent between devices are 32-bit elements; how exact they have to be, the bound alone decides.
A program may use at most 192 MiB of HBM per device.

```python
import math
import jax
import jax.numpy as jnp
import numpy as np
from jax import lax

D = 512
ROWS_DEV = 4096
SLOTS = 32
ROUNDS = 3
TOTAL = 131072
CAND = 1024
N_ITEM = 32


def draw_embeddings(key, part):
    key = jax.random.fold_in(key, 11)
    key_base = jax.random.fold_in(key, 0)
    key_rows = jax.random.fold_in(key, 1)
    key_cols = jax.random.fold_in(key, 2)
    key_far = jax.random.fold_in(key, 4)
    key_pick = jax.random.fold_in(key, 5)
    position = jnp.arange(TOTAL, dtype=jnp.float32)
    rising = jnp.sqrt(1.0 + 2.0 * position / TOTAL)
    row_scale = jnp.exp(0.5 * jnp.log(10.0) * jax.random.uniform(key_rows, (TOTAL,), jnp.float32)) * rising
    row_ids = jnp.arange(TOTAL, dtype=jnp.int32)
    block_ids = row_ids // ROWS_DEV
    chosen = jax.random.randint(key_pick, (TOTAL // ROWS_DEV,), 0, ROWS_DEV, dtype=jnp.int32)
    forced = row_ids % ROWS_DEV == chosen[block_ids]
    spread = jax.random.uniform(key_far, (TOTAL,), jnp.float32) < 0.002
    far_out = jnp.logical_or(forced, spread)
    row_scale = row_scale * jnp.where(far_out, 8.0, 1.0)
    col_scale = jnp.exp(0.25 * jnp.log(10.0) * jax.random.uniform(key_cols, (D,), jnp.float32))
    base = jax.random.normal(key_base, (TOTAL, D), jnp.float32)
    return base * row_scale[:, None] * col_scale[None, :]


def plant(result, rng, low, high):
    longest = result.shape.index(max(result.shape))
    spots = []
    for shift in (0, 1):
        where = [jax.random.randint(jax.random.fold_in(rng, axis), (), 0, length) for axis, length in enumerate(result.shape)]
        where[longest] = (where[longest] + shift) % result.shape[longest]
        spots.append(tuple(where))
    return result.at[spots[0]].set(low).at[spots[1]].set(high)


def split_up(amount, total, most, lean):
    weights = [(1 << 20) // math.isqrt(rank ** lean) + 1 for rank in range(2, amount + 1)]
    rest, counts = total - most - (amount - 1), [1] * (amount - 1)
    while rest > 0:
        movable = [i for i in range(amount - 1) if counts[i] < most]
        whole, budget = sum([weights[i] for i in movable]), rest
        for i in movable:
            addition = min(most - counts[i], max(1, budget * weights[i] // whole), rest)
            counts[i] = counts[i] + addition
            rest = rest - addition
    return np.array([most] + counts)


def ragged(stream_key, number_of, total, reach, slope):
    if number_of == 2:
        one = jax.random.randint(stream_key, (), max(1, total - reach), min(reach, total - 1) + 1)
        return jnp.stack([one, total - one])
    sizes = jnp.asarray(split_up(number_of, total, reach, slope), jnp.int32)
    pairs = (number_of - 1) // 2
    donor, taker = sizes[1:1 + 2 * pairs:2], sizes[2:2 + 2 * pairs:2]
    slack = jnp.minimum(donor - 1, reach - taker)
    shifted = jax.random.randint(jax.random.fold_in(stream_key, 1), (pairs,), 0, 1 << 20) % (slack + 1)
    sizes = sizes.at[1:1 + 2 * pairs:2].set(donor - shifted).at[2:2 + 2 * pairs:2].set(taker + shifted)
    return sizes[jax.random.permutation(jax.random.fold_in(stream_key, 2), number_of)]


def setup_inputs(seed: int = 0) -> dict:
    seeds = jax.random.split(jax.random.key(seed), 4)
    return {
        "embeddings": draw_embeddings(jax.random.fold_in(seeds[3], 71), 0),
        "cand_index": plant(jax.random.randint(seeds[1], (ROUNDS, CAND), 0, ROWS_DEV), jax.random.fold_in(seeds[1], 1), 0, ROWS_DEV - 1).astype(jnp.int32),
        "cand_count": jax.vmap(lambda own: ragged(own, N_ITEM, N_ITEM * SLOTS // 2, SLOTS, 2))(jax.random.split(seeds[2], ROUNDS)).reshape((ROUNDS, N_ITEM)).astype(jnp.int32),
    }


CAP = 4.0


def round_best(embeddings, centers, valid):
    center_norms = jnp.sum(centers * centers, axis=1)
    blocks = embeddings.reshape(-1, ROWS_DEV, D)

    def one_block(block):
        row_norms = jnp.sum(block * block, axis=1)
        dots = jnp.dot(block, centers.T, precision=lax.Precision.HIGHEST)
        distance = jnp.maximum(row_norms[:, None] - 2.0 * dots + center_norms[None, :], 0.0)
        distance = jnp.where(valid[None, :], distance, jnp.inf)
        return jnp.min(distance, axis=1)

    return lax.map(one_block, blocks).reshape(-1)


def reference(embeddings, cand_index, cand_count):
    owners = jnp.arange(N_ITEM, dtype=jnp.int32)[:, None] * ROWS_DEV
    slot_ids = jnp.arange(SLOTS, dtype=jnp.int32)[None, :]
    nearest = jnp.full((TOTAL,), jnp.inf, dtype=jnp.float32)
    results = []
    for step in range(ROUNDS):
        global_rows = (owners + cand_index[step].reshape(N_ITEM, SLOTS)).reshape(-1).astype(jnp.int32)
        valid = (slot_ids < cand_count[step][:, None]).reshape(-1)
        centers = embeddings[global_rows]
        nearest = jnp.minimum(nearest, round_best(embeddings, centers, valid))
        cost = jnp.sum(nearest)
        results.append(jnp.minimum(CAP, TOTAL * nearest / cost))
    return jnp.stack(results)
```

```python
import itertools

import jax
import jax.numpy as jnp
from jax import lax
from jax.experimental import pallas as pl
from jax.experimental.pallas import tpu as pltpu
from jax.sharding import PartitionSpec as P

CAP = 4.0
MESH = pl.DeviceIdType.MESH
ROUNDS = 3
SLOTS = 32
LANES = 128
ROWS = 4096
SHARE = 1024
STEP = 256
PIECES = SHARE // STEP
TOTAL = 131072
STREAM = 512
BF16 = jnp.bfloat16
F32 = jnp.float32


def dot_t(a, b):
    return lax.dot_general(a, b, (((1,), (1,)), ((), ())), preferred_element_type=F32)


def kernel(
    index_ref, count_ref, x_ref, out_ref,
    xv, xfull, relay, cand, ch, cl, nrm, xh, xl, sq, low, part, red_line, red_plane,
    load_sem, send_sem, recv_sem,
):
    item, dim = lax.axis_index("item"), lax.axis_index("dim")
    z, x, core = item // 8, (item // 2) % 4, item % 2
    a = x * (1 - core) + z * core
    b = z * (1 - core) + x * core

    def device(a_, b_):
        return (a_ * (2 + 6 * core) + b_ * (8 - 6 * core) + core, dim)

    def block(r, b_, a_):
        return (((r * 2 + core) * 4 + b_) * 4 + a_) * 4

    a_up, a_down = (a + 1) % 4, (a + 3) % 4
    b_up, b_down = (b + 1) % 4, (b + 3) % 4
    y_up, y_down, y_far = (dim + 1) % 4, (dim + 3) % 4, (dim + 2) % 4
    sibling = (item + 1 - 2 * core, dim)
    rank_line, rank_plane = dim * 2 + core, item // 2

    def line_device(step):
        other = (rank_line + step) % 8
        return (item - core + other % 2, other // 2)

    def plane_device(step):
        return (((rank_plane + step) % 16) * 2 + core, dim)

    load = pltpu.make_async_copy(x_ref, xv, load_sem.at[0])
    load.start()
    own_rows = pltpu.make_async_copy(
        x_ref.at[pl.ds(dim * SHARE, SHARE)], xfull.at[dim], load_sem.at[1]
    )
    own_rows.start()

    barrier = pltpu.get_barrier_semaphore()
    for step in range(1, 8):
        pl.semaphore_signal(barrier, inc=1, device_id=line_device(step), device_id_type=MESH)
    for step in range(1, 16):
        pl.semaphore_signal(barrier, inc=1, device_id=plane_device(step), device_id_type=MESH)

    load.wait()

    def pick(g, carry):
        r, s = g // 4, (g % 4) * 8
        rows = [xv[pl.ds(index_ref[r, s + k], 1), :] for k in range(8)]
        cand[block(r, b, a) + dim, pl.ds(pl.multiple_of(s, 8), 8), :] = jnp.concatenate(rows, axis=0)
        return carry

    lax.fori_loop(0, ROUNDS * 4, pick, 0)
    pl.semaphore_wait(barrier, 22)

    number = itertools.count()
    started = []

    def send(src, dst, target):
        k = next(number)
        copy = pltpu.make_async_remote_copy(
            src_ref=src, dst_ref=dst, send_sem=send_sem.at[k], recv_sem=recv_sem.at[k],
            device_id=target, device_id_type=MESH,
        )
        copy.start()
        started.append(copy)
        return copy

    def send_cand(start, length, target):
        ref = cand.at[pl.ds(start, length)]
        return send(ref, ref, target)

    y_copies = [
        [send_cand(block(r, b, a) + dim, 1, (item, (dim + d) % 4)) for d in (1, 3, 2)]
        for r in range(ROUNDS)
    ]
    half = STEP // 2
    relay_up, relay_down, near_up, near_down = [], [], [], []
    for t in range(PIECES):
        far = y_far * SHARE + t * STEP
        relay_up.append(send(xv.at[pl.ds(far, half)], relay.at[0, t], (item, y_up)))
        relay_down.append(send(xv.at[pl.ds(far + half, half)], relay.at[1, t], (item, y_down)))
        lands = xfull.at[dim, pl.ds(t * STEP, STEP)]
        near_up.append(send(xv.at[pl.ds(y_up * SHARE + t * STEP, STEP)], lands, (item, y_up)))
        near_down.append(send(xv.at[pl.ds(y_down * SHARE + t * STEP, STEP)], lands, (item, y_down)))
    far_up, far_down = [], []

    def pass_rows(t):
        relay_up[t].wait_recv()
        far_up.append(send(relay.at[0, t], xfull.at[y_down, pl.ds(t * STEP, half)], (item, y_up)))
        relay_down[t].wait_recv()
        far_down.append(
            send(relay.at[1, t], xfull.at[y_up, pl.ds(t * STEP + half, half)], (item, y_down))
        )

    first_up, first_down, first_pass, second_up, second_down, second_pass, swap = [], [], [], [], [], [], []

    def first_send(r):
        for copy in y_copies[r]:
            copy.wait_recv()
        first_up.append(send_cand(block(r, b, a), 4, device(a_up, b)))
        first_down.append(send_cand(block(r, b, a), 4, device(a_down, b)))

    def first_forward(r):
        first_up[r].wait_recv()
        up = send_cand(block(r, b, a_down), 2, device(a_up, b))
        first_down[r].wait_recv()
        down = send_cand(block(r, b, a_up) + 2, 2, device(a_down, b))
        first_pass.append((up, down))

    def second_send(r):
        for copy in first_pass[r]:
            copy.wait_recv()
        second_up.append(send_cand(block(r, b, 0), 16, device(a, b_up)))
        second_down.append(send_cand(block(r, b, 0), 16, device(a, b_down)))
        swap.append([send_cand(block(r, b, 0), 16, sibling)])

    def second_forward(r):
        second_up[r].wait_recv()
        up = send_cand(block(r, b_down, 0), 8, device(a, b_up))
        swap[r].append(send_cand(block(r, b_down, 0), 16, sibling))
        second_down[r].wait_recv()
        down = send_cand(block(r, b_up, 0) + 8, 8, device(a, b_down))
        swap[r].append(send_cand(block(r, b_up, 0), 16, sibling))
        second_pass.append((up, down))

    def second_end(r):
        b_far = (b + 2) % 4
        second_pass[r][0].wait_recv()
        swap[r].append(send_cand(block(r, b_far, 0), 8, sibling))
        second_pass[r][1].wait_recv()
        swap[r].append(send_cand(block(r, b_far, 0) + 8, 8, sibling))

    def convert(r):
        for copy in swap[r]:
            copy.wait_recv()

        def one(k, carry):
            c_, b_, a_ = k // 16, (k // 4) % 4, k % 4
            used = count_ref[r, a_ * (2 + 6 * c_) + b_ * (8 - 6 * c_) + c_]
            at = pl.ds(pl.multiple_of(r * 1024 + k * SLOTS, SLOTS), SLOTS)
            total = jnp.zeros((SLOTS, LANES), F32)
            for q in range(4):
                value = cand[(r * 32 + k) * 4 + q]
                total += value * value
                value = -2.0 * value
                high = value.astype(BF16)
                ch[at, q * LANES:(q + 1) * LANES] = high
                cl[at, q * LANES:(q + 1) * LANES] = (value - high.astype(F32)).astype(BF16)
            norm = jnp.broadcast_to(jnp.sum(total, axis=1, keepdims=True), (SLOTS, LANES))
            slot = lax.broadcasted_iota(jnp.int32, (SLOTS, LANES), 0)
            nrm[at, :] = jnp.where(slot < used, norm, jnp.inf)
            return carry

        lax.fori_loop(0, 32, one, 0)

    def prepare(t):
        for copy in (near_up[t], near_down[t], far_up[t], far_down[t]):
            copy.wait_recv()
        at = slice(t * STEP, (t + 1) * STEP)
        total = jnp.zeros((STEP, LANES), F32)
        for q in range(4):
            value = xfull[q, at, :]
            total += value * value
            high = value.astype(BF16)
            xh[at, q * LANES:(q + 1) * LANES] = high
            xl[at, q * LANES:(q + 1) * LANES] = (value - high.astype(F32)).astype(BF16)
        sq[:, at] = jnp.sum(total.T.reshape(LANES // 8, 8, STEP), axis=0)

    def nearest(t, r):
        at = pl.ds(pl.multiple_of(t * STEP, STEP), STEP)
        rows_high, rows_low = xh[at, :], xl[at, :]

        def one(m, best):
            slots = pl.ds(pl.multiple_of(r * 1024 + m * STREAM, STREAM), STREAM)
            high, norm = ch[slots, :], nrm[slots, :]
            value = dot_t(high, rows_high) + dot_t(cl[slots, :], rows_high) + dot_t(high, rows_low)
            value = value + jnp.concatenate([norm] * (STEP // LANES), axis=1)
            return jnp.minimum(best, jnp.min(value.reshape(STREAM // 8, 8, STEP), axis=0))

        low[r, :, at] = lax.fori_loop(0, 1024 // STREAM, one, jnp.full((8, STEP), jnp.inf, F32))

    def many(count, body):
        def one(k, carry):
            body(k)
            return carry

        lax.fori_loop(0, count, one, 0)

    for r in range(ROUNDS):
        first_send(r)
    for r in range(ROUNDS):
        first_forward(r)
    pass_rows(0)
    for r in range(ROUNDS):
        second_send(r)
    pass_rows(1)
    second_forward(0)
    own_rows.wait()
    second_end(0)
    pass_rows(2)
    second_forward(1)
    convert(0)
    prepare(0)
    nearest(0, 0)
    second_end(1)
    second_forward(2)
    pass_rows(3)
    convert(1)
    nearest(0, 1)
    second_end(2)
    prepare(1)
    many(2, lambda r: nearest(1, r))
    convert(2)
    many(2, lambda t: nearest(t, 2))
    for t in range(2, PIECES):
        prepare(t)
        many(ROUNDS, lambda r, t=t: nearest(t, r))

    norm = jnp.sum(sq[...], axis=0, keepdims=True)
    best = [jnp.min(low[r], axis=0, keepdims=True) for r in range(ROUNDS)]
    for r in range(1, ROUNDS):
        best[r] = jnp.minimum(best[r], best[r - 1])
    best = jnp.concatenate([jnp.maximum(value + norm, 0.0) for value in best], axis=0)
    sums = sum([best[:, k * LANES:(k + 1) * LANES] for k in range(SHARE // LANES)])
    part[0] = jnp.concatenate([sums, jnp.zeros((8 - ROUNDS, LANES), F32)], axis=0)
    copies = [send(part.at[0], red_line.at[step - 1], line_device(step)) for step in range(1, 8)]
    line = part[0]
    for step, copy in enumerate(copies):
        copy.wait_recv()
        line = line + red_line[step]
    part[1] = line
    copies = [send(part.at[1], red_plane.at[step - 1], plane_device(step)) for step in range(1, 16)]
    for step, copy in enumerate(copies):
        copy.wait_recv()
        line = line + red_plane[step]
    cost = jnp.sum(line, axis=1, keepdims=True)[:ROUNDS]
    out_ref[...] = jnp.minimum(CAP, TOTAL * best / cost)

    for copy in started:
        copy.wait_send()


COPIES = ROUNDS * 16 + PIECES * 6 + 22


def local(embeddings, cand_index, cand_count):
    return pl.pallas_call(
        kernel,
        out_shape=jax.ShapeDtypeStruct((ROUNDS, SHARE), F32),
        in_specs=[
            pl.BlockSpec(memory_space=pltpu.SMEM),
            pl.BlockSpec(memory_space=pltpu.SMEM),
            pl.BlockSpec(memory_space=pl.ANY),
        ],
        out_specs=pl.BlockSpec(memory_space=pltpu.VMEM),
        scratch_shapes=[
            pltpu.VMEM((ROWS, LANES), F32),
            pltpu.VMEM((4, SHARE, LANES), F32),
            pltpu.VMEM((2, PIECES, STEP // 2, LANES), F32),
            pltpu.VMEM((ROUNDS * 128, SLOTS, LANES), F32),
            pltpu.VMEM((ROUNDS * 1024, 512), BF16),
            pltpu.VMEM((ROUNDS * 1024, 512), BF16),
            pltpu.VMEM((ROUNDS * 1024, LANES), F32),
            pltpu.VMEM((SHARE, 512), BF16),
            pltpu.VMEM((SHARE, 512), BF16),
            pltpu.VMEM((8, SHARE), F32),
            pltpu.VMEM((ROUNDS, 8, SHARE), F32),
            pltpu.VMEM((2, 8, LANES), F32),
            pltpu.VMEM((7, 8, LANES), F32),
            pltpu.VMEM((15, 8, LANES), F32),
            pltpu.SemaphoreType.DMA((2,)),
            pltpu.SemaphoreType.DMA((COPIES,)),
            pltpu.SemaphoreType.DMA((COPIES,)),
        ],
        compiler_params=pltpu.CompilerParams(
            collective_id=0, has_side_effects=True, vmem_limit_bytes=48 * 1024 * 1024
        ),
    )(cand_index, cand_count, embeddings)


def solution(mesh):
    in_specs = (P("item", "dim"), P(None, "item"), P())
    out_specs = P(None, ("item", "dim"))
    return jax.shard_map(local, mesh=mesh, in_specs=in_specs, out_specs=out_specs, check_vma=False)
```

```python
import itertools

import jax
import jax.numpy as jnp
from jax import lax
from jax.experimental import pallas as pl
from jax.experimental.pallas import tpu as pltpu
from jax.sharding import PartitionSpec as P

CAP = 4.0
MESH = pl.DeviceIdType.MESH
ROUNDS = 3
SLOTS = 32
LANES = 128
ROWS = 4096
SHARE = 1024
STEP = 256
PIECES = SHARE // STEP
TOTAL = 131072
HALF = 512
BF16 = jnp.bfloat16
F32 = jnp.float32


def kernel(
    index_ref, count_ref, x_ref, out_ref,
    xv, xfull, relay, cand, ch, cl, nrm, xh, xl, sq, low, part, red_line, red_plane,
    load_sem, send_sem, recv_sem,
):
    item, dim = lax.axis_index("item"), lax.axis_index("dim")
    z, x, core = item // 8, (item // 2) % 4, item % 2
    a = x * (1 - core) + z * core
    b = z * (1 - core) + x * core

    def device(a_, b_):
        return (a_ * (2 + 6 * core) + b_ * (8 - 6 * core) + core, dim)

    def block(r, b_, a_):
        return (((r * 2 + core) * 4 + b_) * 4 + a_) * 4

    a_up, a_down = (a + 1) % 4, (a + 3) % 4
    b_up, b_down = (b + 1) % 4, (b + 3) % 4
    y_up, y_down, y_far = (dim + 1) % 4, (dim + 3) % 4, (dim + 2) % 4
    sibling = (item + 1 - 2 * core, dim)
    rank_line, rank_plane = dim * 2 + core, item // 2

    def line_device(step):
        other = (rank_line + step) % 8
        return (item - core + other % 2, other // 2)

    def plane_device(step):
        return (((rank_plane + step) % 16) * 2 + core, dim)

    load = pltpu.make_async_copy(x_ref, xv, load_sem.at[0])
    load.start()
    own_rows = pltpu.make_async_copy(
        x_ref.at[pl.ds(dim * SHARE, SHARE)], xfull.at[dim], load_sem.at[1]
    )
    own_rows.start()

    barrier = pltpu.get_barrier_semaphore()
    for step in range(1, 8):
        pl.semaphore_signal(barrier, inc=1, device_id=line_device(step), device_id_type=MESH)
    for step in range(1, 16):
        pl.semaphore_signal(barrier, inc=1, device_id=plane_device(step), device_id_type=MESH)

    load.wait()

    def pick(g, carry):
        r, s = g // 4, (g % 4) * 8
        rows = [xv[pl.ds(index_ref[r, s + k], 1), :] for k in range(8)]
        cand[block(r, b, a) + dim, pl.ds(pl.multiple_of(s, 8), 8), :] = jnp.concatenate(rows, axis=0)
        return carry

    lax.fori_loop(0, ROUNDS * 4, pick, 0)
    pl.semaphore_wait(barrier, 22)

    number = itertools.count()
    started = []

    def send(src, dst, target):
        k = next(number)
        copy = pltpu.make_async_remote_copy(
            src_ref=src, dst_ref=dst, send_sem=send_sem.at[k], recv_sem=recv_sem.at[k],
            device_id=target, device_id_type=MESH,
        )
        copy.start()
        started.append(copy)
        return copy

    def send_cand(start, length, target):
        ref = cand.at[pl.ds(start, length)]
        return send(ref, ref, target)

    y_copies = [
        [send_cand(block(r, b, a) + dim, 1, (item, (dim + d) % 4)) for d in (1, 3, 2)]
        for r in range(ROUNDS)
    ]
    half = STEP // 2
    relay_up, relay_down, near_up, near_down = [], [], [], []
    for t in range(PIECES):
        far = y_far * SHARE + t * STEP
        relay_up.append(send(xv.at[pl.ds(far, half)], relay.at[0, t], (item, y_up)))
        relay_down.append(send(xv.at[pl.ds(far + half, half)], relay.at[1, t], (item, y_down)))
        lands = xfull.at[dim, pl.ds(t * STEP, STEP)]
        near_up.append(send(xv.at[pl.ds(y_up * SHARE + t * STEP, STEP)], lands, (item, y_up)))
        near_down.append(send(xv.at[pl.ds(y_down * SHARE + t * STEP, STEP)], lands, (item, y_down)))
    far_up, far_down = [], []

    def pass_rows(t):
        relay_up[t].wait_recv()
        far_up.append(send(relay.at[0, t], xfull.at[y_down, pl.ds(t * STEP, half)], (item, y_up)))
        relay_down[t].wait_recv()
        far_down.append(
            send(relay.at[1, t], xfull.at[y_up, pl.ds(t * STEP + half, half)], (item, y_down))
        )

    first_up, first_down, first_pass, second_up, second_down, second_pass, swap = [], [], [], [], [], [], []

    def first_send(r):
        for copy in y_copies[r]:
            copy.wait_recv()
        first_up.append(send_cand(block(r, b, a), 4, device(a_up, b)))
        first_down.append(send_cand(block(r, b, a), 4, device(a_down, b)))

    def first_forward(r):
        first_up[r].wait_recv()
        up = send_cand(block(r, b, a_down), 2, device(a_up, b))
        first_down[r].wait_recv()
        down = send_cand(block(r, b, a_up) + 2, 2, device(a_down, b))
        first_pass.append((up, down))

    def second_send(r):
        for copy in first_pass[r]:
            copy.wait_recv()
        second_up.append(send_cand(block(r, b, 0), 16, device(a, b_up)))
        second_down.append(send_cand(block(r, b, 0), 16, device(a, b_down)))
        swap.append([send_cand(block(r, b, 0), 16, sibling)])

    def second_forward(r):
        second_up[r].wait_recv()
        up = send_cand(block(r, b_down, 0), 8, device(a, b_up))
        swap[r].append(send_cand(block(r, b_down, 0), 16, sibling))
        second_down[r].wait_recv()
        down = send_cand(block(r, b_up, 0) + 8, 8, device(a, b_down))
        swap[r].append(send_cand(block(r, b_up, 0), 16, sibling))
        second_pass.append((up, down))

    def second_end(r):
        b_far = (b + 2) % 4
        second_pass[r][0].wait_recv()
        swap[r].append(send_cand(block(r, b_far, 0), 8, sibling))
        second_pass[r][1].wait_recv()
        swap[r].append(send_cand(block(r, b_far, 0) + 8, 8, sibling))

    def convert(r, core_, b_):
        def one(a_, carry):
            k = (core_ * 4 + b_) * 4 + a_
            used = count_ref[r, a_ * (2 + 6 * core_) + b_ * (8 - 6 * core_) + core_]
            at = pl.ds(pl.multiple_of(r * 1024 + k * SLOTS, SLOTS), SLOTS)
            total = jnp.zeros((SLOTS, LANES), F32)
            for q in range(4):
                value = cand[(r * 32 + k) * 4 + q]
                total += value * value
                value = -2.0 * value
                high = value.astype(BF16)
                ch[at, q * LANES:(q + 1) * LANES] = high
                cl[at, q * LANES:(q + 1) * LANES] = (value - high.astype(F32)).astype(BF16)
            norm = jnp.broadcast_to(jnp.sum(total, axis=1, keepdims=True), (SLOTS, LANES))
            slot = lax.broadcasted_iota(jnp.int32, (SLOTS, LANES), 0)
            nrm[at, :] = jnp.where(slot < used, norm, jnp.inf)
            return carry

        lax.fori_loop(0, 4, one, 0, unroll=True)

    def prepare(t):
        for copy in (near_up[t], near_down[t], far_up[t], far_down[t]):
            copy.wait_recv()
        total = jnp.zeros((LANES, STEP), F32)
        for q in range(4):
            value = xfull[q, t * STEP:(t + 1) * STEP, :].T
            total += value * value
            high = value.astype(BF16)
            xh[t, q * LANES:(q + 1) * LANES, :] = high
            xl[t, q * LANES:(q + 1) * LANES, :] = (value - high.astype(F32)).astype(BF16)
        sq[:, t * STEP:(t + 1) * STEP] = jnp.sum(total.reshape(LANES // 8, 8, STEP), axis=0)

    def nearest(t, r, core_):
        slots = pl.ds(pl.multiple_of(r * 1024 + core_ * HALF, HALF), HALF)
        high, norm, rows = ch[slots, :], nrm[slots, :], xh[t]
        value = jnp.dot(
            jnp.concatenate([high, cl[slots, :], high], axis=1),
            jnp.concatenate([rows, rows, xl[t]], axis=0),
            preferred_element_type=F32,
        )
        value = value + jnp.concatenate([norm] * (STEP // LANES), axis=1)
        low[r, core_, t] = jnp.min(value.reshape(HALF // 8, 8, STEP), axis=0)

    def many(count, body):
        def one(k, carry):
            body(k)
            return carry

        lax.fori_loop(0, count, one, 0)

    b_far = (b + 2) % 4
    for r in range(ROUNDS):
        first_send(r)
    for r in range(ROUNDS):
        first_forward(r)
    pass_rows(0)
    for r in range(ROUNDS):
        second_send(r)
    pass_rows(1)
    own_rows.wait()
    for r in range(ROUNDS):
        convert(r, core, b)
        second_forward(r)
        convert(r, core, b_down)
        convert(r, core, b_up)
        if r < 2:
            pass_rows(2 + r)
        second_end(r)
        convert(r, core, b_far)
        if r == 0:
            prepare(0)
        else:
            for copy in swap[r - 1]:
                copy.wait_recv()
            many(4, lambda b_, r=r: convert(r - 1, 1 - core, b_))
            many(2, lambda c_, r=r: nearest(0, r - 1, c_))
    for copy in swap[2]:
        copy.wait_recv()
    many(4, lambda b_: convert(2, 1 - core, b_))
    many(2, lambda c_: nearest(0, 2, c_))
    for t in range(1, PIECES):
        if t == PIECES - 1:
            for copy in started:
                copy.wait_send()
            started.clear()
        prepare(t)
        many(ROUNDS * 2, lambda k, t=t: nearest(t, k // 2, k % 2))

    norm = jnp.sum(sq[...], axis=0, keepdims=True)
    best = [
        jnp.concatenate(
            [jnp.min(jnp.minimum(low[r, 0, t], low[r, 1, t]), axis=0, keepdims=True) for t in range(PIECES)],
            axis=1,
        )
        for r in range(ROUNDS)
    ]
    for r in range(1, ROUNDS):
        best[r] = jnp.minimum(best[r], best[r - 1])
    best = jnp.concatenate([jnp.maximum(value + norm, 0.0) for value in best], axis=0)
    sums = sum([best[:, k * LANES:(k + 1) * LANES] for k in range(SHARE // LANES)])
    part[0] = jnp.concatenate([sums, jnp.zeros((8 - ROUNDS, LANES), F32)], axis=0)
    copies = [send(part.at[0], red_line.at[step - 1], line_device(step)) for step in range(1, 8)]
    line = part[0]
    for step, copy in enumerate(copies):
        copy.wait_recv()
        line = line + red_line[step]
    part[1] = line
    copies = [send(part.at[1], red_plane.at[step - 1], plane_device(step)) for step in range(1, 16)]
    for step, copy in enumerate(copies):
        copy.wait_recv()
        line = line + red_plane[step]
    cost = jnp.sum(line, axis=1, keepdims=True)[:ROUNDS]
    out_ref[...] = jnp.minimum(CAP, TOTAL * best / cost)

    for copy in started:
        copy.wait_send()


COPIES = ROUNDS * 16 + PIECES * 6 + 22


def local(embeddings, cand_index, cand_count):
    return pl.pallas_call(
        kernel,
        out_shape=jax.ShapeDtypeStruct((ROUNDS, SHARE), F32),
        in_specs=[
            pl.BlockSpec(memory_space=pltpu.SMEM),
            pl.BlockSpec(memory_space=pltpu.SMEM),
            pl.BlockSpec(memory_space=pl.ANY),
        ],
        out_specs=pl.BlockSpec(memory_space=pltpu.VMEM),
        scratch_shapes=[
            pltpu.VMEM((ROWS, LANES), F32),
            pltpu.VMEM((4, SHARE, LANES), F32),
            pltpu.VMEM((2, PIECES, STEP // 2, LANES), F32),
            pltpu.VMEM((ROUNDS * 128, SLOTS, LANES), F32),
            pltpu.VMEM((ROUNDS * 1024, 512), BF16),
            pltpu.VMEM((ROUNDS * 1024, 512), BF16),
            pltpu.VMEM((ROUNDS * 1024, LANES), F32),
            pltpu.VMEM((PIECES, 512, STEP), BF16),
            pltpu.VMEM((PIECES, 512, STEP), BF16),
            pltpu.VMEM((8, SHARE), F32),
            pltpu.VMEM((ROUNDS, 2, PIECES, 8, STEP), F32),
            pltpu.VMEM((2, 8, LANES), F32),
            pltpu.VMEM((7, 8, LANES), F32),
            pltpu.VMEM((15, 8, LANES), F32),
            pltpu.SemaphoreType.DMA((2,)),
            pltpu.SemaphoreType.DMA((COPIES,)),
            pltpu.SemaphoreType.DMA((COPIES,)),
        ],
        compiler_params=pltpu.CompilerParams(
            collective_id=0, has_side_effects=True, vmem_limit_bytes=56 * 1024 * 1024
        ),
    )(cand_index, cand_count, embeddings)


def solution(mesh):
    in_specs = (P("item", "dim"), P(None, "item"), P())
    out_specs = P(None, ("item", "dim"))
    return jax.shard_map(local, mesh=mesh, in_specs=in_specs, out_specs=out_specs, check_vma=False)
```

```python
import itertools

import jax
import jax.numpy as jnp
from jax import lax
from jax.experimental import pallas as pl
from jax.experimental.pallas import tpu as pltpu
from jax.sharding import PartitionSpec as P

CAP = 4.0
MESH = pl.DeviceIdType.MESH
ROUNDS = 3
SLOTS = 32
LANES = 128
ROWS = 4096
SHARE = 1024
STEP = 256
PIECES = SHARE // STEP
TOTAL = 131072
USED = 512
BF16 = jnp.bfloat16
F32 = jnp.float32


def exchange(index_ref, x_ref, xfull, cand, xv, picked, relay, load_sem, send_sem, recv_sem):
    item, dim = lax.axis_index("item"), lax.axis_index("dim")
    z, x, core = item // 8, (item // 2) % 4, item % 2
    a = x * (1 - core) + z * core
    b = z * (1 - core) + x * core

    def device(a_, b_):
        return (a_ * (2 + 6 * core) + b_ * (8 - 6 * core) + core, dim)

    def block(r, b_, a_):
        return (((r * 2 + core) * 4 + b_) * 4 + a_) * 4

    a_up, a_down = (a + 1) % 4, (a + 3) % 4
    b_up, b_down, b_far = (b + 1) % 4, (b + 3) % 4, (b + 2) % 4
    y_up, y_down, y_far = (dim + 1) % 4, (dim + 3) % 4, (dim + 2) % 4
    sibling = (item + 1 - 2 * core, dim)
    load = pltpu.make_async_copy(x_ref, xv, load_sem.at[0])
    load.start()
    own_rows = pltpu.make_async_copy(
        x_ref.at[pl.ds(dim * SHARE, SHARE)], xfull.at[dim], load_sem.at[1]
    )
    own_rows.start()

    barrier = pltpu.get_barrier_semaphore()
    partners = [(item, y_up), (item, y_down), (item, y_far), sibling]
    partners += [device(a_up, b), device(a_down, b), device(a, b_up), device(a, b_down)]
    for partner in partners:
        pl.semaphore_signal(barrier, inc=1, device_id=partner, device_id_type=MESH)

    load.wait()

    def pick(g, carry):
        r, s = g // 4, (g % 4) * 8
        rows = [xv[pl.ds(index_ref[r, s + k], 1), :] for k in range(8)]
        picked[r, pl.ds(pl.multiple_of(s, 8), 8), :] = jnp.concatenate(rows, axis=0)
        return carry

    lax.fori_loop(0, ROUNDS * 4, pick, 0)
    pl.semaphore_wait(barrier, len(partners))

    number = itertools.count()
    started = []

    def send(src, dst, target):
        k = next(number)
        copy = pltpu.make_async_remote_copy(
            src_ref=src, dst_ref=dst, send_sem=send_sem.at[k], recv_sem=recv_sem.at[k],
            device_id=target, device_id_type=MESH,
        )
        copy.start()
        started.append(copy)
        return copy

    def send_cand(start, length, target):
        ref = cand.at[pl.ds(start, length)]
        return send(ref, ref, target)

    def send_picked(r, target):
        return send(picked.at[pl.ds(r, 1)], cand.at[pl.ds(block(r, b, a) + dim, 1)], target)

    y_copies = [[send_picked(r, (item, (dim + d) % 4)) for d in (1, 3, 2)] for r in range(ROUNDS)]
    own_picked = [
        pltpu.make_async_copy(
            picked.at[pl.ds(r, 1)], cand.at[pl.ds(block(r, b, a) + dim, 1)], load_sem.at[2 + r]
        )
        for r in range(ROUNDS)
    ]
    for copy in own_picked:
        copy.start()
    half = STEP // 2
    relay_up, relay_down, near_up, near_down = [], [], [], []
    for t in range(PIECES):
        far = y_far * SHARE + t * STEP
        relay_up.append(send(xv.at[pl.ds(far, half)], relay.at[0, t], (item, y_up)))
        relay_down.append(send(xv.at[pl.ds(far + half, half)], relay.at[1, t], (item, y_down)))
        lands = xfull.at[dim, pl.ds(t * STEP, STEP)]
        near_up.append(send(xv.at[pl.ds(y_up * SHARE + t * STEP, STEP)], lands, (item, y_up)))
        near_down.append(send(xv.at[pl.ds(y_down * SHARE + t * STEP, STEP)], lands, (item, y_down)))
    far_up, far_down = [], []

    def pass_rows(t):
        relay_up[t].wait_recv()
        far_up.append(send(relay.at[0, t], xfull.at[y_down, pl.ds(t * STEP, half)], (item, y_up)))
        relay_down[t].wait_recv()
        far_down.append(
            send(relay.at[1, t], xfull.at[y_up, pl.ds(t * STEP + half, half)], (item, y_down))
        )

    first_up, first_down, first_pass, second_up, second_down, second_pass, swap = [], [], [], [], [], [], []

    def first_send(r):
        own_picked[r].wait()
        for copy in y_copies[r]:
            copy.wait_recv()
        first_up.append(send_cand(block(r, b, a), 4, device(a_up, b)))
        first_down.append(send_cand(block(r, b, a), 4, device(a_down, b)))

    def first_forward(r):
        first_up[r].wait_recv()
        up = send_cand(block(r, b, a_down), 2, device(a_up, b))
        first_down[r].wait_recv()
        down = send_cand(block(r, b, a_up) + 2, 2, device(a_down, b))
        first_pass.append((up, down))

    def second_send(r):
        for copy in first_pass[r]:
            copy.wait_recv()
        second_up.append(send_cand(block(r, b, 0), 16, device(a, b_up)))
        second_down.append(send_cand(block(r, b, 0), 16, device(a, b_down)))
        swap.append([send_cand(block(r, b, 0), 16, sibling)])

    def second_forward(r):
        second_up[r].wait_recv()
        up = send_cand(block(r, b_down, 0), 8, device(a, b_up))
        swap[r].append(send_cand(block(r, b_down, 0), 16, sibling))
        second_down[r].wait_recv()
        down = send_cand(block(r, b_up, 0) + 8, 8, device(a, b_down))
        swap[r].append(send_cand(block(r, b_up, 0), 16, sibling))
        second_pass.append((up, down))

    def second_end(r):
        second_pass[r][0].wait_recv()
        swap[r].append(send_cand(block(r, b_far, 0), 8, sibling))
        second_pass[r][1].wait_recv()
        swap[r].append(send_cand(block(r, b_far, 0) + 8, 8, sibling))

    for r in range(ROUNDS):
        first_send(r)
    for r in range(ROUNDS):
        first_forward(r)
    pass_rows(0)
    for r in range(ROUNDS):
        second_send(r)
    pass_rows(1)
    own_rows.wait()
    for r in range(ROUNDS):
        second_forward(r)
        if r < 2:
            pass_rows(2 + r)
        second_end(r)
    for copies in swap + [near_up, near_down, far_up, far_down]:
        for copy in copies:
            copy.wait_recv()
    for copy in started:
        copy.wait_send()


def distances(count_ref, cand_ref, x_ref, out_ref, xv, cv, squeezed, ch, cl, nrm, xh, xl, sq, low, load_sem):
    loads = [pltpu.make_async_copy(x_ref, xv, load_sem.at[ROUNDS])]
    for r in range(ROUNDS):
        at = pl.ds(r * 128, 128)
        loads.append(pltpu.make_async_copy(cand_ref.at[at], cv.at[at], load_sem.at[r]))
    for load in loads:
        load.start()

    loads[0].wait()

    def prepare(t, carry):
        at = pl.ds(pl.multiple_of(t * STEP, STEP), STEP)
        total = jnp.zeros((LANES, STEP), F32)
        for q in range(4):
            value = xv[q, at, :].T
            total += value * value
            high = value.astype(BF16)
            xh[t, q * LANES:(q + 1) * LANES, :] = high
            xl[t, q * LANES:(q + 1) * LANES, :] = (value - high.astype(F32)).astype(BF16)
        sq[t] = jnp.sum(total.reshape(LANES // 8, 8, STEP), axis=0)
        return carry

    lax.fori_loop(0, PIECES, prepare, 0)

    for r in range(ROUNDS):
        loads[r + 1].wait()

        def squeeze(k, start):
            core_, b_, a_ = k // 16, (k // 4) % 4, k % 4
            for q in range(4):
                squeezed[q, pl.ds(start, SLOTS), :] = cv[(r * 32 + k) * 4 + q]
            return start + count_ref[r, a_ * (2 + 6 * core_) + b_ * (8 - 6 * core_) + core_]

        lax.fori_loop(0, 32, squeeze, 0)

        def convert(k, carry):
            at = pl.ds(pl.multiple_of(k * 64, 64), 64)
            total = jnp.zeros((64, LANES), F32)
            for q in range(4):
                value = squeezed[q, at, :]
                total += value * value
                value = -2.0 * value
                high = value.astype(BF16)
                ch[at, q * LANES:(q + 1) * LANES] = high
                cl[at, q * LANES:(q + 1) * LANES] = (value - high.astype(F32)).astype(BF16)
            nrm[at, :] = jnp.broadcast_to(jnp.sum(total, axis=1, keepdims=True), (64, LANES))
            return carry

        lax.fori_loop(0, USED // 64, convert, 0)

        def nearest(t, carry):
            high, rows = ch[...], xh[t]
            value = jnp.dot(
                jnp.concatenate([high, cl[...], high], axis=1),
                jnp.concatenate([rows, rows, xl[t]], axis=0),
                preferred_element_type=F32,
            )
            value = value + jnp.concatenate([nrm[...]] * (STEP // LANES), axis=1)
            low[r, t] = jnp.min(value.reshape(USED // 8, 8, STEP), axis=0)
            return carry

        lax.fori_loop(0, PIECES, nearest, 0)

    def along(parts):
        return jnp.concatenate(parts, axis=1)

    norm = along([jnp.sum(sq[t], axis=0, keepdims=True) for t in range(PIECES)])
    best = [along([jnp.min(low[r, t], axis=0, keepdims=True) for t in range(PIECES)]) for r in range(ROUNDS)]
    for r in range(1, ROUNDS):
        best[r] = jnp.minimum(best[r], best[r - 1])
    out_ref[...] = jnp.concatenate([jnp.maximum(value + norm, 0.0) for value in best], axis=0)


def scale(best_ref, out_ref, part, red_line, red_plane, send_sem, recv_sem):
    item, dim = lax.axis_index("item"), lax.axis_index("dim")
    core = item % 2
    rank_line, rank_plane = dim * 2 + core, item // 2

    def line_device(step):
        other = (rank_line + step) % 8
        return (item - core + other % 2, other // 2)

    def plane_device(step):
        return (((rank_plane + step) % 16) * 2 + core, dim)

    barrier = pltpu.get_barrier_semaphore()
    for step in range(1, 8):
        pl.semaphore_signal(barrier, inc=1, device_id=line_device(step), device_id_type=MESH)
    for step in range(1, 16):
        pl.semaphore_signal(barrier, inc=1, device_id=plane_device(step), device_id_type=MESH)
    best = best_ref[...]
    sums = sum([best[:, k * LANES:(k + 1) * LANES] for k in range(SHARE // LANES)])
    line = jnp.concatenate([sums, jnp.zeros((8 - ROUNDS, LANES), F32)], axis=0)
    pl.semaphore_wait(barrier, 22)

    copies = []

    def send(src, dst, target):
        k = len(copies)
        copy = pltpu.make_async_remote_copy(
            src_ref=src, dst_ref=dst, send_sem=send_sem.at[k], recv_sem=recv_sem.at[k],
            device_id=target, device_id_type=MESH,
        )
        copy.start()
        copies.append(copy)

    part[0] = line
    for step in range(1, 8):
        send(part.at[0], red_line.at[step - 1], line_device(step))
    for step in range(7):
        copies[step].wait_recv()
        line = line + red_line[step]
    part[1] = line
    for step in range(1, 16):
        send(part.at[1], red_plane.at[step - 1], plane_device(step))
    for step in range(15):
        copies[7 + step].wait_recv()
        line = line + red_plane[step]
    cost = jnp.sum(line, axis=1, keepdims=True)[:ROUNDS]
    out_ref[...] = jnp.minimum(CAP, TOTAL * best / cost)
    for copy in copies:
        copy.wait_send()


COPIES = ROUNDS * 16 + PIECES * 6
REDUCES = 22
SMEM = pl.BlockSpec(memory_space=pltpu.SMEM)
VMEM = pl.BlockSpec(memory_space=pltpu.VMEM)
ANY = pl.BlockSpec(memory_space=pl.ANY)
MIB = 1024 * 1024


def local(embeddings, cand_index, cand_count):
    rows, candidates = pl.pallas_call(
        exchange,
        out_shape=(
            jax.ShapeDtypeStruct((4, SHARE, LANES), F32),
            jax.ShapeDtypeStruct((ROUNDS * 128, SLOTS, LANES), F32),
        ),
        in_specs=[SMEM, ANY],
        out_specs=(ANY, ANY),
        scratch_shapes=[
            pltpu.VMEM((ROWS, LANES), F32),
            pltpu.VMEM((ROUNDS, SLOTS, LANES), F32),
            pltpu.VMEM((2, PIECES, STEP // 2, LANES), F32),
            pltpu.SemaphoreType.DMA((2 + ROUNDS,)),
            pltpu.SemaphoreType.DMA((COPIES,)),
            pltpu.SemaphoreType.DMA((COPIES,)),
        ],
        compiler_params=pltpu.CompilerParams(
            collective_id=0, has_side_effects=True, vmem_limit_bytes=56 * MIB
        ),
    )(cand_index, embeddings)
    best = pl.pallas_call(
        distances,
        out_shape=jax.ShapeDtypeStruct((ROUNDS, SHARE), F32),
        in_specs=[SMEM, ANY, ANY],
        out_specs=VMEM,
        scratch_shapes=[
            pltpu.VMEM((4, SHARE, LANES), F32),
            pltpu.VMEM((ROUNDS * 128, SLOTS, LANES), F32),
            pltpu.VMEM((4, USED + SLOTS, LANES), F32),
            pltpu.VMEM((USED, 512), BF16),
            pltpu.VMEM((USED, 512), BF16),
            pltpu.VMEM((USED, LANES), F32),
            pltpu.VMEM((PIECES, 512, STEP), BF16),
            pltpu.VMEM((PIECES, 512, STEP), BF16),
            pltpu.VMEM((PIECES, 8, STEP), F32),
            pltpu.VMEM((ROUNDS, PIECES, 8, STEP), F32),
            pltpu.SemaphoreType.DMA((ROUNDS + 1,)),
        ],
        compiler_params=pltpu.CompilerParams(vmem_limit_bytes=56 * MIB),
    )(cand_count, candidates, rows)
    return pl.pallas_call(
        scale,
        out_shape=jax.ShapeDtypeStruct((ROUNDS, SHARE), F32),
        in_specs=[VMEM],
        out_specs=VMEM,
        scratch_shapes=[
            pltpu.VMEM((2, 8, LANES), F32),
            pltpu.VMEM((7, 8, LANES), F32),
            pltpu.VMEM((15, 8, LANES), F32),
            pltpu.SemaphoreType.DMA((REDUCES,)),
            pltpu.SemaphoreType.DMA((REDUCES,)),
        ],
        compiler_params=pltpu.CompilerParams(collective_id=1, has_side_effects=True),
    )(best)


def solution(mesh):
    in_specs = (P("item", "dim"), P(None, "item"), P())
    out_specs = P(None, ("item", "dim"))
    return jax.shard_map(local, mesh=mesh, in_specs=in_specs, out_specs=out_specs, check_vma=False)
```

```python
import itertools

import jax
import jax.numpy as jnp
from jax import lax
from jax.experimental import pallas as pl
from jax.experimental.pallas import tpu as pltpu
from jax.sharding import PartitionSpec as P

CAP = 4.0
MESH = pl.DeviceIdType.MESH
ROUNDS = 3
SLOTS = 32
LANES = 128
ROWS = 4096
SHARE = 1024
STEP = 256
PIECES = SHARE // STEP
TOTAL = 131072
TILES = 92
USED = TILES * 8
BF16 = jnp.bfloat16
F32 = jnp.float32


def exchange(index_ref, x_ref, xfull, cand_0, cand_1, cand_2, xv, picked, relay, load_sem, send_sem, recv_sem):
    cand = (cand_0, cand_1, cand_2)
    item, dim = lax.axis_index("item"), lax.axis_index("dim")
    z, x, core = item // 8, (item // 2) % 4, item % 2
    a = x * (1 - core) + z * core
    b = z * (1 - core) + x * core

    def device(a_, b_):
        return (a_ * (2 + 6 * core) + b_ * (8 - 6 * core) + core, dim)

    def block(b_, a_):
        return ((core * 4 + b_) * 4 + a_) * 4

    a_up, a_down, a_far = (a + 1) % 4, (a + 3) % 4, (a + 2) % 4
    b_up, b_down, b_far = (b + 1) % 4, (b + 3) % 4, (b + 2) % 4
    y_up, y_down, y_far = (dim + 1) % 4, (dim + 3) % 4, (dim + 2) % 4
    sibling = (item + 1 - 2 * core, dim)
    load = pltpu.make_async_copy(x_ref, xv, load_sem.at[0])
    load.start()
    own_rows = pltpu.make_async_copy(
        x_ref.at[pl.ds(dim * SHARE, SHARE)], xfull.at[dim], load_sem.at[1]
    )
    own_rows.start()

    barrier = pltpu.get_barrier_semaphore()
    partners = [(item, y_up), (item, y_down), (item, y_far), sibling]
    partners += [device(a_up, b), device(a_down, b), device(a_far, b), device(a, b_up), device(a, b_down)]
    for partner in partners:
        pl.semaphore_signal(barrier, inc=1, device_id=partner, device_id_type=MESH)

    load.wait()

    def pick(g, carry):
        r, s = g // 4, (g % 4) * 8
        rows = [xv[pl.ds(index_ref[r, s + k], 1), :] for k in range(8)]
        picked[r, pl.ds(pl.multiple_of(s, 8), 8), :] = jnp.concatenate(rows, axis=0)
        return carry

    lax.fori_loop(0, ROUNDS * 4, pick, 0)
    pl.semaphore_wait(barrier, len(partners))

    number = itertools.count()
    started = []

    def send(src, dst, target):
        k = next(number)
        copy = pltpu.make_async_remote_copy(
            src_ref=src, dst_ref=dst, send_sem=send_sem.at[k], recv_sem=recv_sem.at[k],
            device_id=target, device_id_type=MESH,
        )
        copy.start()
        started.append(copy)
        return copy

    def send_cand(r, start, length, target):
        ref = cand[r].at[pl.ds(start, length)]
        return send(ref, ref, target)

    def send_picked(r, target):
        return send(picked.at[pl.ds(r, 1)], cand[r].at[pl.ds(block(b, a) + dim, 1)], target)

    y_copies = [[send_picked(r, (item, (dim + d) % 4)) for d in (1, 3, 2)] for r in range(ROUNDS)]
    own_picked = [
        pltpu.make_async_copy(
            picked.at[pl.ds(r, 1)], cand[r].at[pl.ds(block(b, a) + dim, 1)], load_sem.at[2 + r]
        )
        for r in range(ROUNDS)
    ]
    for copy in own_picked:
        copy.start()
    half = STEP // 2
    relay_up, relay_down, near, passed = [], [], [], []

    def send_near(t):
        lands = xfull.at[dim, pl.ds(t * STEP, STEP)]
        near.append((
            send(xv.at[pl.ds(y_up * SHARE + t * STEP, STEP)], lands, (item, y_up)),
            send(xv.at[pl.ds(y_down * SHARE + t * STEP, STEP)], lands, (item, y_down)),
        ))

    for t in range(PIECES):
        far = y_far * SHARE + t * STEP
        relay_up.append(send(xv.at[pl.ds(far, half)], relay.at[0, t], (item, y_up)))
        relay_down.append(send(xv.at[pl.ds(far + half, half)], relay.at[1, t], (item, y_down)))
    send_near(0)

    def pass_rows(t):
        relay_up[t].wait_recv()
        up = send(relay.at[0, t], xfull.at[y_down, pl.ds(t * STEP, half)], (item, y_up))
        relay_down[t].wait_recv()
        down = send(relay.at[1, t], xfull.at[y_up, pl.ds(t * STEP + half, half)], (item, y_down))
        passed.append((up, down))

    first, second_up, second_down, second_pass, swap = [], [], [], [], []

    def first_send(r):
        own_picked[r].wait()
        for copy in y_copies[r]:
            copy.wait_recv()
        first.append([send_cand(r, block(b, a), 4, device(a_, b)) for a_ in (a_up, a_down, a_far)])

    def second_send(r):
        for copy in first[r]:
            copy.wait_recv()
        second_up.append(send_cand(r, block(b, 0), 16, device(a, b_up)))
        second_down.append(send_cand(r, block(b, 0), 16, device(a, b_down)))
        swap.append([send_cand(r, block(b, 0), 16, sibling)])

    def second_forward(r):
        second_up[r].wait_recv()
        up = send_cand(r, block(b_down, 0), 8, device(a, b_up))
        swap[r].append(send_cand(r, block(b_down, 0), 16, sibling))
        second_down[r].wait_recv()
        down = send_cand(r, block(b_up, 0) + 8, 8, device(a, b_down))
        swap[r].append(send_cand(r, block(b_up, 0), 16, sibling))
        second_pass.append((up, down))

    def second_end(r):
        second_pass[r][0].wait_recv()
        swap[r].append(send_cand(r, block(b_far, 0), 8, sibling))
        second_pass[r][1].wait_recv()
        swap[r].append(send_cand(r, block(b_far, 0) + 8, 8, sibling))

    for r in range(ROUNDS):
        first_send(r)
    pass_rows(0)
    send_near(1)
    second_send(0)
    pass_rows(1)
    send_near(2)
    second_send(1)
    pass_rows(2)
    send_near(3)
    pass_rows(3)
    second_forward(0)
    second_send(2)
    second_end(0)
    second_forward(1)
    second_end(1)
    second_forward(2)
    second_end(2)
    own_rows.wait()
    for copies in swap + near + passed:
        for copy in copies:
            copy.wait_recv()
    for copy in started:
        copy.wait_send()


def distances(count_ref, cand_0, cand_1, cand_2, x_ref, out_ref, xv, table, cv, ch, cl, nrm, xh, xl, sq, low, load_sem):
    loads = [pltpu.make_async_copy(x_ref, xv, load_sem.at[ROUNDS])]
    for r, ref in enumerate((cand_0, cand_1, cand_2)):
        loads.append(pltpu.make_async_copy(ref, cv.at[r], load_sem.at[r]))
    for load in loads:
        load.start()

    for r in range(ROUNDS):
        def entry(p, carry):
            k, o = carry
            core_, b_, a_ = k // 16, (k // 4) % 4, k % 4
            count = count_ref[r, a_ * (2 + 6 * core_) + b_ * (8 - 6 * core_) + core_]
            count = jnp.where(k < 32, count, 0)
            table[r, p] = jnp.minimum(k, 31) * 128 + o * 8
            table[ROUNDS + r, p] = count - o * 8
            more = o * 8 + 8 < count
            return jnp.where(more, k, jnp.minimum(k + 1, 32)), jnp.where(more, o + 1, 0)

        lax.fori_loop(0, TILES, entry, (jnp.int32(0), jnp.int32(0)))

    loads[0].wait()

    def prepare(t, carry):
        at = pl.ds(pl.multiple_of(t * STEP, STEP), STEP)
        total = jnp.zeros((LANES, STEP), F32)
        for q in range(4):
            value = xv[q, at, :].T
            total += value * value
            high = value.astype(BF16)
            xh[t, q * LANES:(q + 1) * LANES, :] = high
            xl[t, q * LANES:(q + 1) * LANES, :] = (value - high.astype(F32)).astype(BF16)
        sq[t] = jnp.sum(total.reshape(LANES // 8, 8, STEP), axis=0)
        return carry

    lax.fori_loop(0, PIECES, prepare, 0)

    for r in range(ROUNDS):
        loads[r + 1].wait()

        def convert(g, carry):
            at = pl.ds(pl.multiple_of(g * 16, 16), 16)
            place = [table[r, g * 2 + k] for k in range(2)]
            total = jnp.zeros((16, LANES), F32)
            for q in range(4):
                value = jnp.concatenate(
                    [cv[r, pl.ds(pl.multiple_of(p + q * SLOTS, 8), 8), :] for p in place], axis=0
                )
                total += value * value
                value = -2.0 * value
                high = value.astype(BF16)
                ch[at, q * LANES:(q + 1) * LANES] = high
                cl[at, q * LANES:(q + 1) * LANES] = (value - high.astype(F32)).astype(BF16)
            norm = jnp.broadcast_to(jnp.sum(total, axis=1, keepdims=True), (16, LANES))
            slot = lax.broadcasted_iota(jnp.int32, (8, LANES), 0)
            used = jnp.concatenate([slot < table[ROUNDS + r, g * 2 + k] for k in range(2)], axis=0)
            nrm[at, :] = jnp.where(used, norm, jnp.inf)
            return carry

        lax.fori_loop(0, TILES // 2, convert, 0, unroll=2)

        def nearest(t, carry):
            high, rows = ch[...], xh[t]
            value = jnp.dot(
                jnp.concatenate([high, cl[...], high], axis=1),
                jnp.concatenate([rows, rows, xl[t]], axis=0),
                preferred_element_type=F32,
            )
            value = value + jnp.concatenate([nrm[...]] * (STEP // LANES), axis=1)
            low[r, t] = jnp.min(value.reshape(USED // 8, 8, STEP), axis=0)
            return carry

        lax.fori_loop(0, PIECES, nearest, 0)

    def along(parts):
        return jnp.concatenate(parts, axis=1)

    norm = along([jnp.sum(sq[t], axis=0, keepdims=True) for t in range(PIECES)])
    best = [along([jnp.min(low[r, t], axis=0, keepdims=True) for t in range(PIECES)]) for r in range(ROUNDS)]
    for r in range(1, ROUNDS):
        best[r] = jnp.minimum(best[r], best[r - 1])
    out_ref[...] = jnp.concatenate([jnp.maximum(value + norm, 0.0) for value in best], axis=0)


def scale(best_ref, out_ref, part, red_line, red_plane, send_sem, recv_sem):
    item, dim = lax.axis_index("item"), lax.axis_index("dim")
    core = item % 2
    rank_line, rank_plane = dim * 2 + core, item // 2

    def line_device(step):
        other = (rank_line + step) % 8
        return (item - core + other % 2, other // 2)

    def plane_device(step):
        return (((rank_plane + step) % 16) * 2 + core, dim)

    barrier = pltpu.get_barrier_semaphore()
    for step in range(1, 8):
        pl.semaphore_signal(barrier, inc=1, device_id=line_device(step), device_id_type=MESH)
    for step in range(1, 16):
        pl.semaphore_signal(barrier, inc=1, device_id=plane_device(step), device_id_type=MESH)
    best = best_ref[...]
    sums = sum([best[:, k * LANES:(k + 1) * LANES] for k in range(SHARE // LANES)])
    line = jnp.concatenate([sums, jnp.zeros((8 - ROUNDS, LANES), F32)], axis=0)
    pl.semaphore_wait(barrier, 22)

    copies = []

    def send(src, dst, target):
        k = len(copies)
        copy = pltpu.make_async_remote_copy(
            src_ref=src, dst_ref=dst, send_sem=send_sem.at[k], recv_sem=recv_sem.at[k],
            device_id=target, device_id_type=MESH,
        )
        copy.start()
        copies.append(copy)

    part[0] = line
    for step in range(1, 8):
        send(part.at[0], red_line.at[step - 1], line_device(step))
    for step in range(7):
        copies[step].wait_recv()
        line = line + red_line[step]
    part[1] = line
    for step in range(1, 16):
        send(part.at[1], red_plane.at[step - 1], plane_device(step))
    for step in range(15):
        copies[7 + step].wait_recv()
        line = line + red_plane[step]
    cost = jnp.sum(line, axis=1, keepdims=True)[:ROUNDS]
    out_ref[...] = jnp.minimum(CAP, TOTAL * best / cost)
    for copy in copies:
        copy.wait_send()


COPIES = ROUNDS * 15 + PIECES * 6
REDUCES = 22
SMEM = pl.BlockSpec(memory_space=pltpu.SMEM)
VMEM = pl.BlockSpec(memory_space=pltpu.VMEM)
ANY = pl.BlockSpec(memory_space=pl.ANY)
MIB = 1024 * 1024


def local(embeddings, cand_index, cand_count):
    rows, *candidates = pl.pallas_call(
        exchange,
        out_shape=(
            jax.ShapeDtypeStruct((4, SHARE, LANES), F32),
            *[jax.ShapeDtypeStruct((128, SLOTS, LANES), F32)] * ROUNDS,
        ),
        in_specs=[SMEM, ANY],
        out_specs=(ANY,) * (1 + ROUNDS),
        scratch_shapes=[
            pltpu.VMEM((ROWS, LANES), F32),
            pltpu.VMEM((ROUNDS, SLOTS, LANES), F32),
            pltpu.VMEM((2, PIECES, STEP // 2, LANES), F32),
            pltpu.SemaphoreType.DMA((2 + ROUNDS,)),
            pltpu.SemaphoreType.DMA((COPIES,)),
            pltpu.SemaphoreType.DMA((COPIES,)),
        ],
        compiler_params=pltpu.CompilerParams(
            collective_id=0, has_side_effects=True, vmem_limit_bytes=56 * MIB
        ),
    )(cand_index, embeddings)
    best = pl.pallas_call(
        distances,
        out_shape=jax.ShapeDtypeStruct((ROUNDS, SHARE), F32),
        in_specs=[SMEM] + [ANY] * (ROUNDS + 1),
        out_specs=VMEM,
        scratch_shapes=[
            pltpu.VMEM((4, SHARE, LANES), F32),
            pltpu.SMEM((2 * ROUNDS, TILES), jnp.int32),
            pltpu.VMEM((ROUNDS, 128 * SLOTS, LANES), F32),
            pltpu.VMEM((USED, 512), BF16),
            pltpu.VMEM((USED, 512), BF16),
            pltpu.VMEM((USED, LANES), F32),
            pltpu.VMEM((PIECES, 512, STEP), BF16),
            pltpu.VMEM((PIECES, 512, STEP), BF16),
            pltpu.VMEM((PIECES, 8, STEP), F32),
            pltpu.VMEM((ROUNDS, PIECES, 8, STEP), F32),
            pltpu.SemaphoreType.DMA((ROUNDS + 1,)),
        ],
        compiler_params=pltpu.CompilerParams(vmem_limit_bytes=56 * MIB),
    )(cand_count, *[c.reshape(128 * SLOTS, LANES) for c in candidates], rows)
    return pl.pallas_call(
        scale,
        out_shape=jax.ShapeDtypeStruct((ROUNDS, SHARE), F32),
        in_specs=[VMEM],
        out_specs=VMEM,
        scratch_shapes=[
            pltpu.VMEM((2, 8, LANES), F32),
            pltpu.VMEM((7, 8, LANES), F32),
            pltpu.VMEM((15, 8, LANES), F32),
            pltpu.SemaphoreType.DMA((REDUCES,)),
            pltpu.SemaphoreType.DMA((REDUCES,)),
        ],
        compiler_params=pltpu.CompilerParams(collective_id=1, has_side_effects=True),
    )(best)


def solution(mesh):
    in_specs = (P("item", "dim"), P(None, "item"), P())
    out_specs = P(None, ("item", "dim"))
    return jax.shard_map(local, mesh=mesh, in_specs=in_specs, out_specs=out_specs, check_vma=False)
```

```python
import itertools

import jax
import jax.numpy as jnp
from jax import lax
from jax.experimental import pallas as pl
from jax.experimental.pallas import tpu as pltpu
from jax.sharding import PartitionSpec as P

CAP = 4.0
MESH = pl.DeviceIdType.MESH
ROUNDS = 3
SLOTS = 32
LANES = 128
ITEMS = 32
ROWS = 4096
SHARE = 1024
STEP = 256
PIECES = SHARE // STEP
TOTAL = 131072
TILE = 8
TILES_SLOTS = SLOTS // TILE
BLOCK = 4 * TILES_SLOTS
TILES = 92
USED = TILES * 8
GROUP = 4
BF16 = jnp.bfloat16
F32 = jnp.float32


def kernel(
    index_hbm, count_hbm, x_ref, out_ref,
    index_ref, count_ref, ordered, table, xv, xfull, relay, cand_0, cand_1, cand_2,
    ch, cl, nrm, xh, xl, sq, low, done, part, red_line, red_plane,
    load_sem, send_sem, recv_sem,
):
    cand = (cand_0, cand_1, cand_2)
    item, dim = lax.axis_index("item"), lax.axis_index("dim")
    z, x, core = item // 8, (item // 2) % 4, item % 2
    a = x * (1 - core) + z * core
    b = z * (1 - core) + x * core

    def device(a_, b_):
        return (a_ * (2 + 6 * core) + b_ * (8 - 6 * core) + core, dim)

    def block(b_, a_):
        return ((core * 4 + b_) * 4 + a_) * BLOCK

    a_up, a_down, a_far = (a + 1) % 4, (a + 3) % 4, (a + 2) % 4
    b_up, b_down, b_far = (b + 1) % 4, (b + 3) % 4, (b + 2) % 4
    y_up, y_down, y_far = (dim + 1) % 4, (dim + 3) % 4, (dim + 2) % 4
    sibling = (item + 1 - 2 * core, dim)
    rank_line, rank_plane = dim * 2 + core, item // 2

    def line_device(step):
        other = (rank_line + step) % 8
        return (item - core + other % 2, other // 2)

    def plane_device(step):
        return (((rank_plane + step) % 16) * 2 + core, dim)

    loads = [
        pltpu.make_async_copy(index_hbm, index_ref, load_sem.at[0]),
        pltpu.make_async_copy(x_ref, xv, load_sem.at[1]),
        pltpu.make_async_copy(count_hbm, count_ref, load_sem.at[2]),
        pltpu.make_async_copy(x_ref.at[pl.ds(dim * SHARE, SHARE)], xfull.at[dim], load_sem.at[3]),
    ]
    for copy in loads:
        copy.start()
    index_load, x_load, count_load, own_rows = loads

    barrier = pltpu.get_barrier_semaphore()
    for step in range(1, 8):
        pl.semaphore_signal(barrier, inc=1, device_id=line_device(step), device_id_type=MESH)
    for step in range(1, 16):
        pl.semaphore_signal(barrier, inc=1, device_id=plane_device(step), device_id_type=MESH)

    index_load.wait()
    x_load.wait()
    for r in range(ROUNDS):
        def pick(g, carry, r=r):
            rows = [xv[pl.ds(index_ref[r, g * TILE + k], 1), :] for k in range(TILE)]
            cand[r][block(b, a) + dim * TILES_SLOTS + g] = jnp.concatenate(rows, axis=0)
            return carry

        lax.fori_loop(0, TILES_SLOTS, pick, 0)
    pl.semaphore_wait(barrier, 22)

    number = itertools.count()
    started = []

    def send(src, dst, target):
        k = next(number)
        copy = pltpu.make_async_remote_copy(
            src_ref=src, dst_ref=dst, send_sem=send_sem.at[k], recv_sem=recv_sem.at[k],
            device_id=target, device_id_type=MESH,
        )
        copy.start()
        started.append(copy)
        return copy

    def send_cand(r, start, length, target):
        ref = cand[r].at[pl.ds(start, length)]
        return send(ref, ref, target)

    y_copies = [
        [send_cand(r, block(b, a) + dim * TILES_SLOTS, TILES_SLOTS, (item, (dim + d) % 4)) for d in (1, 3, 2)]
        for r in range(ROUNDS)
    ]
    half = STEP // 2
    relay_up, relay_down, near, passed = [], [], [], []

    def send_near(t):
        lands = xfull.at[dim, pl.ds(t * STEP, STEP)]
        near.append((
            send(xv.at[pl.ds(y_up * SHARE + t * STEP, STEP)], lands, (item, y_up)),
            send(xv.at[pl.ds(y_down * SHARE + t * STEP, STEP)], lands, (item, y_down)),
        ))

    for t in range(PIECES):
        far = y_far * SHARE + t * STEP
        relay_up.append(send(xv.at[pl.ds(far, half)], relay.at[0, t], (item, y_up)))
        relay_down.append(send(xv.at[pl.ds(far + half, half)], relay.at[1, t], (item, y_down)))
    send_near(0)

    def pass_rows(t):
        relay_up[t].wait_recv()
        up = send(relay.at[0, t], xfull.at[y_down, pl.ds(t * STEP, half)], (item, y_up))
        relay_down[t].wait_recv()
        down = send(relay.at[1, t], xfull.at[y_up, pl.ds(t * STEP + half, half)], (item, y_down))
        passed.append((up, down))

    first, second_up, second_down, second_pass, swap = [], [], [], [], []

    def first_send(r):
        for copy in y_copies[r]:
            copy.wait_recv()
        first.append([send_cand(r, block(b, a), BLOCK, device(a_, b)) for a_ in (a_up, a_down, a_far)])

    def second_send(r):
        for copy in first[r]:
            copy.wait_recv()
        second_up.append(send_cand(r, block(b, 0), 4 * BLOCK, device(a, b_up)))
        second_down.append(send_cand(r, block(b, 0), 4 * BLOCK, device(a, b_down)))
        swap.append([send_cand(r, block(b, 0), 4 * BLOCK, sibling)])

    def second_forward(r):
        second_up[r].wait_recv()
        up = send_cand(r, block(b_down, 0), 2 * BLOCK, device(a, b_up))
        swap[r].append(send_cand(r, block(b_down, 0), 4 * BLOCK, sibling))
        second_down[r].wait_recv()
        down = send_cand(r, block(b_up, 2), 2 * BLOCK, device(a, b_down))
        swap[r].append(send_cand(r, block(b_up, 0), 4 * BLOCK, sibling))
        second_pass.append((up, down))

    def second_end(r):
        second_pass[r][0].wait_recv()
        swap[r].append(send_cand(r, block(b_far, 0), 2 * BLOCK, sibling))
        second_pass[r][1].wait_recv()
        swap[r].append(send_cand(r, block(b_far, 2), 2 * BLOCK, sibling))

    def tabulate(r):
        for k in range(ITEMS):
            core_, b_, a_ = k // 16, (k // 4) % 4, k % 4
            ordered[k] = count_ref[r, a_ * (2 + 6 * core_) + b_ * (8 - 6 * core_) + core_]
        ordered[ITEMS] = jnp.int32(0)

        def entry(p, carry):
            k, o, rest = carry
            table[r, p] = jnp.minimum(k, ITEMS - 1) * BLOCK + o
            table[ROUNDS + r, p] = rest
            later = jnp.minimum(k + 1, ITEMS)
            later_count = ordered[later]
            more = rest > 8
            return jnp.where(more, k, later), jnp.where(more, o + 1, 0), jnp.where(more, rest - 8, later_count)

        lax.fori_loop(0, TILES, entry, (jnp.int32(0), jnp.int32(0), ordered[0]), unroll=4)

    def convert(r):
        for copy in swap[r]:
            copy.wait_recv()

        def one(g, carry):
            at = pl.ds(pl.multiple_of(g * (GROUP * 8), GROUP * 8), GROUP * 8)
            place = [table[r, g * GROUP + k] for k in range(GROUP)]
            total = jnp.zeros((GROUP * 8, LANES), F32)
            for q in range(4):
                value = jnp.concatenate(
                    [cand[r][p + q * TILES_SLOTS] for p in place], axis=0
                )
                total += value * value
                value = -2.0 * value
                high = value.astype(BF16)
                ch[r, at, q * LANES:(q + 1) * LANES] = high
                cl[r, at, q * LANES:(q + 1) * LANES] = (value - high.astype(F32)).astype(BF16)
            norm = jnp.broadcast_to(jnp.sum(total, axis=1, keepdims=True), (GROUP * 8, LANES))
            slot = lax.broadcasted_iota(jnp.int32, (8, LANES), 0)
            used = jnp.concatenate(
                [slot < table[ROUNDS + r, g * GROUP + k] for k in range(GROUP)], axis=0
            )
            nrm[r, at, :] = jnp.where(used, norm, jnp.inf)
            return carry

        lax.fori_loop(0, TILES // GROUP, one, 0)

    def prepare(t):
        for copy in near[t] + passed[t]:
            copy.wait_recv()
        total = jnp.zeros((LANES, STEP), F32)
        for q in range(4):
            value = xfull[q, t * STEP:(t + 1) * STEP, :].T
            total += value * value
            high = value.astype(BF16)
            xh[t, q * LANES:(q + 1) * LANES, :] = high
            xl[t, q * LANES:(q + 1) * LANES, :] = (value - high.astype(F32)).astype(BF16)
        sq[t] = jnp.sum(total.reshape(LANES // 8, 8, STEP), axis=0)

    def nearest(t, r):
        high, rows = ch[r], xh[t]
        value = jnp.dot(
            jnp.concatenate([high, cl[r], high], axis=1),
            jnp.concatenate([rows, rows, xl[t]], axis=0),
            preferred_element_type=F32,
        )
        value = value + jnp.concatenate([nrm[r]] * (STEP // LANES), axis=1)
        low[t, r] = jnp.min(value.reshape(TILES, 8, STEP), axis=0)

    def finish(t):
        norm = jnp.sum(sq[t], axis=0, keepdims=True)
        best = [jnp.min(low[t, r], axis=0, keepdims=True) for r in range(ROUNDS)]
        for r in range(1, ROUNDS):
            best[r] = jnp.minimum(best[r], best[r - 1])
        done[:, t * STEP:(t + 1) * STEP] = jnp.concatenate(
            [jnp.maximum(value + norm, 0.0) for value in best], axis=0
        )

    def many(count, body):
        def one(k, carry):
            body(k)
            return carry

        lax.fori_loop(0, count, one, 0)

    count_load.wait()
    tabulate(0)
    for r in range(ROUNDS):
        first_send(r)
    pass_rows(0)
    send_near(1)
    second_send(0)
    pass_rows(1)
    send_near(2)
    second_send(1)
    tabulate(1)
    pass_rows(2)
    send_near(3)
    pass_rows(3)
    tabulate(2)
    own_rows.wait()
    second_forward(0)
    second_send(2)
    second_end(0)
    prepare(0)
    second_forward(1)
    convert(0)
    second_end(1)
    nearest(0, 0)
    prepare(1)
    nearest(1, 0)
    second_forward(2)
    convert(1)
    second_end(2)
    many(2, lambda t: nearest(t, 1))
    prepare(2)
    many(2, lambda r: nearest(2, r))
    convert(2)
    many(3, lambda t: nearest(t, 2))
    for t in range(PIECES - 1):
        finish(t)
    for copy in started:
        copy.wait_send()
    started.clear()
    prepare(PIECES - 1)
    many(ROUNDS, lambda r: nearest(PIECES - 1, r))
    finish(PIECES - 1)

    sums = sum([done[:, k * LANES:(k + 1) * LANES] for k in range(SHARE // LANES)])
    line = jnp.concatenate([sums, jnp.zeros((8 - ROUNDS, LANES), F32)], axis=0)
    part[0] = line
    copies = [send(part.at[0], red_line.at[step - 1], line_device(step)) for step in range(1, 8)]
    for step, copy in enumerate(copies):
        copy.wait_recv()
        line = line + red_line[step]
    part[1] = line
    copies = [send(part.at[1], red_plane.at[step - 1], plane_device(step)) for step in range(1, 16)]
    for step, copy in enumerate(copies):
        copy.wait_recv()
        line = line + red_plane[step]
    cost = jnp.sum(line, axis=1, keepdims=True)[:ROUNDS]
    out_ref[...] = jnp.minimum(CAP, TOTAL * done[...] / cost)

    for copy in started:
        copy.wait_send()


COPIES = ROUNDS * 15 + PIECES * 6 + 22
ANY = pl.BlockSpec(memory_space=pl.ANY)


def local(embeddings, cand_index, cand_count):
    return pl.pallas_call(
        kernel,
        out_shape=jax.ShapeDtypeStruct((ROUNDS, SHARE), F32),
        in_specs=[ANY, ANY, ANY],
        out_specs=pl.BlockSpec(memory_space=pltpu.VMEM),
        scratch_shapes=[
            pltpu.SMEM((ROUNDS, SLOTS), jnp.int32),
            pltpu.SMEM((ROUNDS, ITEMS), jnp.int32),
            pltpu.SMEM((ITEMS + 1,), jnp.int32),
            pltpu.SMEM((2 * ROUNDS, TILES), jnp.int32),
            pltpu.VMEM((ROWS, LANES), F32),
            pltpu.VMEM((4, SHARE, LANES), F32),
            pltpu.VMEM((2, PIECES, STEP // 2, LANES), F32),
            *[pltpu.VMEM((ITEMS * BLOCK, TILE, LANES), F32)] * ROUNDS,
            pltpu.VMEM((ROUNDS, USED, 512), BF16),
            pltpu.VMEM((ROUNDS, USED, 512), BF16),
            pltpu.VMEM((ROUNDS, USED, LANES), F32),
            pltpu.VMEM((PIECES, 512, STEP), BF16),
            pltpu.VMEM((PIECES, 512, STEP), BF16),
            pltpu.VMEM((PIECES, 8, STEP), F32),
            pltpu.VMEM((PIECES, ROUNDS, 8, STEP), F32),
            pltpu.VMEM((ROUNDS, SHARE), F32),
            pltpu.VMEM((2, 8, LANES), F32),
            pltpu.VMEM((7, 8, LANES), F32),
            pltpu.VMEM((15, 8, LANES), F32),
            pltpu.SemaphoreType.DMA((4,)),
            pltpu.SemaphoreType.DMA((COPIES,)),
            pltpu.SemaphoreType.DMA((COPIES,)),
        ],
        compiler_params=pltpu.CompilerParams(
            collective_id=0, has_side_effects=True, vmem_limit_bytes=56 * 1024 * 1024
        ),
    )(cand_index, cand_count, embeddings)


def solution(mesh):
    in_specs = (P("item", "dim"), P(None, "item"), P())
    out_specs = P(None, ("item", "dim"))
    return jax.shard_map(local, mesh=mesh, in_specs=in_specs, out_specs=out_specs, check_vma=False)
```

```python
import itertools

import jax
import jax.numpy as jnp
from jax import lax
from jax.experimental import pallas as pl
from jax.experimental.pallas import tpu as pltpu
from jax.sharding import PartitionSpec as P

CAP = 4.0
MESH = pl.DeviceIdType.MESH
ROUNDS = 3
SLOTS = 32
LANES = 128
ITEMS = 32
ROWS = 4096
SHARE = 1024
STEP = 256
PIECES = SHARE // STEP
TOTAL = 131072
TILE = 8
TILES_SLOTS = SLOTS // TILE
BLOCK = 4 * TILES_SLOTS
TILES = 92
USED = TILES * 8
GROUP = 4
BF16 = jnp.bfloat16
F32 = jnp.float32


def kernel(
    index_hbm, count_hbm, x_ref, out_ref,
    index_ref, count_ref, ordered, table, xv, xfull, relay_buf, cand_0, cand_1, cand_2,
    ch, cl, nrm, xh, xl, sq, low, done, part, red_line, red_plane,
    load_sem, send_sem, recv_sem,
):
    cand = (cand_0, cand_1, cand_2)
    item, dim = lax.axis_index("item"), lax.axis_index("dim")
    z, x, core = item // 8, (item // 2) % 4, item % 2
    a = x * (1 - core) + z * core
    b = z * (1 - core) + x * core

    def device(a_, b_):
        return (a_ * (2 + 6 * core) + b_ * (8 - 6 * core) + core, dim)

    def block(b_, a_):
        return ((core * 4 + b_) * 4 + a_) * BLOCK

    a_up, a_down, a_far = (a + 1) % 4, (a + 3) % 4, (a + 2) % 4
    b_up, b_down, b_far = (b + 1) % 4, (b + 3) % 4, (b + 2) % 4
    y_up, y_down, y_far = (dim + 1) % 4, (dim + 3) % 4, (dim + 2) % 4
    sibling = (item + 1 - 2 * core, dim)
    rank_line, rank_plane = dim * 2 + core, item // 2

    def line_device(step):
        other = (rank_line + step) % 8
        return (item - core + other % 2, other // 2)

    def plane_device(step):
        return (((rank_plane + step) % 16) * 2 + core, dim)

    loads = [
        pltpu.make_async_copy(index_hbm, index_ref, load_sem.at[0]),
        pltpu.make_async_copy(x_ref, xv, load_sem.at[1]),
        pltpu.make_async_copy(count_hbm, count_ref, load_sem.at[2]),
        pltpu.make_async_copy(x_ref.at[pl.ds(dim * SHARE, SHARE)], xfull.at[dim], load_sem.at[3]),
    ]
    for copy in loads:
        copy.start()
    index_load, x_load, count_load, own_rows = loads

    barrier = pltpu.get_barrier_semaphore()
    for step in range(1, 8):
        pl.semaphore_signal(barrier, inc=1, device_id=line_device(step), device_id_type=MESH)
    for step in range(1, 16):
        pl.semaphore_signal(barrier, inc=1, device_id=plane_device(step), device_id_type=MESH)

    index_load.wait()
    x_load.wait()
    for r in range(ROUNDS):
        def pick(g, carry, r=r):
            rows = [xv[pl.ds(index_ref[r, g * TILE + k], 1), :] for k in range(TILE)]
            cand[r][block(b, a) + dim * TILES_SLOTS + g] = jnp.concatenate(rows, axis=0)
            return carry

        lax.fori_loop(0, TILES_SLOTS, pick, 0)
    pl.semaphore_wait(barrier, 22)

    number = itertools.count()
    started = []

    def send(src, dst, target):
        k = next(number)
        copy = pltpu.make_async_remote_copy(
            src_ref=src, dst_ref=dst, send_sem=send_sem.at[k], recv_sem=recv_sem.at[k],
            device_id=target, device_id_type=MESH,
        )
        copy.start()
        started.append(copy)
        return copy

    def send_cand(r, start, length, target):
        ref = cand[r].at[pl.ds(start, length)]
        return send(ref, ref, target)

    y_copies, first, second_up, second_down, pass_up, pass_down, swap = [{} for _ in range(7)]
    relay, near, passed = [{} for _ in range(3)]

    def pick_send(r):
        start = block(b, a) + dim * TILES_SLOTS
        y_copies[r] = [send_cand(r, start, TILES_SLOTS, (item, (dim + d) % 4)) for d in (1, 3, 2)]

    half = STEP // 2

    def near_send(t):
        lands = xfull.at[dim, pl.ds(t * STEP, STEP)]
        near[t] = (
            send(xv.at[pl.ds(y_up * SHARE + t * STEP, STEP)], lands, (item, y_up)),
            send(xv.at[pl.ds(y_down * SHARE + t * STEP, STEP)], lands, (item, y_down)),
        )

    def far_send(t):
        far = y_far * SHARE + t * STEP
        relay[t] = (
            send(xv.at[pl.ds(far, half)], relay_buf.at[0, t], (item, y_up)),
            send(xv.at[pl.ds(far + half, half)], relay_buf.at[1, t], (item, y_down)),
        )

    def far_pass(t):
        relay[t][0].wait_recv()
        up = send(relay_buf.at[0, t], xfull.at[y_down, pl.ds(t * STEP, half)], (item, y_up))
        relay[t][1].wait_recv()
        down = send(relay_buf.at[1, t], xfull.at[y_up, pl.ds(t * STEP + half, half)], (item, y_down))
        passed[t] = (up, down)

    def first_send(r):
        for copy in y_copies[r]:
            copy.wait_recv()
        first[r] = [send_cand(r, block(b, a), BLOCK, device(a_, b)) for a_ in (a_up, a_down, a_far)]

    def second_send(r):
        for copy in first[r]:
            copy.wait_recv()
        second_up[r] = send_cand(r, block(b, 0), 4 * BLOCK, device(a, b_up))
        second_down[r] = send_cand(r, block(b, 0), 4 * BLOCK, device(a, b_down))
        swap[r] = [send_cand(r, block(b, 0), 4 * BLOCK, sibling)]

    def second_pass(r):
        second_up[r].wait_recv()
        pass_up[r] = send_cand(r, block(b_down, 0), 2 * BLOCK, device(a, b_up))
        swap[r].append(send_cand(r, block(b_down, 0), 4 * BLOCK, sibling))
        second_down[r].wait_recv()
        pass_down[r] = send_cand(r, block(b_up, 2), 2 * BLOCK, device(a, b_down))
        swap[r].append(send_cand(r, block(b_up, 0), 4 * BLOCK, sibling))

    def second_end(r):
        pass_up[r].wait_recv()
        swap[r].append(send_cand(r, block(b_far, 0), 2 * BLOCK, sibling))
        pass_down[r].wait_recv()
        swap[r].append(send_cand(r, block(b_far, 2), 2 * BLOCK, sibling))

    def tabulate(r):
        for k in range(ITEMS):
            core_, b_, a_ = k // 16, (k // 4) % 4, k % 4
            ordered[k] = count_ref[r, a_ * (2 + 6 * core_) + b_ * (8 - 6 * core_) + core_]
        ordered[ITEMS] = jnp.int32(0)

        def entry(p, carry):
            k, o, rest = carry
            table[r, p] = jnp.minimum(k, ITEMS - 1) * BLOCK + o
            table[ROUNDS + r, p] = rest
            later = jnp.minimum(k + 1, ITEMS)
            later_count = ordered[later]
            more = rest > 8
            return jnp.where(more, k, later), jnp.where(more, o + 1, 0), jnp.where(more, rest - 8, later_count)

        lax.fori_loop(0, TILES, entry, (jnp.int32(0), jnp.int32(0), ordered[0]), unroll=4)

    def convert(r):
        for copy in swap[r]:
            copy.wait_recv()

        def one(g, carry):
            at = pl.ds(pl.multiple_of(g * (GROUP * 8), GROUP * 8), GROUP * 8)
            place = [table[r, g * GROUP + k] for k in range(GROUP)]
            total = jnp.zeros((GROUP * 8, LANES), F32)
            for q in range(4):
                value = jnp.concatenate(
                    [cand[r][p + q * TILES_SLOTS] for p in place], axis=0
                )
                total += value * value
                value = -2.0 * value
                high = value.astype(BF16)
                ch[r, at, q * LANES:(q + 1) * LANES] = high
                cl[r, at, q * LANES:(q + 1) * LANES] = (value - high.astype(F32)).astype(BF16)
            norm = jnp.broadcast_to(jnp.sum(total, axis=1, keepdims=True), (GROUP * 8, LANES))
            slot = lax.broadcasted_iota(jnp.int32, (8, LANES), 0)
            used = jnp.concatenate(
                [slot < table[ROUNDS + r, g * GROUP + k] for k in range(GROUP)], axis=0
            )
            nrm[r, at, :] = jnp.where(used, norm, jnp.inf)
            return carry

        lax.fori_loop(0, TILES // GROUP, one, 0)

    def prepare(t):
        for copy in near[t] + passed[t]:
            copy.wait_recv()
        total = jnp.zeros((LANES, STEP), F32)
        for q in range(4):
            value = xfull[q, t * STEP:(t + 1) * STEP, :].T
            total += value * value
            high = value.astype(BF16)
            xh[t, q * LANES:(q + 1) * LANES, :] = high
            xl[t, q * LANES:(q + 1) * LANES, :] = (value - high.astype(F32)).astype(BF16)
        sq[t] = jnp.sum(total.reshape(LANES // 8, 8, STEP), axis=0)

    def nearest(t, r):
        high, rows = ch[r], xh[t]
        value = jnp.dot(
            jnp.concatenate([high, cl[r], high], axis=1),
            jnp.concatenate([rows, rows, xl[t]], axis=0),
            preferred_element_type=F32,
        )
        value = value + jnp.concatenate([nrm[r]] * (STEP // LANES), axis=1)
        low[t, r] = jnp.min(value.reshape(TILES, 8, STEP), axis=0)

    def finish(t):
        norm = jnp.sum(sq[t], axis=0, keepdims=True)
        best = [jnp.min(low[t, r], axis=0, keepdims=True) for r in range(ROUNDS)]
        for r in range(1, ROUNDS):
            best[r] = jnp.minimum(best[r], best[r - 1])
        done[:, t * STEP:(t + 1) * STEP] = jnp.concatenate(
            [jnp.maximum(value + norm, 0.0) for value in best], axis=0
        )

    def many(count, body):
        def one(k, carry):
            body(k)
            return carry

        lax.fori_loop(0, count, one, 0)

    pick_send(0)
    count_load.wait()
    tabulate(0)
    pick_send(1)
    near_send(0)
    tabulate(1)
    first_send(0)
    first_send(1)
    pick_send(2)
    far_send(0)
    near_send(1)
    far_send(1)
    second_send(0)
    tabulate(2)
    far_send(2)
    second_send(1)
    second_pass(0)
    far_pass(0)
    first_send(2)
    second_end(0)
    far_pass(1)
    second_pass(1)
    second_send(2)
    far_send(3)
    far_pass(2)
    convert(0)
    second_end(1)
    near_send(2)
    own_rows.wait()
    prepare(0)
    prepare(1)
    many(2, lambda t: nearest(t, 0))
    second_pass(2)
    convert(1)
    near_send(3)
    many(2, lambda t: nearest(t, 1))
    second_end(2)
    prepare(2)
    many(2, lambda r: nearest(2, r))
    far_pass(3)
    convert(2)
    many(3, lambda t: nearest(t, 2))
    for t in range(PIECES - 1):
        finish(t)
    for copy in started:
        copy.wait_send()
    started.clear()
    prepare(PIECES - 1)
    many(ROUNDS, lambda r: nearest(PIECES - 1, r))
    finish(PIECES - 1)

    sums = sum([done[:, k * LANES:(k + 1) * LANES] for k in range(SHARE // LANES)])
    line = jnp.concatenate([sums, jnp.zeros((8 - ROUNDS, LANES), F32)], axis=0)
    part[0] = line
    copies = [send(part.at[0], red_line.at[step - 1], line_device(step)) for step in range(1, 8)]
    for step, copy in enumerate(copies):
        copy.wait_recv()
        line = line + red_line[step]
    part[1] = line
    copies = [send(part.at[1], red_plane.at[step - 1], plane_device(step)) for step in range(1, 16)]
    for step, copy in enumerate(copies):
        copy.wait_recv()
        line = line + red_plane[step]
    cost = jnp.sum(line, axis=1, keepdims=True)[:ROUNDS]
    out_ref[...] = jnp.minimum(CAP, TOTAL * done[...] / cost)

    for copy in started:
        copy.wait_send()


COPIES = ROUNDS * 15 + PIECES * 6 + 22
ANY = pl.BlockSpec(memory_space=pl.ANY)


def local(embeddings, cand_index, cand_count):
    return pl.pallas_call(
        kernel,
        out_shape=jax.ShapeDtypeStruct((ROUNDS, SHARE), F32),
        in_specs=[ANY, ANY, ANY],
        out_specs=pl.BlockSpec(memory_space=pltpu.VMEM),
        scratch_shapes=[
            pltpu.SMEM((ROUNDS, SLOTS), jnp.int32),
            pltpu.SMEM((ROUNDS, ITEMS), jnp.int32),
            pltpu.SMEM((ITEMS + 1,), jnp.int32),
            pltpu.SMEM((2 * ROUNDS, TILES), jnp.int32),
            pltpu.VMEM((ROWS, LANES), F32),
            pltpu.VMEM((4, SHARE, LANES), F32),
            pltpu.VMEM((2, PIECES, STEP // 2, LANES), F32),
            *[pltpu.VMEM((ITEMS * BLOCK, TILE, LANES), F32)] * ROUNDS,
            pltpu.VMEM((ROUNDS, USED, 512), BF16),
            pltpu.VMEM((ROUNDS, USED, 512), BF16),
            pltpu.VMEM((ROUNDS, USED, LANES), F32),
            pltpu.VMEM((PIECES, 512, STEP), BF16),
            pltpu.VMEM((PIECES, 512, STEP), BF16),
            pltpu.VMEM((PIECES, 8, STEP), F32),
            pltpu.VMEM((PIECES, ROUNDS, 8, STEP), F32),
            pltpu.VMEM((ROUNDS, SHARE), F32),
            pltpu.VMEM((2, 8, LANES), F32),
            pltpu.VMEM((7, 8, LANES), F32),
            pltpu.VMEM((15, 8, LANES), F32),
            pltpu.SemaphoreType.DMA((4,)),
            pltpu.SemaphoreType.DMA((COPIES,)),
            pltpu.SemaphoreType.DMA((COPIES,)),
        ],
        compiler_params=pltpu.CompilerParams(
            collective_id=0, has_side_effects=True, vmem_limit_bytes=56 * 1024 * 1024
        ),
    )(cand_index, cand_count, embeddings)


def solution(mesh):
    in_specs = (P("item", "dim"), P(None, "item"), P())
    out_specs = P(None, ("item", "dim"))
    return jax.shard_map(local, mesh=mesh, in_specs=in_specs, out_specs=out_specs, check_vma=False)
```

```python
import itertools

import jax
import jax.numpy as jnp
from jax import lax
from jax.experimental import pallas as pl
from jax.experimental.pallas import tpu as pltpu
from jax.sharding import PartitionSpec as P

CAP = 4.0
MESH = pl.DeviceIdType.MESH
ROUNDS = 3
SLOTS = 32
LANES = 128
ITEMS = 32
ROWS = 4096
SHARE = 1024
STEP = 256
PIECES = SHARE // STEP
WIDE = 512
PAIRS = SHARE // WIDE
TOTAL = 131072
TILE = 8
TILES_SLOTS = SLOTS // TILE
BLOCK = 4 * TILES_SLOTS
TILES = 92
USED = TILES * 8
GROUP = 4
BF16 = jnp.bfloat16
F32 = jnp.float32


def kernel(
    index_hbm, count_hbm, x_ref, out_ref,
    index_ref, count_ref, ordered, table, xv, xfull, relay_buf, cand_0, cand_1, cand_2,
    ch, cl, nrm, xh, xl, sq, low, done, part, red_line, red_plane,
    load_sem, send_sem, recv_sem,
):
    cand = (cand_0, cand_1, cand_2)
    item, dim = lax.axis_index("item"), lax.axis_index("dim")
    z, x, core = item // 8, (item // 2) % 4, item % 2
    a = x * (1 - core) + z * core
    b = z * (1 - core) + x * core

    def device(a_, b_):
        return (a_ * (2 + 6 * core) + b_ * (8 - 6 * core) + core, dim)

    def block(b_, a_):
        return ((core * 4 + b_) * 4 + a_) * BLOCK

    a_up, a_down, a_far = (a + 1) % 4, (a + 3) % 4, (a + 2) % 4
    b_up, b_down, b_far = (b + 1) % 4, (b + 3) % 4, (b + 2) % 4
    y_up, y_down, y_far = (dim + 1) % 4, (dim + 3) % 4, (dim + 2) % 4
    sibling = (item + 1 - 2 * core, dim)
    rank_line, rank_plane = dim * 2 + core, item // 2

    def line_device(step):
        other = (rank_line + step) % 8
        return (item - core + other % 2, other // 2)

    def plane_device(step):
        return (((rank_plane + step) % 16) * 2 + core, dim)

    loads = [
        pltpu.make_async_copy(index_hbm, index_ref, load_sem.at[0]),
        pltpu.make_async_copy(x_ref, xv, load_sem.at[1]),
        pltpu.make_async_copy(count_hbm, count_ref, load_sem.at[2]),
        pltpu.make_async_copy(x_ref.at[pl.ds(dim * SHARE, SHARE)], xfull.at[dim], load_sem.at[3]),
    ]
    for copy in loads:
        copy.start()
    index_load, x_load, count_load, own_rows = loads

    barrier = pltpu.get_barrier_semaphore()
    for step in range(1, 8):
        pl.semaphore_signal(barrier, inc=1, device_id=line_device(step), device_id_type=MESH)
    for step in range(1, 16):
        pl.semaphore_signal(barrier, inc=1, device_id=plane_device(step), device_id_type=MESH)

    index_load.wait()
    x_load.wait()
    for r in range(ROUNDS):
        def pick(g, carry, r=r):
            rows = [xv[pl.ds(index_ref[r, g * TILE + k], 1), :] for k in range(TILE)]
            cand[r][block(b, a) + dim * TILES_SLOTS + g] = jnp.concatenate(rows, axis=0)
            return carry

        lax.fori_loop(0, TILES_SLOTS, pick, 0)
    def tabulate(r):
        for k in range(ITEMS):
            core_, b_, a_ = k // 16, (k // 4) % 4, k % 4
            ordered[k] = count_ref[r, a_ * (2 + 6 * core_) + b_ * (8 - 6 * core_) + core_]
        ordered[ITEMS] = jnp.int32(0)

        def entry(p, carry):
            k, o, rest = carry
            table[r, p] = jnp.minimum(k, ITEMS - 1) * BLOCK + o
            table[ROUNDS + r, p] = rest
            later = jnp.minimum(k + 1, ITEMS)
            later_count = ordered[later]
            more = rest > 8
            return jnp.where(more, k, later), jnp.where(more, o + 1, 0), jnp.where(more, rest - 8, later_count)

        lax.fori_loop(0, TILES, entry, (jnp.int32(0), jnp.int32(0), ordered[0]), unroll=4)

    count_load.wait()
    for r in range(ROUNDS):
        tabulate(r)
    pl.semaphore_wait(barrier, 22)

    number = itertools.count()
    started = []

    def send(src, dst, target):
        k = next(number)
        copy = pltpu.make_async_remote_copy(
            src_ref=src, dst_ref=dst, send_sem=send_sem.at[k], recv_sem=recv_sem.at[k],
            device_id=target, device_id_type=MESH,
        )
        copy.start()
        started.append(copy)
        return copy

    def send_cand(r, start, length, target):
        ref = cand[r].at[pl.ds(start, length)]
        return send(ref, ref, target)

    y_copies, first, second_up, second_down, pass_up, pass_down, swap = [{} for _ in range(7)]
    relay, near, passed = [{} for _ in range(3)]

    def pick_send(r):
        start = block(b, a) + dim * TILES_SLOTS
        y_copies[r] = [send_cand(r, start, TILES_SLOTS, (item, (dim + d) % 4)) for d in (1, 3, 2)]

    half = STEP // 2

    def near_send(t):
        lands = xfull.at[dim, pl.ds(t * STEP, STEP)]
        near[t] = (
            send(xv.at[pl.ds(y_up * SHARE + t * STEP, STEP)], lands, (item, y_up)),
            send(xv.at[pl.ds(y_down * SHARE + t * STEP, STEP)], lands, (item, y_down)),
        )

    def far_send(t):
        far = y_far * SHARE + t * STEP
        relay[t] = (
            send(xv.at[pl.ds(far, half)], relay_buf.at[0, t], (item, y_up)),
            send(xv.at[pl.ds(far + half, half)], relay_buf.at[1, t], (item, y_down)),
        )

    def far_pass(t):
        relay[t][0].wait_recv()
        up = send(relay_buf.at[0, t], xfull.at[y_down, pl.ds(t * STEP, half)], (item, y_up))
        relay[t][1].wait_recv()
        down = send(relay_buf.at[1, t], xfull.at[y_up, pl.ds(t * STEP + half, half)], (item, y_down))
        passed[t] = (up, down)

    def first_send(r):
        for copy in y_copies[r]:
            copy.wait_recv()
        first[r] = [send_cand(r, block(b, a), BLOCK, device(a_, b)) for a_ in (a_up, a_down, a_far)]

    def second_send(r):
        for copy in first[r]:
            copy.wait_recv()
        second_up[r] = send_cand(r, block(b, 0), 4 * BLOCK, device(a, b_up))
        second_down[r] = send_cand(r, block(b, 0), 4 * BLOCK, device(a, b_down))
        swap[r] = [send_cand(r, block(b, 0), 4 * BLOCK, sibling)]

    def second_pass(r):
        second_up[r].wait_recv()
        pass_up[r] = send_cand(r, block(b_down, 0), 2 * BLOCK, device(a, b_up))
        swap[r].append(send_cand(r, block(b_down, 0), 4 * BLOCK, sibling))
        second_down[r].wait_recv()
        pass_down[r] = send_cand(r, block(b_up, 2), 2 * BLOCK, device(a, b_down))
        swap[r].append(send_cand(r, block(b_up, 0), 4 * BLOCK, sibling))

    def second_end(r):
        pass_up[r].wait_recv()
        swap[r].append(send_cand(r, block(b_far, 0), 2 * BLOCK, sibling))
        pass_down[r].wait_recv()
        swap[r].append(send_cand(r, block(b_far, 2), 2 * BLOCK, sibling))

    def convert(r):
        for copy in swap[r]:
            copy.wait_recv()

        def one(g, carry):
            at = pl.ds(pl.multiple_of(g * (GROUP * 8), GROUP * 8), GROUP * 8)
            place = [table[r, g * GROUP + k] for k in range(GROUP)]
            total = jnp.zeros((GROUP * 8, LANES), F32)
            for q in range(4):
                value = jnp.concatenate(
                    [cand[r][p + q * TILES_SLOTS] for p in place], axis=0
                )
                total += value * value
                value = -2.0 * value
                high = value.astype(BF16)
                ch[r, at, q * LANES:(q + 1) * LANES] = high
                cl[r, at, q * LANES:(q + 1) * LANES] = (value - high.astype(F32)).astype(BF16)
            norm = jnp.broadcast_to(jnp.sum(total, axis=1, keepdims=True), (GROUP * 8, LANES))
            slot = lax.broadcasted_iota(jnp.int32, (8, LANES), 0)
            used = jnp.concatenate(
                [slot < table[ROUNDS + r, g * GROUP + k] for k in range(GROUP)], axis=0
            )
            nrm[r, at, :] = jnp.where(used, norm, jnp.inf)
            return carry

        lax.fori_loop(0, TILES // GROUP, one, 0, unroll=True)

    def prepare(t):
        for copy in near[t] + passed[t]:
            copy.wait_recv()
        at = slice(t % 2 * STEP, (t % 2 + 1) * STEP)
        total = jnp.zeros((LANES, STEP), F32)
        for q in range(4):
            value = xfull[q, t * STEP:(t + 1) * STEP, :].T
            total += value * value
            high = value.astype(BF16)
            xh[t // 2, q * LANES:(q + 1) * LANES, at] = high
            xl[t // 2, q * LANES:(q + 1) * LANES, at] = (value - high.astype(F32)).astype(BF16)
        sq[t // 2, :, at] = jnp.sum(total.reshape(LANES // 8, 8, STEP), axis=0)

    def nearest(t, r):
        high, rows = ch[r], xh[t]
        value = jnp.dot(
            jnp.concatenate([high, cl[r], high], axis=1),
            jnp.concatenate([rows, rows, xl[t]], axis=0),
            preferred_element_type=F32,
        )
        value = value + jnp.concatenate([nrm[r]] * (WIDE // LANES), axis=1)
        low[t, r] = jnp.min(value.reshape(TILES, 8, WIDE), axis=0)

    def finish(t):
        norm = jnp.sum(sq[t], axis=0, keepdims=True)
        best = [jnp.min(low[t, r], axis=0, keepdims=True) for r in range(ROUNDS)]
        for r in range(1, ROUNDS):
            best[r] = jnp.minimum(best[r], best[r - 1])
        done[:, t * WIDE:(t + 1) * WIDE] = jnp.concatenate(
            [jnp.maximum(value + norm, 0.0) for value in best], axis=0
        )

    def many(count, body):
        def one(k, carry):
            body(k)
            return carry

        lax.fori_loop(0, count, one, 0)

    pick_send(0)
    pick_send(1)
    near_send(0)
    first_send(0)
    first_send(1)
    pick_send(2)
    far_send(0)
    near_send(1)
    far_send(1)
    second_send(0)
    far_send(2)
    second_send(1)
    second_pass(0)
    far_pass(0)
    first_send(2)
    second_end(0)
    far_pass(1)
    second_pass(1)
    second_send(2)
    far_send(3)
    far_pass(2)
    convert(0)
    second_end(1)
    near_send(2)
    own_rows.wait()
    prepare(0)
    prepare(1)
    near_send(3)
    nearest(0, 0)
    second_pass(2)
    convert(1)
    nearest(0, 1)
    second_end(2)
    far_pass(3)
    convert(2)
    nearest(0, 2)
    finish(0)
    for copy in started:
        copy.wait_send()
    started.clear()
    prepare(2)
    prepare(3)
    many(ROUNDS, lambda r: nearest(1, r))
    finish(1)

    sums = sum([done[:, k * LANES:(k + 1) * LANES] for k in range(SHARE // LANES)])
    line = jnp.concatenate([sums, jnp.zeros((8 - ROUNDS, LANES), F32)], axis=0)
    part[0] = line
    copies = [send(part.at[0], red_line.at[step - 1], line_device(step)) for step in range(1, 8)]
    for step, copy in enumerate(copies):
        copy.wait_recv()
        line = line + red_line[step]
    part[1] = line
    copies = [send(part.at[1], red_plane.at[step - 1], plane_device(step)) for step in range(1, 16)]
    for step, copy in enumerate(copies):
        copy.wait_recv()
        line = line + red_plane[step]
    cost = jnp.sum(line, axis=1, keepdims=True)[:ROUNDS]
    out_ref[...] = jnp.minimum(CAP, TOTAL * done[...] / cost)

    for copy in started:
        copy.wait_send()


COPIES = ROUNDS * 15 + PIECES * 6 + 22
ANY = pl.BlockSpec(memory_space=pl.ANY)


def local(embeddings, cand_index, cand_count):
    return pl.pallas_call(
        kernel,
        out_shape=jax.ShapeDtypeStruct((ROUNDS, SHARE), F32),
        in_specs=[ANY, ANY, ANY],
        out_specs=pl.BlockSpec(memory_space=pltpu.VMEM),
        scratch_shapes=[
            pltpu.SMEM((ROUNDS, SLOTS), jnp.int32),
            pltpu.SMEM((ROUNDS, ITEMS), jnp.int32),
            pltpu.SMEM((ITEMS + 1,), jnp.int32),
            pltpu.SMEM((2 * ROUNDS, TILES), jnp.int32),
            pltpu.VMEM((ROWS, LANES), F32),
            pltpu.VMEM((4, SHARE, LANES), F32),
            pltpu.VMEM((2, PIECES, STEP // 2, LANES), F32),
            *[pltpu.VMEM((ITEMS * BLOCK, TILE, LANES), F32)] * ROUNDS,
            pltpu.VMEM((ROUNDS, USED, 512), BF16),
            pltpu.VMEM((ROUNDS, USED, 512), BF16),
            pltpu.VMEM((ROUNDS, USED, LANES), F32),
            pltpu.VMEM((PAIRS, 512, WIDE), BF16),
            pltpu.VMEM((PAIRS, 512, WIDE), BF16),
            pltpu.VMEM((PAIRS, 8, WIDE), F32),
            pltpu.VMEM((PAIRS, ROUNDS, 8, WIDE), F32),
            pltpu.VMEM((ROUNDS, SHARE), F32),
            pltpu.VMEM((2, 8, LANES), F32),
            pltpu.VMEM((7, 8, LANES), F32),
            pltpu.VMEM((15, 8, LANES), F32),
            pltpu.SemaphoreType.DMA((4,)),
            pltpu.SemaphoreType.DMA((COPIES,)),
            pltpu.SemaphoreType.DMA((COPIES,)),
        ],
        compiler_params=pltpu.CompilerParams(
            collective_id=0, has_side_effects=True, vmem_limit_bytes=56 * 1024 * 1024
        ),
    )(cand_index, cand_count, embeddings)


def solution(mesh):
    in_specs = (P("item", "dim"), P(None, "item"), P())
    out_specs = P(None, ("item", "dim"))
    return jax.shard_map(local, mesh=mesh, in_specs=in_specs, out_specs=out_specs, check_vma=False)
```

```python
import itertools

import jax
import jax.numpy as jnp
from jax import lax
from jax.experimental import pallas as pl
from jax.experimental.pallas import tpu as pltpu
from jax.sharding import PartitionSpec as P

CAP = 4.0
MESH = pl.DeviceIdType.MESH
ROUNDS = 3
SLOTS = 32
LANES = 128
ITEMS = 32
ROWS = 4096
SHARE = 1024
STEP = 256
PIECES = SHARE // STEP
TOTAL = 131072
TILE = 8
TILES_SLOTS = SLOTS // TILE
BLOCK = 4 * TILES_SLOTS
TILES = 92
USED = TILES * 8
GROUP = 4
BF16 = jnp.bfloat16
F32 = jnp.float32


def kernel(
    index_hbm, count_hbm, x_ref, out_ref,
    index_ref, count_ref, ordered, table, xv, xfull, relay_buf, cand_0, cand_1, cand_2,
    ch, cl, nrm, xh, xl, sq, low, done, part, red_line, red_plane,
    load_sem, send_sem, recv_sem,
):
    cand = (cand_0, cand_1, cand_2)
    item, dim = lax.axis_index("item"), lax.axis_index("dim")
    z, x, core = item // 8, (item // 2) % 4, item % 2
    a = x * (1 - core) + z * core
    b = z * (1 - core) + x * core

    def device(a_, b_):
        return (a_ * (2 + 6 * core) + b_ * (8 - 6 * core) + core, dim)

    def block(b_, a_):
        return ((core * 4 + b_) * 4 + a_) * BLOCK

    a_up, a_down = (a + 1) % 4, (a + 3) % 4
    b_up, b_down, b_far = (b + 1) % 4, (b + 3) % 4, (b + 2) % 4
    y_up, y_down, y_far = (dim + 1) % 4, (dim + 3) % 4, (dim + 2) % 4
    sibling = (item + 1 - 2 * core, dim)
    rank_line, rank_plane = dim * 2 + core, item // 2

    def line_device(step):
        other = (rank_line + step) % 8
        return (item - core + other % 2, other // 2)

    def plane_device(step):
        return (((rank_plane + step) % 16) * 2 + core, dim)

    loads = [
        pltpu.make_async_copy(index_hbm, index_ref, load_sem.at[0]),
        pltpu.make_async_copy(x_ref, xv, load_sem.at[1]),
        pltpu.make_async_copy(count_hbm, count_ref, load_sem.at[2]),
        pltpu.make_async_copy(x_ref.at[pl.ds(dim * SHARE, SHARE)], xfull.at[dim], load_sem.at[3]),
    ]
    for copy in loads:
        copy.start()
    index_load, x_load, count_load, own_rows = loads

    barrier = pltpu.get_barrier_semaphore()
    for step in range(1, 8):
        pl.semaphore_signal(barrier, inc=1, device_id=line_device(step), device_id_type=MESH)
    for step in range(1, 16):
        pl.semaphore_signal(barrier, inc=1, device_id=plane_device(step), device_id_type=MESH)

    index_load.wait()
    x_load.wait()
    for r in range(ROUNDS):
        def pick(g, carry, r=r):
            rows = [xv[pl.ds(index_ref[r, g * TILE + k], 1), :] for k in range(TILE)]
            cand[r][block(b, a) + dim * TILES_SLOTS + g] = jnp.concatenate(rows, axis=0)
            return carry

        lax.fori_loop(0, TILES_SLOTS, pick, 0)
    pl.semaphore_wait(barrier, 22)

    number = itertools.count()
    started = []

    def send(src, dst, target):
        k = next(number)
        copy = pltpu.make_async_remote_copy(
            src_ref=src, dst_ref=dst, send_sem=send_sem.at[k], recv_sem=recv_sem.at[k],
            device_id=target, device_id_type=MESH,
        )
        copy.start()
        started.append(copy)
        return copy

    def send_cand(r, start, length, target):
        ref = cand[r].at[pl.ds(start, length)]
        return send(ref, ref, target)

    y_copies, first, second_up, second_down, pass_up, pass_down, swap = [{} for _ in range(7)]
    relay, near, passed = [{} for _ in range(3)]

    def pick_send(r):
        start = block(b, a) + dim * TILES_SLOTS
        y_copies[r] = [send_cand(r, start, TILES_SLOTS, (item, (dim + d) % 4)) for d in (1, 3, 2)]

    half = STEP // 2

    def near_send(t):
        lands = xfull.at[dim, pl.ds(t * STEP, STEP)]
        near[t] = (
            send(xv.at[pl.ds(y_up * SHARE + t * STEP, STEP)], lands, (item, y_up)),
            send(xv.at[pl.ds(y_down * SHARE + t * STEP, STEP)], lands, (item, y_down)),
        )

    def far_send(t):
        far = y_far * SHARE + t * STEP
        relay[t] = (
            send(xv.at[pl.ds(far, half)], relay_buf.at[0, t], (item, y_up)),
            send(xv.at[pl.ds(far + half, half)], relay_buf.at[1, t], (item, y_down)),
        )

    def far_pass(t):
        relay[t][0].wait_recv()
        up = send(relay_buf.at[0, t], xfull.at[y_down, pl.ds(t * STEP, half)], (item, y_up))
        relay[t][1].wait_recv()
        down = send(relay_buf.at[1, t], xfull.at[y_up, pl.ds(t * STEP + half, half)], (item, y_down))
        passed[t] = (up, down)

    def first_send(r):
        for copy in y_copies[r]:
            copy.wait_recv()
        first[r] = [send_cand(r, block(b, a), BLOCK, device(a_, b)) for a_ in (a_up, a_down)]

    def first_pass(r):
        first[r][0].wait_recv()
        up = send_cand(r, block(b, a_down), BLOCK // 2, device(a_up, b))
        first[r][1].wait_recv()
        down = send_cand(r, block(b, a_up) + BLOCK // 2, BLOCK // 2, device(a_down, b))
        first[r] = (up, down)

    def second_send(r):
        for copy in first[r]:
            copy.wait_recv()
        second_up[r] = send_cand(r, block(b, 0), 4 * BLOCK, device(a, b_up))
        second_down[r] = send_cand(r, block(b, 0), 4 * BLOCK, device(a, b_down))
        swap[r] = [send_cand(r, block(b, 0), 4 * BLOCK, sibling)]

    def second_pass(r):
        second_up[r].wait_recv()
        pass_up[r] = send_cand(r, block(b_down, 0), 2 * BLOCK, device(a, b_up))
        swap[r].append(send_cand(r, block(b_down, 0), 4 * BLOCK, sibling))
        second_down[r].wait_recv()
        pass_down[r] = send_cand(r, block(b_up, 2), 2 * BLOCK, device(a, b_down))
        swap[r].append(send_cand(r, block(b_up, 0), 4 * BLOCK, sibling))

    def second_end(r):
        pass_up[r].wait_recv()
        swap[r].append(send_cand(r, block(b_far, 0), 2 * BLOCK, sibling))
        pass_down[r].wait_recv()
        swap[r].append(send_cand(r, block(b_far, 2), 2 * BLOCK, sibling))

    def tabulate(r):
        for k in range(ITEMS):
            core_, b_, a_ = k // 16, (k // 4) % 4, k % 4
            ordered[k] = count_ref[r, a_ * (2 + 6 * core_) + b_ * (8 - 6 * core_) + core_]
        ordered[ITEMS] = jnp.int32(0)

        def entry(p, carry):
            k, o, rest = carry
            table[r, p] = jnp.minimum(k, ITEMS - 1) * BLOCK + o
            table[ROUNDS + r, p] = rest
            later = jnp.minimum(k + 1, ITEMS)
            later_count = ordered[later]
            more = rest > 8
            return jnp.where(more, k, later), jnp.where(more, o + 1, 0), jnp.where(more, rest - 8, later_count)

        lax.fori_loop(0, TILES, entry, (jnp.int32(0), jnp.int32(0), ordered[0]), unroll=4)

    def convert(r):
        for copy in swap[r]:
            copy.wait_recv()

        def one(g, carry):
            at = pl.ds(pl.multiple_of(g * (GROUP * 8), GROUP * 8), GROUP * 8)
            place = [table[r, g * GROUP + k] for k in range(GROUP)]
            total = jnp.zeros((GROUP * 8, LANES), F32)
            for q in range(4):
                value = jnp.concatenate(
                    [cand[r][p + q * TILES_SLOTS] for p in place], axis=0
                )
                total += value * value
                value = -2.0 * value
                high = value.astype(BF16)
                ch[r, at, q * LANES:(q + 1) * LANES] = high
                cl[r, at, q * LANES:(q + 1) * LANES] = (value - high.astype(F32)).astype(BF16)
            norm = jnp.broadcast_to(jnp.sum(total, axis=1, keepdims=True), (GROUP * 8, LANES))
            slot = lax.broadcasted_iota(jnp.int32, (8, LANES), 0)
            used = jnp.concatenate(
                [slot < table[ROUNDS + r, g * GROUP + k] for k in range(GROUP)], axis=0
            )
            nrm[r, at, :] = jnp.where(used, norm, jnp.inf)
            return carry

        lax.fori_loop(0, TILES // GROUP, one, 0, unroll=True)

    def prepare(t):
        for copy in near[t] + passed[t]:
            copy.wait_recv()
        total = jnp.zeros((LANES, STEP), F32)
        for q in range(4):
            value = xfull[q, t * STEP:(t + 1) * STEP, :].T
            total += value * value
            high = value.astype(BF16)
            xh[t, q * LANES:(q + 1) * LANES, :] = high
            xl[t, q * LANES:(q + 1) * LANES, :] = (value - high.astype(F32)).astype(BF16)
        sq[t] = jnp.sum(total.reshape(LANES // 8, 8, STEP), axis=0)

    def nearest(t, r):
        high, rows = ch[r], xh[t]
        value = jnp.dot(
            jnp.concatenate([high, cl[r], high], axis=1),
            jnp.concatenate([rows, rows, xl[t]], axis=0),
            preferred_element_type=F32,
        )
        value = value + jnp.concatenate([nrm[r]] * (STEP // LANES), axis=1)
        low[t, r] = jnp.min(value.reshape(TILES, 8, STEP), axis=0)

    def finish(t):
        norm = jnp.sum(sq[t], axis=0, keepdims=True)
        best = [jnp.min(low[t, r], axis=0, keepdims=True) for r in range(ROUNDS)]
        for r in range(1, ROUNDS):
            best[r] = jnp.minimum(best[r], best[r - 1])
        done[:, t * STEP:(t + 1) * STEP] = jnp.concatenate(
            [jnp.maximum(value + norm, 0.0) for value in best], axis=0
        )

    def many(count, body):
        def one(k, carry):
            body(k)
            return carry

        lax.fori_loop(0, count, one, 0)

    pick_send(0)
    count_load.wait()
    tabulate(0)
    pick_send(1)
    first_send(0)
    pick_send(2)
    tabulate(1)
    far_send(0)
    first_send(1)
    far_send(1)
    first_pass(0)
    first_send(2)
    first_pass(1)
    second_send(0)
    near_send(0)
    second_send(1)
    tabulate(2)
    far_send(2)
    far_pass(0)
    second_pass(0)
    near_send(1)
    first_pass(2)
    far_pass(1)
    second_pass(1)
    own_rows.wait()
    prepare(0)
    second_end(0)
    far_pass(2)
    near_send(2)
    second_send(2)
    far_send(3)
    second_end(1)
    convert(0)
    nearest(0, 0)
    convert(1)
    second_pass(2)
    prepare(1)
    near_send(3)
    nearest(1, 0)
    many(2, lambda t: nearest(t, 1))
    second_end(2)
    prepare(2)
    far_pass(3)
    many(2, lambda r: nearest(2, r))
    convert(2)
    many(3, lambda t: nearest(t, 2))
    for t in range(PIECES - 1):
        finish(t)
    for copy in started:
        copy.wait_send()
    started.clear()
    prepare(PIECES - 1)
    many(ROUNDS, lambda r: nearest(PIECES - 1, r))
    finish(PIECES - 1)

    sums = sum([done[:, k * LANES:(k + 1) * LANES] for k in range(SHARE // LANES)])
    line = jnp.concatenate([sums, jnp.zeros((8 - ROUNDS, LANES), F32)], axis=0)
    part[0] = line
    copies = [send(part.at[0], red_line.at[step - 1], line_device(step)) for step in range(1, 8)]
    for step, copy in enumerate(copies):
        copy.wait_recv()
        line = line + red_line[step]
    part[1] = line
    copies = [send(part.at[1], red_plane.at[step - 1], plane_device(step)) for step in range(1, 16)]
    for step, copy in enumerate(copies):
        copy.wait_recv()
        line = line + red_plane[step]
    cost = jnp.sum(line, axis=1, keepdims=True)[:ROUNDS]
    out_ref[...] = jnp.minimum(CAP, TOTAL * done[...] / cost)

    for copy in started:
        copy.wait_send()


COPIES = ROUNDS * 16 + PIECES * 6 + 22
ANY = pl.BlockSpec(memory_space=pl.ANY)


def local(embeddings, cand_index, cand_count):
    return pl.pallas_call(
        kernel,
        out_shape=jax.ShapeDtypeStruct((ROUNDS, SHARE), F32),
        in_specs=[ANY, ANY, ANY],
        out_specs=pl.BlockSpec(memory_space=pltpu.VMEM),
        scratch_shapes=[
            pltpu.SMEM((ROUNDS, SLOTS), jnp.int32),
            pltpu.SMEM((ROUNDS, ITEMS), jnp.int32),
            pltpu.SMEM((ITEMS + 1,), jnp.int32),
            pltpu.SMEM((2 * ROUNDS, TILES), jnp.int32),
            pltpu.VMEM((ROWS, LANES), F32),
            pltpu.VMEM((4, SHARE, LANES), F32),
            pltpu.VMEM((2, PIECES, STEP // 2, LANES), F32),
            *[pltpu.VMEM((ITEMS * BLOCK, TILE, LANES), F32)] * ROUNDS,
            pltpu.VMEM((ROUNDS, USED, 512), BF16),
            pltpu.VMEM((ROUNDS, USED, 512), BF16),
            pltpu.VMEM((ROUNDS, USED, LANES), F32),
            pltpu.VMEM((PIECES, 512, STEP), BF16),
            pltpu.VMEM((PIECES, 512, STEP), BF16),
            pltpu.VMEM((PIECES, 8, STEP), F32),
            pltpu.VMEM((PIECES, ROUNDS, 8, STEP), F32),
            pltpu.VMEM((ROUNDS, SHARE), F32),
            pltpu.VMEM((2, 8, LANES), F32),
            pltpu.VMEM((7, 8, LANES), F32),
            pltpu.VMEM((15, 8, LANES), F32),
            pltpu.SemaphoreType.DMA((4,)),
            pltpu.SemaphoreType.DMA((COPIES,)),
            pltpu.SemaphoreType.DMA((COPIES,)),
        ],
        compiler_params=pltpu.CompilerParams(
            collective_id=0, has_side_effects=True, vmem_limit_bytes=56 * 1024 * 1024
        ),
    )(cand_index, cand_count, embeddings)


def solution(mesh):
    in_specs = (P("item", "dim"), P(None, "item"), P())
    out_specs = P(None, ("item", "dim"))
    return jax.shard_map(local, mesh=mesh, in_specs=in_specs, out_specs=out_specs, check_vma=False)
```

```python
import itertools

import jax
import jax.numpy as jnp
from jax import lax
from jax.experimental import pallas as pl
from jax.experimental.pallas import tpu as pltpu
from jax.sharding import PartitionSpec as P

CAP = 4.0
MESH = pl.DeviceIdType.MESH
ROUNDS = 3
SLOTS = 32
LANES = 128
ROWS = 4096
SHARE = 1024
STEP = 512
PIECES = SHARE // STEP
TOTAL = 131072
USED = 512
OFFSET = (0, 3, 1, 2)
BF16 = jnp.bfloat16
F32 = jnp.float32


def exchange(index_ref, x_ref, xfull, cand_0, cand_1, cand_2, xv, picked, relay_buf, load_sem, send_sem, recv_sem):
    cand = (cand_0, cand_1, cand_2)
    item, dim = lax.axis_index("item"), lax.axis_index("dim")
    z, x, core = item // 8, (item // 2) % 4, item % 2
    a = x * (1 - core) + z * core
    b = z * (1 - core) + x * core

    def device(a_, b_):
        return (a_ * (2 + 6 * core) + b_ * (8 - 6 * core) + core, dim)

    up_a, down_a = device((a + 1) % 4, b), device((a + 3) % 4, b)
    up_b, down_b = device(a, (b + 1) % 4), device(a, (b + 3) % 4)
    y_up, y_down, y_far = (dim + 1) % 4, (dim + 3) % 4, (dim + 2) % 4
    up_y, down_y, far_y = (item, y_up), (item, y_down), (item, y_far)
    sibling = (item + 1 - 2 * core, dim)

    load = pltpu.make_async_copy(x_ref, xv, load_sem.at[0])
    load.start()
    own_rows = pltpu.make_async_copy(
        x_ref.at[pl.ds(dim * SHARE, SHARE)], xfull.at[dim], load_sem.at[1]
    )
    own_rows.start()

    barrier = pltpu.get_barrier_semaphore()
    partners = [up_y, down_y, far_y, sibling, up_a, down_a, up_b, down_b]
    for partner in partners:
        pl.semaphore_signal(barrier, inc=1, device_id=partner, device_id_type=MESH)

    load.wait()

    def pick(g, carry):
        r, s = g // 4, (g % 4) * 8
        rows = [xv[pl.ds(index_ref[r, s + k], 1), :] for k in range(8)]
        picked[dim, r, pl.ds(pl.multiple_of(s, 8), 8), :] = jnp.concatenate(rows, axis=0)
        return carry

    lax.fori_loop(0, ROUNDS * 4, pick, 0)
    pl.semaphore_wait(barrier, len(partners))

    number = itertools.count()
    started = []

    def send(src, dst, target):
        k = next(number)
        copy = pltpu.make_async_remote_copy(
            src_ref=src, dst_ref=dst, send_sem=send_sem.at[k], recv_sem=recv_sem.at[k],
            device_id=target, device_id_type=MESH,
        )
        copy.start()
        started.append(copy)
        return copy

    y_copies = [send(picked.at[dim], picked.at[dim], target) for target in (up_y, down_y, far_y)]

    half = STEP // 2
    relay, near, passed, first, second, swap = {}, {}, {}, {}, {}, {}

    def near_send(t):
        lands = xfull.at[dim, pl.ds(t * STEP, STEP)]
        near[t] = (
            send(xv.at[pl.ds(y_up * SHARE + t * STEP, STEP)], lands, up_y),
            send(xv.at[pl.ds(y_down * SHARE + t * STEP, STEP)], lands, down_y),
        )

    def far_send(t):
        far = y_far * SHARE + t * STEP
        relay[t] = (
            send(xv.at[pl.ds(far, half)], relay_buf.at[0, t], up_y),
            send(xv.at[pl.ds(far + half, half)], relay_buf.at[1, t], down_y),
        )

    def far_pass(t):
        relay[t][0].wait_recv()
        up = send(relay_buf.at[0, t], xfull.at[y_down, pl.ds(t * STEP, half)], up_y)
        relay[t][1].wait_recv()
        down = send(relay_buf.at[1, t], xfull.at[y_up, pl.ds(t * STEP + half, half)], down_y)
        passed[t] = (up, down)

    def first_send(r):
        block = cand[r].at[core, 0, 0]
        own = pltpu.make_async_copy(picked.at[:, r], block, load_sem.at[2 + r])
        own.start()
        own.wait()
        first[r] = (send(block, cand[r].at[core, 0, 1], up_a), send(block, cand[r].at[core, 0, 2], down_a))

    def first_pass(r):
        first[r][0].wait_recv()
        up = send(cand[r].at[core, 0, 1, pl.ds(0, 2)], cand[r].at[core, 0, 3, pl.ds(0, 2)], up_a)
        first[r][1].wait_recv()
        down = send(cand[r].at[core, 0, 2, pl.ds(2, 2)], cand[r].at[core, 0, 3, pl.ds(2, 2)], down_a)
        first[r] = (up, down)

    def second_send(r):
        for copy in first[r]:
            copy.wait_recv()
        bundle = cand[r].at[core, 0]
        second[r] = (send(bundle, cand[r].at[core, 1], up_b), send(bundle, cand[r].at[core, 2], down_b))

    def second_pass(r):
        second[r][0].wait_recv()
        up = send(cand[r].at[core, 1, pl.ds(0, 2)], cand[r].at[core, 3, pl.ds(0, 2)], up_b)
        second[r][1].wait_recv()
        down = send(cand[r].at[core, 2, pl.ds(2, 2)], cand[r].at[core, 3, pl.ds(2, 2)], down_b)
        second[r] = (up, down)
        ready = cand[r].at[core, pl.ds(0, 3)]
        swap[r] = [send(ready, ready, sibling)]

    def second_end(r):
        for copy in second[r]:
            copy.wait_recv()
        ready = cand[r].at[core, 3]
        swap[r].append(send(ready, ready, sibling))

    far_send(0)
    for copy in y_copies:
        copy.wait_recv()
    for r in range(ROUNDS):
        first_send(r)
    near_send(0)
    far_send(1)
    for r in range(ROUNDS):
        first_pass(r)
    far_pass(0)
    near_send(1)
    for r in range(ROUNDS):
        second_send(r)
    second_pass(0)
    far_pass(1)
    second_end(0)
    second_pass(1)
    second_end(1)
    second_pass(2)
    second_end(2)
    own_rows.wait()
    for copies in (*swap.values(), *near.values(), *passed.values()):
        for copy in copies:
            copy.wait_recv()
    for copy in started:
        copy.wait_send()


def distances(count_ref, cand_0, cand_1, cand_2, x_ref, out_ref, xv, cv, squeezed, ch, cl, nrm, xh, xl, sq, low, load_sem):
    loads = [pltpu.make_async_copy(x_ref, xv, load_sem.at[ROUNDS])]
    for r, ref in enumerate((cand_0, cand_1, cand_2)):
        loads.append(pltpu.make_async_copy(ref, cv.at[r], load_sem.at[r]))
    for load in loads:
        load.start()
    item = lax.axis_index("item")
    x, z = (item // 2) % 4, item // 8

    loads[0].wait()

    def prepare(t, carry):
        at = pl.ds(pl.multiple_of(t * STEP, STEP), STEP)
        total = jnp.zeros((LANES, STEP), F32)
        for q in range(4):
            value = xv[q, at, :].T
            total += value * value
            high = value.astype(BF16)
            xh[t, q * LANES:(q + 1) * LANES, :] = high
            xl[t, q * LANES:(q + 1) * LANES, :] = (value - high.astype(F32)).astype(BF16)
        sq[t] = jnp.sum(total.reshape(LANES // 8, 8, STEP), axis=0)
        return carry

    lax.fori_loop(0, PIECES, prepare, 0)

    for r in range(ROUNDS):
        loads[r + 1].wait()

        start = 0
        for core_ in range(2):
            for b_ in range(4):
                for a_ in range(4):
                    for q in range(4):
                        squeezed[q, pl.ds(start, SLOTS), :] = cv[r, core_, b_, a_, q]
                    x_ = (x + OFFSET[b_ if core_ else a_]) % 4
                    z_ = (z + OFFSET[a_ if core_ else b_]) % 4
                    start = start + count_ref[r, z_ * 8 + x_ * 2 + core_]

        def convert(k, carry):
            at = pl.ds(pl.multiple_of(k * 64, 64), 64)
            total = jnp.zeros((64, LANES), F32)
            for q in range(4):
                value = squeezed[q, at, :]
                total += value * value
                value = -2.0 * value
                high = value.astype(BF16)
                ch[at, q * LANES:(q + 1) * LANES] = high
                cl[at, q * LANES:(q + 1) * LANES] = (value - high.astype(F32)).astype(BF16)
            nrm[at, :] = jnp.broadcast_to(jnp.sum(total, axis=1, keepdims=True), (64, LANES))
            return carry

        lax.fori_loop(0, USED // 64, convert, 0, unroll=True)

        def nearest(t, carry):
            high, rows = ch[...], xh[t]
            value = jnp.dot(
                jnp.concatenate([high, cl[...], high], axis=1),
                jnp.concatenate([rows, rows, xl[t]], axis=0),
                preferred_element_type=F32,
            )
            value = value + jnp.concatenate([nrm[...]] * (STEP // LANES), axis=1)
            low[r, t] = jnp.min(value.reshape(USED // 8, 8, STEP), axis=0)
            return carry

        lax.fori_loop(0, PIECES, nearest, 0)

    def along(parts):
        return jnp.concatenate(parts, axis=1)

    norm = along([jnp.sum(sq[t], axis=0, keepdims=True) for t in range(PIECES)])
    best = [along([jnp.min(low[r, t], axis=0, keepdims=True) for t in range(PIECES)]) for r in range(ROUNDS)]
    for r in range(1, ROUNDS):
        best[r] = jnp.minimum(best[r], best[r - 1])
    out_ref[...] = jnp.concatenate([jnp.maximum(value + norm, 0.0) for value in best], axis=0)


def scale(best_ref, out_ref, part, landed, send_sem, recv_sem):
    item, dim = lax.axis_index("item"), lax.axis_index("dim")
    core = item % 2
    x, z = (item // 2) % 4, item // 8

    def line_device(step):
        other = (dim * 2 + core + step) % 8
        return (item - core + other % 2, other // 2)

    groups = (
        [line_device(step) for step in range(1, 8)],
        [(z * 8 + (x + step) % 4 * 2 + core, dim) for step in range(1, 4)],
        [((z + step) % 4 * 8 + x * 2 + core, dim) for step in range(1, 4)],
    )
    barrier = pltpu.get_barrier_semaphore()
    for group in groups:
        for target in group:
            pl.semaphore_signal(barrier, inc=1, device_id=target, device_id_type=MESH)
    best = best_ref[...]
    sums = sum([best[:, k * LANES:(k + 1) * LANES] for k in range(SHARE // LANES)])
    line = jnp.concatenate([sums, jnp.zeros((8 - ROUNDS, LANES), F32)], axis=0)
    pl.semaphore_wait(barrier, REDUCES)

    copies = []

    def send(src, dst, target):
        k = len(copies)
        copy = pltpu.make_async_remote_copy(
            src_ref=src, dst_ref=dst, send_sem=send_sem.at[k], recv_sem=recv_sem.at[k],
            device_id=target, device_id_type=MESH,
        )
        copy.start()
        copies.append(copy)

    for stage, group in enumerate(groups):
        part[stage] = line
        first = len(copies)
        for target in group:
            send(part.at[stage], landed.at[len(copies)], target)
        for k in range(first, len(copies)):
            copies[k].wait_recv()
            line = line + landed[k]
    cost = jnp.sum(line, axis=1, keepdims=True)[:ROUNDS]
    out_ref[...] = jnp.minimum(CAP, TOTAL * best / cost)
    for copy in copies:
        copy.wait_send()


COPIES = 3 + ROUNDS * 10 + PIECES * 6
REDUCES = 13
SMEM = pl.BlockSpec(memory_space=pltpu.SMEM)
VMEM = pl.BlockSpec(memory_space=pltpu.VMEM)
ANY = pl.BlockSpec(memory_space=pl.ANY)
MIB = 1024 * 1024


def local(embeddings, cand_index, cand_count):
    rows, *candidates = pl.pallas_call(
        exchange,
        out_shape=(
            jax.ShapeDtypeStruct((4, SHARE, LANES), F32),
            *[jax.ShapeDtypeStruct((2, 4, 4, 4, SLOTS, LANES), F32)] * ROUNDS,
        ),
        in_specs=[SMEM, ANY],
        out_specs=(ANY,) * (1 + ROUNDS),
        scratch_shapes=[
            pltpu.VMEM((ROWS, LANES), F32),
            pltpu.VMEM((4, ROUNDS, SLOTS, LANES), F32),
            pltpu.VMEM((2, PIECES, STEP // 2, LANES), F32),
            pltpu.SemaphoreType.DMA((2 + ROUNDS,)),
            pltpu.SemaphoreType.DMA((COPIES,)),
            pltpu.SemaphoreType.DMA((COPIES,)),
        ],
        compiler_params=pltpu.CompilerParams(
            collective_id=0, has_side_effects=True, vmem_limit_bytes=56 * MIB
        ),
    )(cand_index, embeddings)
    best = pl.pallas_call(
        distances,
        out_shape=jax.ShapeDtypeStruct((ROUNDS, SHARE), F32),
        in_specs=[SMEM] + [ANY] * (ROUNDS + 1),
        out_specs=VMEM,
        scratch_shapes=[
            pltpu.VMEM((4, SHARE, LANES), F32),
            pltpu.VMEM((ROUNDS, 2, 4, 4, 4, SLOTS, LANES), F32),
            pltpu.VMEM((4, USED + SLOTS, LANES), F32),
            pltpu.VMEM((USED, 512), BF16),
            pltpu.VMEM((USED, 512), BF16),
            pltpu.VMEM((USED, LANES), F32),
            pltpu.VMEM((PIECES, 512, STEP), BF16),
            pltpu.VMEM((PIECES, 512, STEP), BF16),
            pltpu.VMEM((PIECES, 8, STEP), F32),
            pltpu.VMEM((ROUNDS, PIECES, 8, STEP), F32),
            pltpu.SemaphoreType.DMA((ROUNDS + 1,)),
        ],
        compiler_params=pltpu.CompilerParams(vmem_limit_bytes=56 * MIB),
    )(cand_count, *candidates, rows)
    return pl.pallas_call(
        scale,
        out_shape=jax.ShapeDtypeStruct((ROUNDS, SHARE), F32),
        in_specs=[VMEM],
        out_specs=VMEM,
        scratch_shapes=[
            pltpu.VMEM((3, 8, LANES), F32),
            pltpu.VMEM((REDUCES, 8, LANES), F32),
            pltpu.SemaphoreType.DMA((REDUCES,)),
            pltpu.SemaphoreType.DMA((REDUCES,)),
        ],
        compiler_params=pltpu.CompilerParams(collective_id=1, has_side_effects=True),
    )(best)


def solution(mesh):
    in_specs = (P("item", "dim"), P(None, "item"), P())
    out_specs = P(None, ("item", "dim"))
    return jax.shard_map(local, mesh=mesh, in_specs=in_specs, out_specs=out_specs, check_vma=False)
```

```python
import itertools

import jax
import jax.numpy as jnp
from jax import lax
from jax.experimental import pallas as pl
from jax.experimental.pallas import tpu as pltpu
from jax.sharding import PartitionSpec as P

CAP = 4.0
MESH = pl.DeviceIdType.MESH
ROUNDS = 3
SLOTS = 32
LANES = 128
ITEMS = 32
ROWS = 4096
SHARE = 1024
STEP = 256
PIECES = SHARE // STEP
WIDE = 512
PAIRS = SHARE // WIDE
TOTAL = 131072
TILE = 8
QUARTER = SLOTS // TILE
BLOCK = 4 * QUARTER
BUNDLE = 4 * BLOCK
HALF = 4 * BUNDLE
OFFSET = (0, 3, 1, 2)
TILES = 92
USED = TILES * 8
GROUP = 4
BF16 = jnp.bfloat16
F32 = jnp.float32


def kernel(
    index_hbm, count_hbm, x_ref, out_ref,
    index_ref, count_ref, ordered, table, xv, xfull, relay_buf, cand_0, cand_1, cand_2,
    ch, cl, nrm, xh, xl, sq, low, done, part, red_line, red_plane,
    load_sem, send_sem, recv_sem, cost_sem,
):
    cand = (cand_0, cand_1, cand_2)
    item, dim = lax.axis_index("item"), lax.axis_index("dim")
    z = lax.div(item, 8)
    x = lax.div(item - z * 8, 2)
    core = item - z * 8 - x * 2

    def ring(place):
        return [place] + [jnp.where(place + k > 3, place + k - 4, place + k) for k in range(1, 4)]

    xs, ys, zs = ring(x), ring(dim), ring(z)
    sibling = item + 1 - 2 * core

    def plane(dz, dx):
        return (zs[dz] * 8 + xs[dx] * 2 + core, dim)

    def axis(k, first):
        over_x, over_z = plane(0, k)[0], plane(k, 0)[0]
        lead = 1 - core if first else core
        return (over_z + lead * (over_x - over_z), dim)

    up_a, far_a, down_a = [axis(k, True) for k in range(1, 4)]
    up_b, far_b, down_b = [axis(k, False) for k in range(1, 4)]
    up_y, far_y, down_y = [(item, ys[k]) for k in range(1, 4)]
    _, y_up, y_far, y_down = ys
    line_devices = [(sibling, dim)]
    for k in range(1, 4):
        line_devices += [(item, ys[k]), (sibling, ys[k])]
    plane_devices = [plane(dz, dx) for dz in range(4) for dx in range(4) if dz or dx]

    loads = [
        pltpu.make_async_copy(index_hbm, index_ref, load_sem.at[0]),
        pltpu.make_async_copy(x_ref, xv, load_sem.at[1]),
        pltpu.make_async_copy(count_hbm, count_ref, load_sem.at[2]),
        pltpu.make_async_copy(x_ref.at[pl.ds(dim * SHARE, SHARE)], xfull.at[dim], load_sem.at[3]),
    ]
    for copy in loads:
        copy.start()
    index_load, x_load, count_load, own_rows = loads

    barrier = pltpu.get_barrier_semaphore()
    for target in line_devices + plane_devices:
        pl.semaphore_signal(barrier, inc=1, device_id=target, device_id_type=MESH)

    index_load.wait()
    x_load.wait()
    for r in range(ROUNDS):
        def pick(g, carry, r=r):
            rows = [xv[pl.ds(index_ref[r, g * TILE + k], 1), :] for k in range(TILE)]
            cand[r][core * HALF + dim * QUARTER + g] = jnp.concatenate(rows, axis=0)
            return carry

        lax.fori_loop(0, QUARTER, pick, 0, unroll=True)
    pl.semaphore_wait(barrier, REDUCES)

    number = itertools.count()

    def send(src, dst, target, group):
        k = next(number)
        copy = pltpu.make_async_remote_copy(
            src_ref=src, dst_ref=dst, send_sem=send_sem.at[group], recv_sem=recv_sem.at[k],
            device_id=target, device_id_type=MESH,
        )
        copy.start()
        return copy

    def sent(ref, group):
        pltpu.make_async_copy(ref, ref, send_sem.at[group]).wait()

    half = STEP // 2
    y_copies, first, second, passes, swap, relay, near, passed = [{} for _ in range(8)]

    def near_send(t):
        lands = xfull.at[dim, pl.ds(t * STEP, STEP)]
        near[t] = (
            send(xv.at[pl.ds(y_up * SHARE + t * STEP, STEP)], lands, up_y, NEAR),
            send(xv.at[pl.ds(y_down * SHARE + t * STEP, STEP)], lands, down_y, NEAR),
        )

    def far_send(t):
        far = y_far * SHARE + t * STEP
        relay[t] = (
            send(xv.at[pl.ds(far, half)], relay_buf.at[0, t], up_y, RELAY),
            send(xv.at[pl.ds(far + half, half)], relay_buf.at[1, t], down_y, RELAY),
        )

    def far_pass(t):
        relay[t][0].wait_recv()
        up = send(relay_buf.at[0, t], xfull.at[y_down, pl.ds(t * STEP, half)], up_y, PASSED)
        relay[t][1].wait_recv()
        down = send(relay_buf.at[1, t], xfull.at[y_up, pl.ds(t * STEP + half, half)], down_y, PASSED)
        passed[t] = (up, down)

    def tiles(r, start, count):
        return cand[r].at[pl.ds(core * HALF + start, count)]

    def pick_send(r):
        ref = tiles(r, dim * QUARTER, QUARTER)
        y_copies[r] = [send(ref, ref, target, PICK + r) for target in (up_y, down_y, far_y)]

    def first_send(r):
        for copy in y_copies[r]:
            copy.wait_recv()
        block = tiles(r, 0, BLOCK)
        first[r] = [
            send(block, tiles(r, k * BLOCK, BLOCK), target, FIRST + r)
            for k, target in ((3, far_a), (1, up_a), (2, down_a))
        ]

    def second_send(r):
        for copy in first[r]:
            copy.wait_recv()
        bundle = tiles(r, 0, BUNDLE)
        second[r] = (
            send(bundle, tiles(r, BUNDLE, BUNDLE), up_b, SECOND + r),
            send(bundle, tiles(r, 2 * BUNDLE, BUNDLE), down_b, SECOND + r),
        )
        swap[r] = [send(bundle, bundle, (sibling, dim), SWAP + r)]

    def second_pass(r):
        part = 2 * BLOCK
        second[r][0].wait_recv()
        up = send(tiles(r, BUNDLE, part), tiles(r, 3 * BUNDLE, part), up_b, SECOND + r)
        second[r][1].wait_recv()
        down = send(tiles(r, 2 * BUNDLE + part, part), tiles(r, 3 * BUNDLE + part, part), down_b, SECOND + r)
        passes[r] = (up, down)
        ready = tiles(r, BUNDLE, 2 * BUNDLE)
        swap[r].append(send(ready, ready, (sibling, dim), SWAP + r))

    def second_end(r):
        for copy in passes[r]:
            copy.wait_recv()
        ready = tiles(r, 3 * BUNDLE, BUNDLE)
        swap[r].append(send(ready, ready, (sibling, dim), SWAP + r))

    def tabulate(r):
        for k in range(ITEMS):
            core_, b_, a_ = k // 16, (k // 4) % 4, k % 4
            x_, z_ = xs[OFFSET[b_ if core_ else a_]], zs[OFFSET[a_ if core_ else b_]]
            ordered[k] = count_ref[r, z_ * 8 + x_ * 2 + core_]
        ordered[ITEMS] = jnp.int32(0)

        def entry(p, carry):
            k, o, rest = carry
            table[r, p] = jnp.minimum(k, ITEMS - 1) * BLOCK + o
            table[ROUNDS + r, p] = rest
            later = jnp.minimum(k + 1, ITEMS)
            later_count = ordered[later]
            more = rest > 8
            return jnp.where(more, k, later), jnp.where(more, o + 1, 0), jnp.where(more, rest - 8, later_count)

        lax.fori_loop(0, TILES, entry, (jnp.int32(0), jnp.int32(0), ordered[0]), unroll=4)

    def convert(r):
        for copy in swap[r]:
            copy.wait_recv()

        def one(g, carry):
            at = pl.ds(pl.multiple_of(g * (GROUP * 8), GROUP * 8), GROUP * 8)
            place = [table[r, g * GROUP + k] for k in range(GROUP)]
            total = jnp.zeros((GROUP * 8, LANES), F32)
            for q in range(4):
                value = jnp.concatenate(
                    [cand[r][p + q * QUARTER] for p in place], axis=0
                )
                total += value * value
                value = -2.0 * value
                high = value.astype(BF16)
                ch[r, at, q * LANES:(q + 1) * LANES] = high
                cl[r, at, q * LANES:(q + 1) * LANES] = (value - high.astype(F32)).astype(BF16)
            norm = jnp.broadcast_to(jnp.sum(total, axis=1, keepdims=True), (GROUP * 8, LANES))
            slot = lax.broadcasted_iota(jnp.int32, (8, LANES), 0)
            used = jnp.concatenate(
                [slot < table[ROUNDS + r, g * GROUP + k] for k in range(GROUP)], axis=0
            )
            nrm[r, at, :] = jnp.where(used, norm, jnp.inf)
            return carry

        lax.fori_loop(0, TILES // GROUP, one, 0, unroll=True)

    def prepare(t):
        for copy in near[t] + passed[t]:
            copy.wait_recv()
        at = slice(t % 2 * STEP, (t % 2 + 1) * STEP)
        total = jnp.zeros((LANES, STEP), F32)
        for q in range(4):
            value = xfull[q, t * STEP:(t + 1) * STEP, :].T
            total += value * value
            high = value.astype(BF16)
            xh[t // 2, q * LANES:(q + 1) * LANES, at] = high
            xl[t // 2, q * LANES:(q + 1) * LANES, at] = (value - high.astype(F32)).astype(BF16)
        sq[t // 2, :, at] = jnp.sum(total.reshape(LANES // 8, 8, STEP), axis=0)

    def nearest(t, r):
        high, rows = ch[r], xh[t]
        value = jnp.dot(
            jnp.concatenate([high, cl[r], high], axis=1),
            jnp.concatenate([rows, rows, xl[t]], axis=0),
            preferred_element_type=F32,
        )
        value = value + jnp.concatenate([nrm[r]] * (WIDE // LANES), axis=1)
        low[t, r] = jnp.min(value.reshape(TILES, 8, WIDE), axis=0)

    def finish(t):
        norm = jnp.sum(sq[t], axis=0, keepdims=True)
        best = [jnp.min(low[t, r], axis=0, keepdims=True) for r in range(ROUNDS)]
        for r in range(1, ROUNDS):
            best[r] = jnp.minimum(best[r], best[r - 1])
        done[:, t * WIDE:(t + 1) * WIDE] = jnp.concatenate(
            [jnp.maximum(value + norm, 0.0) for value in best], axis=0
        )

    def many(count, body):
        def one(k, carry):
            body(k)
            return carry

        lax.fori_loop(0, count, one, 0)

    pick_send(0)
    count_load.wait()
    tabulate(0)
    pick_send(1)
    far_send(0)
    first_send(0)
    far_send(1)
    first_send(1)
    near_send(0)
    far_send(2)
    second_send(0)
    far_pass(0)
    tabulate(1)
    pick_send(2)
    second_send(1)
    tabulate(2)
    far_pass(1)
    second_pass(0)
    near_send(1)
    first_send(2)
    own_rows.wait()
    prepare(0)
    second_pass(1)
    near_send(2)
    far_send(3)
    second_end(0)
    far_pass(2)
    second_send(2)
    prepare(1)
    second_end(1)
    near_send(3)
    convert(0)
    nearest(0, 0)
    far_pass(3)
    second_pass(2)
    convert(1)
    nearest(0, 1)
    prepare(2)
    second_end(2)
    prepare(3)
    many(2, lambda r: nearest(1, r))
    for r in range(ROUNDS):
        sent(cand[r].at[pl.ds(0, 3 * QUARTER)], PICK + r)
        sent(cand[r].at[pl.ds(0, 3 * BLOCK)], FIRST + r)
        sent(cand[r].at[pl.ds(0, 3 * BUNDLE)], SECOND + r)
        sent(cand[r].at[pl.ds(0, HALF)], SWAP + r)
    sent(xfull.at[pl.ds(0, 1)], RELAY)
    sent(xfull.at[pl.ds(0, 2)], NEAR)
    sent(xfull.at[pl.ds(0, 1)], PASSED)
    convert(2)
    many(PAIRS, lambda t: nearest(t, 2))
    for t in range(PAIRS):
        finish(t)

    sums = sum([done[:, k * LANES:(k + 1) * LANES] for k in range(SHARE // LANES)])
    line = jnp.concatenate([sums, jnp.zeros((8 - ROUNDS, LANES), F32)], axis=0)
    for stage, (targets, landed) in enumerate(((line_devices, red_line), (plane_devices, red_plane))):
        part[stage] = line
        for k, target in enumerate(targets):
            pltpu.make_async_remote_copy(
                src_ref=part.at[stage], dst_ref=landed.at[k], send_sem=send_sem.at[COST + stage],
                recv_sem=cost_sem.at[stage], device_id=target, device_id_type=MESH,
            ).start()
        pltpu.make_async_copy(landed, landed, cost_sem.at[stage]).wait()
        line = line + jnp.sum(landed[...], axis=0)
    cost = jnp.sum(line, axis=1, keepdims=True)[:ROUNDS]
    out_ref[...] = jnp.minimum(CAP, TOTAL * done[...] / cost)
    sent(red_line, COST)
    sent(red_plane, COST + 1)


COPIES = ROUNDS * 13 + PIECES * 6
REDUCES = 22
PICK, FIRST, SECOND, SWAP, RELAY, NEAR, PASSED, COST = 0, 3, 6, 9, 12, 13, 14, 15
ANY = pl.BlockSpec(memory_space=pl.ANY)


def local(embeddings, cand_index, cand_count):
    return pl.pallas_call(
        kernel,
        out_shape=jax.ShapeDtypeStruct((ROUNDS, SHARE), F32),
        in_specs=[ANY, ANY, ANY],
        out_specs=pl.BlockSpec(memory_space=pltpu.VMEM),
        scratch_shapes=[
            pltpu.SMEM((ROUNDS, SLOTS), jnp.int32),
            pltpu.SMEM((ROUNDS, ITEMS), jnp.int32),
            pltpu.SMEM((ITEMS + 1,), jnp.int32),
            pltpu.SMEM((2 * ROUNDS, TILES), jnp.int32),
            pltpu.VMEM((ROWS, LANES), F32),
            pltpu.VMEM((4, SHARE, LANES), F32),
            pltpu.VMEM((2, PIECES, STEP // 2, LANES), F32),
            *[pltpu.VMEM((ITEMS * BLOCK, TILE, LANES), F32)] * ROUNDS,
            pltpu.VMEM((ROUNDS, USED, 512), BF16),
            pltpu.VMEM((ROUNDS, USED, 512), BF16),
            pltpu.VMEM((ROUNDS, USED, LANES), F32),
            pltpu.VMEM((PAIRS, 512, WIDE), BF16),
            pltpu.VMEM((PAIRS, 512, WIDE), BF16),
            pltpu.VMEM((PAIRS, 8, WIDE), F32),
            pltpu.VMEM((PAIRS, ROUNDS, 8, WIDE), F32),
            pltpu.VMEM((ROUNDS, SHARE), F32),
            pltpu.VMEM((2, 8, LANES), F32),
            pltpu.VMEM((7, 8, LANES), F32),
            pltpu.VMEM((15, 8, LANES), F32),
            pltpu.SemaphoreType.DMA((4,)),
            pltpu.SemaphoreType.DMA((COST + 2,)),
            pltpu.SemaphoreType.DMA((COPIES,)),
            pltpu.SemaphoreType.DMA((2,)),
        ],
        compiler_params=pltpu.CompilerParams(
            collective_id=0, has_side_effects=True, vmem_limit_bytes=56 * 1024 * 1024
        ),
    )(cand_index, cand_count, embeddings)


def solution(mesh):
    in_specs = (P("item", "dim"), P(None, "item"), P())
    out_specs = P(None, ("item", "dim"))
    return jax.shard_map(local, mesh=mesh, in_specs=in_specs, out_specs=out_specs, check_vma=False)
```

```python
import itertools

import jax
import jax.numpy as jnp
from jax import lax
from jax.experimental import pallas as pl
from jax.experimental.pallas import tpu as pltpu
from jax.sharding import PartitionSpec as P

CAP = 4.0
MESH = pl.DeviceIdType.MESH
ROUNDS = 3
SLOTS = 32
LANES = 128
ITEMS = 32
ROWS = 4096
SHARE = 1024
STEP = 256
PIECES = SHARE // STEP
WIDE = 512
PAIRS = SHARE // WIDE
TOTAL = 131072
QUARTER = SLOTS
BLOCK = 4 * QUARTER
BUNDLE = 4 * BLOCK
HALF = 4 * BUNDLE
OFFSET = (0, 3, 1, 2)
USED = 512
BF16 = jnp.bfloat16
F32 = jnp.float32


def kernel(
    index_hbm, count_hbm, x_ref, out_ref,
    index_ref, count_ref, table_vec, table, xv, xfull, relay_buf, cand_0, cand_1, cand_2,
    ch, cl, nrm, xh, xl, sq, low, done, part, red_line, red_plane,
    load_sem, send_sem, recv_sem, cost_sem,
):
    cand = (cand_0, cand_1, cand_2)
    item, dim = lax.axis_index("item"), lax.axis_index("dim")
    z = lax.div(item, 8)
    x = lax.div(item - z * 8, 2)
    core = item - z * 8 - x * 2

    def ring(place):
        return [place] + [jnp.where(place + k > 3, place + k - 4, place + k) for k in range(1, 4)]

    xs, ys, zs = ring(x), ring(dim), ring(z)
    sibling = item + 1 - 2 * core

    def plane(dz, dx):
        return (zs[dz] * 8 + xs[dx] * 2 + core, dim)

    def axis(k, first):
        over_x, over_z = plane(0, k)[0], plane(k, 0)[0]
        lead = 1 - core if first else core
        return (over_z + lead * (over_x - over_z), dim)

    up_a, far_a, down_a = [axis(k, True) for k in range(1, 4)]
    up_b, far_b, down_b = [axis(k, False) for k in range(1, 4)]
    up_y, far_y, down_y = [(item, ys[k]) for k in range(1, 4)]
    _, y_up, y_far, y_down = ys
    line_devices = [(sibling, dim)]
    for k in range(1, 4):
        line_devices += [(item, ys[k]), (sibling, ys[k])]
    plane_devices = [plane(dz, dx) for dz in range(4) for dx in range(4) if dz or dx]

    loads = [
        pltpu.make_async_copy(index_hbm, index_ref, load_sem.at[0]),
        pltpu.make_async_copy(x_ref, xv, load_sem.at[1]),
        pltpu.make_async_copy(count_hbm, count_ref, load_sem.at[2]),
        pltpu.make_async_copy(x_ref.at[pl.ds(dim * SHARE, SHARE)], xfull.at[dim], load_sem.at[3]),
    ]
    for copy in loads:
        copy.start()
    index_load, x_load, count_load, own_rows = loads
    table_load = pltpu.make_async_copy(table_vec, table, load_sem.at[4])

    barrier = pltpu.get_barrier_semaphore()
    for target in line_devices + plane_devices:
        pl.semaphore_signal(barrier, inc=1, device_id=target, device_id_type=MESH)

    pl.semaphore_wait(barrier, REDUCES)

    number = itertools.count()

    def send(src, dst, target, group):
        k = next(number)
        copy = pltpu.make_async_remote_copy(
            src_ref=src, dst_ref=dst, send_sem=send_sem.at[group], recv_sem=recv_sem.at[k],
            device_id=target, device_id_type=MESH,
        )
        copy.start()
        return copy

    def sent(ref, group):
        pltpu.make_async_copy(ref, ref, send_sem.at[group]).wait()

    half = STEP // 2
    y_copies, first, second, passes, swap, relay, near, passed = [{} for _ in range(8)]

    def near_send(t):
        lands = xfull.at[dim, pl.ds(t * STEP, STEP)]
        near[t] = (
            send(x_ref.at[pl.ds(y_up * SHARE + t * STEP, STEP)], lands, up_y, NEAR),
            send(x_ref.at[pl.ds(y_down * SHARE + t * STEP, STEP)], lands, down_y, NEAR),
        )

    def far_send(t):
        far = y_far * SHARE + t * STEP
        relay[t] = (
            send(x_ref.at[pl.ds(far, half)], relay_buf.at[0, t], up_y, RELAY),
            send(x_ref.at[pl.ds(far + half, half)], relay_buf.at[1, t], down_y, RELAY),
        )

    def far_pass(t):
        relay[t][0].wait_recv()
        up = send(relay_buf.at[0, t], xfull.at[y_down, pl.ds(t * STEP, half)], up_y, PASSED)
        relay[t][1].wait_recv()
        down = send(relay_buf.at[1, t], xfull.at[y_up, pl.ds(t * STEP + half, half)], down_y, PASSED)
        passed[t] = (up, down)

    def tiles(r, start, count):
        return cand[r].at[pl.ds(pl.multiple_of(core * HALF + start, QUARTER), count)]

    def pick_send(r):
        ref = tiles(r, dim * QUARTER, QUARTER)
        y_copies[r] = [send(ref, ref, target, PICK + r) for target in (up_y, down_y, far_y)]

    def first_send(r):
        for copy in y_copies[r]:
            copy.wait_recv()
        block = tiles(r, 0, BLOCK)
        first[r] = [
            send(block, tiles(r, k * BLOCK, BLOCK), target, FIRST + r)
            for k, target in ((3, far_a), (1, up_a), (2, down_a))
        ]

    def second_send(r):
        for copy in first[r]:
            copy.wait_recv()
        bundle = tiles(r, 0, BUNDLE)
        second[r] = (
            send(bundle, tiles(r, BUNDLE, BUNDLE), up_b, SECOND + r),
            send(bundle, tiles(r, 2 * BUNDLE, BUNDLE), down_b, SECOND + r),
        )
        swap[r] = [send(bundle, bundle, (sibling, dim), SWAP + r)]

    def second_pass(r):
        part = 2 * BLOCK
        second[r][0].wait_recv()
        up = send(tiles(r, BUNDLE, part), tiles(r, 3 * BUNDLE, part), up_b, SECOND + r)
        second[r][1].wait_recv()
        down = send(tiles(r, 2 * BUNDLE + part, part), tiles(r, 3 * BUNDLE + part, part), down_b, SECOND + r)
        passes[r] = (up, down)
        ready = tiles(r, BUNDLE, 2 * BUNDLE)
        swap[r].append(send(ready, ready, (sibling, dim), SWAP + r))

    def second_end(r):
        for copy in passes[r]:
            copy.wait_recv()
        ready = tiles(r, 3 * BUNDLE, BUNDLE)
        swap[r].append(send(ready, ready, (sibling, dim), SWAP + r))

    def tabulate():
        count_load.wait()
        place = lax.broadcasted_iota(jnp.int32, (8, LANES), 0) * LANES
        place = place + lax.broadcasted_iota(jnp.int32, (8, LANES), 1)
        for r in range(ROUNDS):
            end, row = 0, place
            for k in range(ITEMS):
                core_, b_, a_ = k // 16, (k // 4) % 4, k % 4
                x_, z_ = xs[OFFSET[b_ if core_ else a_]], zs[OFFSET[a_ if core_ else b_]]
                count = count_ref[r, z_ * 8 + x_ * 2 + core_]
                end = end + count
                row = jnp.where(place < end, row, row + (BLOCK - count))
            table_vec[r] = jnp.minimum(row, (ITEMS - 1) * BLOCK + SLOTS - 1)
        table_load.start()

    def convert(r):
        for copy in swap[r]:
            copy.wait_recv()
        slot = lax.broadcasted_iota(jnp.int32, (8, LANES), 0)

        def gather(line, g, q):
            value = None
            for k in range(8):
                row = cand[r][pl.ds(table[r, line, g * 8 + k] + q * QUARTER, 1), :]
                row = jnp.broadcast_to(row, (8, LANES))
                value = row if k == 0 else jnp.where(slot == k, row, value)
            return value

        def one(line, carry):
            for g in range(0, LANES // 8, 2):
                at = pl.ds(pl.multiple_of(line * LANES + g * 8, 16), 16)
                total = jnp.zeros((16, LANES), F32)
                for q in range(4):
                    value = jnp.concatenate([gather(line, g, q), gather(line, g + 1, q)], axis=0)
                    total += value * value
                    high = value.astype(BF16)
                    ch[r, at, q * LANES:(q + 1) * LANES] = high
                    cl[r, at, q * LANES:(q + 1) * LANES] = (value - high.astype(F32)).astype(BF16)
                nrm[r, at, :] = jnp.broadcast_to(jnp.sum(total, axis=1, keepdims=True), (16, LANES))
            return carry

        lax.fori_loop(0, USED // LANES, one, 0)

    def prepare(t):
        for copy in near[t] + passed[t]:
            copy.wait_recv()
        at = slice(t % 2 * STEP, (t % 2 + 1) * STEP)
        total = jnp.zeros((LANES, STEP), F32)
        for q in range(4):
            value = xfull[q, t * STEP:(t + 1) * STEP, :].T
            total += value * value
            value = -2.0 * value
            high = value.astype(BF16)
            xh[t // 2, q * LANES:(q + 1) * LANES, at] = high
            xl[t // 2, q * LANES:(q + 1) * LANES, at] = (value - high.astype(F32)).astype(BF16)
        sq[t // 2, :, at] = jnp.sum(total.reshape(LANES // 8, 8, STEP), axis=0)

    def nearest(t, r):
        high, rows = ch[r], xh[t]
        value = jnp.dot(
            jnp.concatenate([high, cl[r], high], axis=1),
            jnp.concatenate([rows, rows, xl[t]], axis=0),
            preferred_element_type=F32,
        )
        value = value + jnp.concatenate([nrm[r]] * (WIDE // LANES), axis=1)
        low[t, r] = jnp.min(value.reshape(USED // 8, 8, WIDE), axis=0)

    def finish(t):
        norm = jnp.sum(sq[t], axis=0, keepdims=True)
        best = [jnp.min(low[t, r], axis=0, keepdims=True) for r in range(ROUNDS)]
        for r in range(1, ROUNDS):
            best[r] = jnp.minimum(best[r], best[r - 1])
        done[:, t * WIDE:(t + 1) * WIDE] = jnp.concatenate(
            [jnp.maximum(value + norm, 0.0) for value in best], axis=0
        )

    def many(count, body):
        def one(k, carry):
            body(k)
            return carry

        lax.fori_loop(0, count, one, 0)

    far_send(0)
    index_load.wait()
    x_load.wait()
    for r in range(ROUNDS):
        def pick(g, carry, r=r):
            rows = [xv[pl.ds(index_ref[r, g * 8 + k], 1), :] for k in range(8)]
            at = pl.multiple_of(core * HALF + dim * QUARTER + g * 8, 8)
            cand[r][pl.ds(at, 8), :] = jnp.concatenate(rows, axis=0)
            return carry

        lax.fori_loop(0, SLOTS // 8, pick, 0, unroll=True)
    pick_send(0)
    pick_send(1)
    far_send(1)
    tabulate()
    first_send(0)
    first_send(1)
    near_send(0)
    far_send(2)
    second_send(0)
    far_pass(0)
    pick_send(2)
    second_send(1)
    far_pass(1)
    second_pass(0)
    near_send(1)
    first_send(2)
    own_rows.wait()
    prepare(0)
    second_pass(1)
    near_send(2)
    far_send(3)
    second_end(0)
    far_pass(2)
    second_send(2)
    prepare(1)
    second_end(1)
    near_send(3)
    table_load.wait()
    convert(0)
    nearest(0, 0)
    far_pass(3)
    second_pass(2)
    convert(1)
    nearest(0, 1)
    prepare(2)
    second_end(2)
    prepare(3)
    many(2, lambda r: nearest(1, r))
    for r in range(ROUNDS):
        sent(cand[r].at[pl.ds(0, 3 * QUARTER)], PICK + r)
        sent(cand[r].at[pl.ds(0, 3 * BLOCK)], FIRST + r)
        sent(cand[r].at[pl.ds(0, 3 * BUNDLE)], SECOND + r)
        sent(cand[r].at[pl.ds(0, HALF)], SWAP + r)
    sent(xfull.at[pl.ds(0, 1)], RELAY)
    sent(xfull.at[pl.ds(0, 2)], NEAR)
    sent(xfull.at[pl.ds(0, 1)], PASSED)
    convert(2)
    many(PAIRS, lambda t: nearest(t, 2))
    for t in range(PAIRS):
        finish(t)

    sums = sum([done[:, k * LANES:(k + 1) * LANES] for k in range(SHARE // LANES)])
    line = jnp.concatenate([sums, jnp.zeros((8 - ROUNDS, LANES), F32)], axis=0)
    for stage, (targets, landed) in enumerate(((line_devices, red_line), (plane_devices, red_plane))):
        part[stage] = line
        for k, target in enumerate(targets):
            pltpu.make_async_remote_copy(
                src_ref=part.at[stage], dst_ref=landed.at[k], send_sem=send_sem.at[COST + stage],
                recv_sem=cost_sem.at[stage], device_id=target, device_id_type=MESH,
            ).start()
        pltpu.make_async_copy(landed, landed, cost_sem.at[stage]).wait()
        line = line + jnp.sum(landed[...], axis=0)
    cost = jnp.sum(line, axis=1, keepdims=True)[:ROUNDS]
    out_ref[...] = jnp.minimum(CAP, TOTAL * done[...] / cost)
    sent(red_line, COST)
    sent(red_plane, COST + 1)


COPIES = ROUNDS * 13 + PIECES * 6
REDUCES = 22
PICK, FIRST, SECOND, SWAP, RELAY, NEAR, PASSED, COST = 0, 3, 6, 9, 12, 13, 14, 15
ANY = pl.BlockSpec(memory_space=pl.ANY)


def local(embeddings, cand_index, cand_count):
    return pl.pallas_call(
        kernel,
        out_shape=jax.ShapeDtypeStruct((ROUNDS, SHARE), F32),
        in_specs=[ANY, ANY, ANY],
        out_specs=pl.BlockSpec(memory_space=pltpu.VMEM),
        scratch_shapes=[
            pltpu.SMEM((ROUNDS, SLOTS), jnp.int32),
            pltpu.SMEM((ROUNDS, ITEMS), jnp.int32),
            pltpu.VMEM((ROUNDS, 8, LANES), jnp.int32),
            pltpu.SMEM((ROUNDS, 8, LANES), jnp.int32),
            pltpu.VMEM((ROWS, LANES), F32),
            pltpu.VMEM((4, SHARE, LANES), F32),
            pltpu.VMEM((2, PIECES, STEP // 2, LANES), F32),
            *[pltpu.VMEM((ITEMS * BLOCK, LANES), F32)] * ROUNDS,
            pltpu.VMEM((ROUNDS, USED, 512), BF16),
            pltpu.VMEM((ROUNDS, USED, 512), BF16),
            pltpu.VMEM((ROUNDS, USED, LANES), F32),
            pltpu.VMEM((PAIRS, 512, WIDE), BF16),
            pltpu.VMEM((PAIRS, 512, WIDE), BF16),
            pltpu.VMEM((PAIRS, 8, WIDE), F32),
            pltpu.VMEM((PAIRS, ROUNDS, 8, WIDE), F32),
            pltpu.VMEM((ROUNDS, SHARE), F32),
            pltpu.VMEM((2, 8, LANES), F32),
            pltpu.VMEM((7, 8, LANES), F32),
            pltpu.VMEM((15, 8, LANES), F32),
            pltpu.SemaphoreType.DMA((5,)),
            pltpu.SemaphoreType.DMA((COST + 2,)),
            pltpu.SemaphoreType.DMA((COPIES,)),
            pltpu.SemaphoreType.DMA((2,)),
        ],
        compiler_params=pltpu.CompilerParams(
            collective_id=0, has_side_effects=True, vmem_limit_bytes=56 * 1024 * 1024
        ),
    )(cand_index, cand_count, embeddings)


def solution(mesh):
    in_specs = (P("item", "dim"), P(None, "item"), P())
    out_specs = P(None, ("item", "dim"))
    return jax.shard_map(local, mesh=mesh, in_specs=in_specs, out_specs=out_specs, check_vma=False)
```

```python
import itertools

import jax
import jax.numpy as jnp
from jax import lax
from jax.experimental import pallas as pl
from jax.experimental.pallas import tpu as pltpu
from jax.sharding import PartitionSpec as P

CAP = 4.0
MESH = pl.DeviceIdType.MESH
ROUNDS = 3
SLOTS = 32
LANES = 128
ITEMS = 32
ROWS = 4096
SHARE = 1024
STEP = 256
PIECES = SHARE // STEP
WIDE = 512
PAIRS = SHARE // WIDE
TOTAL = 131072
TILE = 8
QUARTER = SLOTS // TILE
BLOCK = 4 * QUARTER
BUNDLE = 4 * BLOCK
HALF = 4 * BUNDLE
OFFSET = (0, 3, 1, 2)
TILES = 96
USED = TILES * TILE
GROUP = 4
GROUPS = 6
BF16 = jnp.bfloat16
F32 = jnp.float32


def kernel(
    index_hbm, count_hbm, x_ref, out_ref,
    index_ref, count_ref, table_vec, table, xv, xfull, relay_buf, cand_0, cand_1, cand_2,
    ch, cl, nrm, xh, xl, sq, low, done, part, red_line, red_plane,
    load_sem, send_sem, recv_sem, cost_sem,
):
    cand = (cand_0, cand_1, cand_2)
    item, dim = lax.axis_index("item"), lax.axis_index("dim")
    z = lax.div(item, 8)
    x = lax.div(item - z * 8, 2)
    core = item - z * 8 - x * 2

    def ring(place):
        return [place] + [jnp.where(place + k > 3, place + k - 4, place + k) for k in range(1, 4)]

    xs, ys, zs = ring(x), ring(dim), ring(z)
    sibling = item + 1 - 2 * core

    def plane(dz, dx):
        return (zs[dz] * 8 + xs[dx] * 2 + core, dim)

    def axis(k, first):
        over_x, over_z = plane(0, k)[0], plane(k, 0)[0]
        lead = 1 - core if first else core
        return (over_z + lead * (over_x - over_z), dim)

    up_a, far_a, down_a = [axis(k, True) for k in range(1, 4)]
    up_b, far_b, down_b = [axis(k, False) for k in range(1, 4)]
    up_y, far_y, down_y = [(item, ys[k]) for k in range(1, 4)]
    _, y_up, y_far, y_down = ys
    line_devices = [(sibling, dim)]
    for k in range(1, 4):
        line_devices += [(item, ys[k]), (sibling, ys[k])]
    plane_devices = [plane(dz, dx) for dz in range(4) for dx in range(4) if dz or dx]

    loads = [
        pltpu.make_async_copy(index_hbm, index_ref, load_sem.at[0]),
        pltpu.make_async_copy(x_ref, xv, load_sem.at[1]),
        pltpu.make_async_copy(count_hbm, count_ref, load_sem.at[2]),
        pltpu.make_async_copy(x_ref.at[pl.ds(dim * SHARE, SHARE)], xfull.at[dim], load_sem.at[3]),
    ]
    for copy in loads:
        copy.start()
    index_load, x_load, count_load, own_rows = loads
    table_load = pltpu.make_async_copy(table_vec, table, load_sem.at[4])

    barrier = pltpu.get_barrier_semaphore()
    for target in line_devices + plane_devices:
        pl.semaphore_signal(barrier, inc=1, device_id=target, device_id_type=MESH)

    index_load.wait()
    count_load.wait()
    x_load.wait()
    for r in range(ROUNDS):
        def pick(g, carry, r=r):
            slots = [g * TILE + k for k in range(TILE)]
            slots = [jnp.where(slot < count_ref[r, item], slot, 0) for slot in slots]
            rows = [xv[pl.ds(index_ref[r, slot], 1), :] for slot in slots]
            cand[r][core * HALF + dim * QUARTER + g] = jnp.concatenate(rows, axis=0)
            return carry

        lax.fori_loop(0, QUARTER, pick, 0, unroll=True)
    pl.semaphore_wait(barrier, REDUCES)

    number = itertools.count()

    def send(src, dst, target, group):
        k = next(number)
        copy = pltpu.make_async_remote_copy(
            src_ref=src, dst_ref=dst, send_sem=send_sem.at[group], recv_sem=recv_sem.at[k],
            device_id=target, device_id_type=MESH,
        )
        copy.start()
        return copy

    def sent(ref, group):
        pltpu.make_async_copy(ref, ref, send_sem.at[group]).wait()

    half = STEP // 2
    y_copies, first, second, passes, swap, relay, near, passed = [{} for _ in range(8)]

    def near_send(t):
        lands = xfull.at[dim, pl.ds(t * STEP, STEP)]
        near[t] = (
            send(xv.at[pl.ds(y_up * SHARE + t * STEP, STEP)], lands, up_y, NEAR),
            send(xv.at[pl.ds(y_down * SHARE + t * STEP, STEP)], lands, down_y, NEAR),
        )

    def far_send(t):
        far = y_far * SHARE + t * STEP
        relay[t] = (
            send(xv.at[pl.ds(far, half)], relay_buf.at[0, t], up_y, RELAY),
            send(xv.at[pl.ds(far + half, half)], relay_buf.at[1, t], down_y, RELAY),
        )

    def far_pass(t):
        relay[t][0].wait_recv()
        up = send(relay_buf.at[0, t], xfull.at[y_down, pl.ds(t * STEP, half)], up_y, PASSED)
        relay[t][1].wait_recv()
        down = send(relay_buf.at[1, t], xfull.at[y_up, pl.ds(t * STEP + half, half)], down_y, PASSED)
        passed[t] = (up, down)

    def tiles(r, start, count):
        return cand[r].at[pl.ds(core * HALF + start, count)]

    def pick_send(r):
        ref = tiles(r, dim * QUARTER, QUARTER)
        y_copies[r] = [send(ref, ref, target, PICK + r) for target in (up_y, down_y, far_y)]

    def first_send(r):
        for copy in y_copies[r]:
            copy.wait_recv()
        block = tiles(r, 0, BLOCK)
        first[r] = [
            send(block, tiles(r, k * BLOCK, BLOCK), target, FIRST + r)
            for k, target in ((3, far_a), (1, up_a), (2, down_a))
        ]

    def second_send(r):
        for copy in first[r]:
            copy.wait_recv()
        bundle = tiles(r, 0, BUNDLE)
        second[r] = (
            send(bundle, tiles(r, BUNDLE, BUNDLE), up_b, SECOND + r),
            send(bundle, tiles(r, 2 * BUNDLE, BUNDLE), down_b, SECOND + r),
        )
        swap[r] = [send(bundle, bundle, (sibling, dim), SWAP + r)]

    def second_pass(r):
        part = 2 * BLOCK
        second[r][0].wait_recv()
        up = send(tiles(r, BUNDLE, part), tiles(r, 3 * BUNDLE, part), up_b, SECOND + r)
        second[r][1].wait_recv()
        down = send(tiles(r, 2 * BUNDLE + part, part), tiles(r, 3 * BUNDLE + part, part), down_b, SECOND + r)
        passes[r] = (up, down)
        ready = tiles(r, BUNDLE, 2 * BUNDLE)
        swap[r].append(send(ready, ready, (sibling, dim), SWAP + r))

    def second_end(r):
        for copy in passes[r]:
            copy.wait_recv()
        ready = tiles(r, 3 * BUNDLE, BUNDLE)
        swap[r].append(send(ready, ready, (sibling, dim), SWAP + r))

    def tabulate():
        place = lax.broadcasted_iota(jnp.int32, (8, LANES), 1)
        for r in range(ROUNDS):
            end, tile = 0, place
            for k in range(ITEMS):
                core_, b_, a_ = k // 16, (k // 4) % 4, k % 4
                x_, z_ = xs[OFFSET[b_ if core_ else a_]], zs[OFFSET[a_ if core_ else b_]]
                count = lax.div(count_ref[r, z_ * 8 + x_ * 2 + core_] + (TILE - 1), TILE)
                end = end + count
                tile = jnp.where(place < end, tile, tile + (BLOCK - count))
            table_vec[r] = jnp.where(place < end, tile, 0)
        table_load.start()

    def convert(r):
        for copy in swap[r]:
            copy.wait_recv()

        def one(step, carry):
            for g in range(GROUPS):
                first_tile = (step * GROUPS + g) * GROUP
                at = pl.ds(pl.multiple_of(first_tile * TILE, GROUP * TILE), GROUP * TILE)
                place = [table[r, 0, first_tile + k] for k in range(GROUP)]
                total = jnp.zeros((GROUP * TILE, LANES), F32)
                for q in range(4):
                    value = jnp.concatenate([cand[r][p + q * QUARTER] for p in place], axis=0)
                    total += value * value
                    high = value.astype(BF16)
                    ch[r, at, q * LANES:(q + 1) * LANES] = high
                    cl[r, at, q * LANES:(q + 1) * LANES] = (value - high.astype(F32)).astype(BF16)
                norm = jnp.sum(total, axis=1, keepdims=True)
                nrm[r, at, :] = jnp.broadcast_to(norm, (GROUP * TILE, LANES))
            return carry

        lax.fori_loop(0, TILES // (GROUP * GROUPS), one, 0)

    def prepare(t):
        for copy in near[t] + passed[t]:
            copy.wait_recv()
        at = slice(t % 2 * STEP, (t % 2 + 1) * STEP)
        total = jnp.zeros((LANES, STEP), F32)
        for q in range(4):
            value = xfull[q, t * STEP:(t + 1) * STEP, :].T
            total += value * value
            value = -2.0 * value
            high = value.astype(BF16)
            xh[t // 2, q * LANES:(q + 1) * LANES, at] = high
            xl[t // 2, q * LANES:(q + 1) * LANES, at] = (value - high.astype(F32)).astype(BF16)
        sq[t // 2, :, at] = jnp.sum(total.reshape(LANES // 8, 8, STEP), axis=0)

    def nearest(t, r):
        high, rows = ch[r], xh[t]
        value = jnp.dot(
            jnp.concatenate([high, cl[r], high], axis=1),
            jnp.concatenate([rows, rows, xl[t]], axis=0),
            preferred_element_type=F32,
        )
        value = value + jnp.concatenate([nrm[r]] * (WIDE // LANES), axis=1)
        low[t, r] = jnp.min(value.reshape(TILES, 8, WIDE), axis=0)

    def finish(t):
        norm = jnp.sum(sq[t], axis=0, keepdims=True)
        best = [jnp.min(low[t, r], axis=0, keepdims=True) for r in range(ROUNDS)]
        for r in range(1, ROUNDS):
            best[r] = jnp.minimum(best[r], best[r - 1])
        done[:, t * WIDE:(t + 1) * WIDE] = jnp.concatenate(
            [jnp.maximum(value + norm, 0.0) for value in best], axis=0
        )

    def many(count, body):
        def one(k, carry):
            body(k)
            return carry

        lax.fori_loop(0, count, one, 0)

    pick_send(0)
    pick_send(1)
    far_send(0)
    tabulate()
    first_send(0)
    far_send(1)
    first_send(1)
    near_send(0)
    far_send(2)
    second_send(0)
    far_pass(0)
    pick_send(2)
    second_send(1)
    far_pass(1)
    second_pass(0)
    near_send(1)
    first_send(2)
    own_rows.wait()
    prepare(0)
    second_pass(1)
    near_send(2)
    far_send(3)
    second_end(0)
    far_pass(2)
    second_send(2)
    prepare(1)
    second_end(1)
    near_send(3)
    table_load.wait()
    convert(0)
    nearest(0, 0)
    far_pass(3)
    second_pass(2)
    convert(1)
    nearest(0, 1)
    prepare(2)
    second_end(2)
    prepare(3)
    many(2, lambda r: nearest(1, r))
    for r in range(ROUNDS):
        sent(cand[r].at[pl.ds(0, 3 * QUARTER)], PICK + r)
        sent(cand[r].at[pl.ds(0, 3 * BLOCK)], FIRST + r)
        sent(cand[r].at[pl.ds(0, 3 * BUNDLE)], SECOND + r)
        sent(cand[r].at[pl.ds(0, HALF)], SWAP + r)
    sent(xfull.at[pl.ds(0, 1)], RELAY)
    sent(xfull.at[pl.ds(0, 2)], NEAR)
    sent(xfull.at[pl.ds(0, 1)], PASSED)
    convert(2)
    many(PAIRS, lambda t: nearest(t, 2))
    for t in range(PAIRS):
        finish(t)

    sums = sum([done[:, k * LANES:(k + 1) * LANES] for k in range(SHARE // LANES)])
    line = jnp.concatenate([sums, jnp.zeros((8 - ROUNDS, LANES), F32)], axis=0)
    for stage, (targets, landed) in enumerate(((line_devices, red_line), (plane_devices, red_plane))):
        part[stage] = line
        for k, target in enumerate(targets):
            pltpu.make_async_remote_copy(
                src_ref=part.at[stage], dst_ref=landed.at[k], send_sem=send_sem.at[COST + stage],
                recv_sem=cost_sem.at[stage], device_id=target, device_id_type=MESH,
            ).start()
        pltpu.make_async_copy(landed, landed, cost_sem.at[stage]).wait()
        line = line + jnp.sum(landed[...], axis=0)
    cost = jnp.sum(line, axis=1, keepdims=True)[:ROUNDS]
    out_ref[...] = jnp.minimum(CAP, TOTAL * done[...] / cost)
    sent(red_line, COST)
    sent(red_plane, COST + 1)


COPIES = ROUNDS * 13 + PIECES * 6
REDUCES = 22
PICK, FIRST, SECOND, SWAP, RELAY, NEAR, PASSED, COST = 0, 3, 6, 9, 12, 13, 14, 15
ANY = pl.BlockSpec(memory_space=pl.ANY)


def local(embeddings, cand_index, cand_count):
    return pl.pallas_call(
        kernel,
        out_shape=jax.ShapeDtypeStruct((ROUNDS, SHARE), F32),
        in_specs=[ANY, ANY, ANY],
        out_specs=pl.BlockSpec(memory_space=pltpu.VMEM),
        scratch_shapes=[
            pltpu.SMEM((ROUNDS, SLOTS), jnp.int32),
            pltpu.SMEM((ROUNDS, ITEMS), jnp.int32),
            pltpu.VMEM((ROUNDS, 8, LANES), jnp.int32),
            pltpu.SMEM((ROUNDS, 8, LANES), jnp.int32),
            pltpu.VMEM((ROWS, LANES), F32),
            pltpu.VMEM((4, SHARE, LANES), F32),
            pltpu.VMEM((2, PIECES, STEP // 2, LANES), F32),
            *[pltpu.VMEM((ITEMS * BLOCK, TILE, LANES), F32)] * ROUNDS,
            pltpu.VMEM((ROUNDS, USED, 512), BF16),
            pltpu.VMEM((ROUNDS, USED, 512), BF16),
            pltpu.VMEM((ROUNDS, USED, LANES), F32),
            pltpu.VMEM((PAIRS, 512, WIDE), BF16),
            pltpu.VMEM((PAIRS, 512, WIDE), BF16),
            pltpu.VMEM((PAIRS, 8, WIDE), F32),
            pltpu.VMEM((PAIRS, ROUNDS, 8, WIDE), F32),
            pltpu.VMEM((ROUNDS, SHARE), F32),
            pltpu.VMEM((2, 8, LANES), F32),
            pltpu.VMEM((7, 8, LANES), F32),
            pltpu.VMEM((15, 8, LANES), F32),
            pltpu.SemaphoreType.DMA((5,)),
            pltpu.SemaphoreType.DMA((COST + 2,)),
            pltpu.SemaphoreType.DMA((COPIES,)),
            pltpu.SemaphoreType.DMA((2,)),
        ],
        compiler_params=pltpu.CompilerParams(
            collective_id=0, has_side_effects=True, vmem_limit_bytes=56 * 1024 * 1024
        ),
    )(cand_index, cand_count, embeddings)


def solution(mesh):
    in_specs = (P("item", "dim"), P(None, "item"), P())
    out_specs = P(None, ("item", "dim"))
    return jax.shard_map(local, mesh=mesh, in_specs=in_specs, out_specs=out_specs, check_vma=False)
```

```python
import itertools

import jax
import jax.numpy as jnp
from jax import lax
from jax.experimental import pallas as pl
from jax.experimental.pallas import tpu as pltpu
from jax.sharding import PartitionSpec as P

CAP = 4.0
MESH = pl.DeviceIdType.MESH
ROUNDS = 3
SLOTS = 32
LANES = 128
ITEMS = 32
ROWS = 4096
SHARE = 1024
STEP = 256
PIECES = SHARE // STEP
WIDE = 512
PAIRS = SHARE // WIDE
TOTAL = 131072
TILE = 8
QUARTER = SLOTS // TILE
BLOCK = 4 * QUARTER
BUNDLE = 4 * BLOCK
HALF = 4 * BUNDLE
CORE_SLOTS = 512
BF16 = jnp.bfloat16
F32 = jnp.float32


def kernel(
    index_hbm, count_hbm, x_ref, out_ref,
    index_ref, count_ref, xv, xfull, relay_buf, cand_0, cand_1, cand_2,
    ch, cl, nrm, xh, xl, sq, low, done, part, red_line, red_plane,
    load_sem, send_sem, recv_sem, cost_sem,
):
    cand = (cand_0, cand_1, cand_2)
    item, dim = lax.axis_index("item"), lax.axis_index("dim")
    z = lax.div(item, 8)
    x = lax.div(item - z * 8, 2)
    core = item - z * 8 - x * 2

    def ring(place):
        return [place] + [jnp.where(place + k > 3, place + k - 4, place + k) for k in range(1, 4)]

    xs, ys, zs = ring(x), ring(dim), ring(z)
    sibling = item + 1 - 2 * core

    def plane(dz, dx):
        return (zs[dz] * 8 + xs[dx] * 2 + core, dim)

    def axis(k, first):
        over_x, over_z = plane(0, k)[0], plane(k, 0)[0]
        lead = 1 - core if first else core
        return (over_z + lead * (over_x - over_z), dim)

    up_a, far_a, down_a = [axis(k, True) for k in range(1, 4)]
    up_b, far_b, down_b = [axis(k, False) for k in range(1, 4)]
    up_y, far_y, down_y = [(item, ys[k]) for k in range(1, 4)]
    _, y_up, y_far, y_down = ys
    line_devices = [(sibling, dim)]
    for k in range(1, 4):
        line_devices += [(item, ys[k]), (sibling, ys[k])]
    plane_devices = [plane(dz, dx) for dz in range(4) for dx in range(4) if dz or dx]

    loads = [
        pltpu.make_async_copy(index_hbm, index_ref, load_sem.at[0]),
        pltpu.make_async_copy(x_ref, xv, load_sem.at[1]),
        pltpu.make_async_copy(count_hbm, count_ref, load_sem.at[2]),
        pltpu.make_async_copy(x_ref.at[pl.ds(dim * SHARE, SHARE)], xfull.at[dim], load_sem.at[3]),
    ]
    for copy in loads:
        copy.start()
    index_load, x_load, count_load, own_rows = loads

    barrier = pltpu.get_barrier_semaphore()
    for target in line_devices + plane_devices:
        pl.semaphore_signal(barrier, inc=1, device_id=target, device_id_type=MESH)

    index_load.wait()
    count_load.wait()
    x_load.wait()
    pl.semaphore_wait(barrier, REDUCES)

    number = itertools.count()

    def send(src, dst, target, group):
        k = next(number)
        copy = pltpu.make_async_remote_copy(
            src_ref=src, dst_ref=dst, send_sem=send_sem.at[group], recv_sem=recv_sem.at[k],
            device_id=target, device_id_type=MESH,
        )
        copy.start()
        return copy

    def sent(ref, group):
        pltpu.make_async_copy(ref, ref, send_sem.at[group]).wait()

    half = STEP // 2
    y_copies, first, second, passes, swap, relay, near, passed = [{} for _ in range(8)]

    def near_send(t):
        lands = xfull.at[dim, pl.ds(t * STEP, STEP)]
        near[t] = (
            send(xv.at[pl.ds(y_up * SHARE + t * STEP, STEP)], lands, up_y, NEAR),
            send(xv.at[pl.ds(y_down * SHARE + t * STEP, STEP)], lands, down_y, NEAR),
        )

    def far_send(t):
        far = y_far * SHARE + t * STEP
        relay[t] = (
            send(xv.at[pl.ds(far, half)], relay_buf.at[0, t], up_y, RELAY),
            send(xv.at[pl.ds(far + half, half)], relay_buf.at[1, t], down_y, RELAY),
        )

    def far_pass(t):
        relay[t][0].wait_recv()
        up = send(relay_buf.at[0, t], xfull.at[y_down, pl.ds(t * STEP, half)], up_y, PASSED)
        relay[t][1].wait_recv()
        down = send(relay_buf.at[1, t], xfull.at[y_up, pl.ds(t * STEP + half, half)], down_y, PASSED)
        passed[t] = (up, down)

    def tiles(r, start, count):
        return cand[r].at[pl.ds(core * HALF + start, count)]

    def pick_send(r):
        def pick(g, carry):
            slots = [g * TILE + k for k in range(TILE)]
            slots = [jnp.where(slot < count_ref[r, item], slot, 0) for slot in slots]
            rows = [xv[pl.ds(index_ref[r, slot], 1), :] for slot in slots]
            cand[r][core * HALF + dim * QUARTER + g] = jnp.concatenate(rows, axis=0)
            return carry

        lax.fori_loop(0, QUARTER, pick, 0, unroll=True)

        ref = tiles(r, dim * QUARTER, QUARTER)
        y_copies[r] = [send(ref, ref, target, PICK + r) for target in (up_y, down_y, far_y)]

    def first_send(r):
        for copy in y_copies[r]:
            copy.wait_recv()
        block = tiles(r, 0, BLOCK)
        first[r] = [
            send(block, tiles(r, k * BLOCK, BLOCK), target, FIRST + r)
            for k, target in ((3, far_a), (1, up_a), (2, down_a))
        ]

    def second_send(r):
        for copy in first[r]:
            copy.wait_recv()
        bundle = tiles(r, 0, BUNDLE)
        second[r] = (
            send(bundle, tiles(r, BUNDLE, BUNDLE), up_b, SECOND + r),
            send(bundle, tiles(r, 2 * BUNDLE, BUNDLE), down_b, SECOND + r),
        )
        swap[r] = [send(bundle, bundle, (sibling, dim), SWAP + r)]

    def second_pass(r):
        part = 2 * BLOCK
        second[r][0].wait_recv()
        up = send(tiles(r, BUNDLE, part), tiles(r, 3 * BUNDLE, part), up_b, SECOND + r)
        second[r][1].wait_recv()
        down = send(tiles(r, 2 * BUNDLE + part, part), tiles(r, 3 * BUNDLE + part, part), down_b, SECOND + r)
        passes[r] = (up, down)
        ready = tiles(r, BUNDLE, 2 * BUNDLE)
        swap[r].append(send(ready, ready, (sibling, dim), SWAP + r))

    def second_end(r):
        for copy in passes[r]:
            copy.wait_recv()
        ready = tiles(r, 3 * BUNDLE, BUNDLE)
        swap[r].append(send(ready, ready, (sibling, dim), SWAP + r))

    def convert(r, side, bundle, count=1):
        start = (core * HALF if side == 0 else (1 - core) * HALF) + bundle * BUNDLE

        def one(step, carry):
            for k in range(4):
                at = pl.ds(pl.multiple_of(step * 4 * SLOTS + k * SLOTS, SLOTS), SLOTS)
                total = jnp.zeros((SLOTS, LANES), F32)
                for q in range(4):
                    place = start + (step - bundle) * BUNDLE + k * BLOCK + q * QUARTER
                    value = cand[r][pl.ds(place, QUARTER)].reshape(SLOTS, LANES)
                    total += value * value
                    high = value.astype(BF16)
                    ch[r, side, at, q * LANES:(q + 1) * LANES] = high
                    cl[r, side, at, q * LANES:(q + 1) * LANES] = (value - high.astype(F32)).astype(BF16)
                norm = jnp.sum(total, axis=1, keepdims=True)
                nrm[r, side, at, :] = jnp.broadcast_to(norm, (SLOTS, LANES))
            return carry

        lax.fori_loop(bundle, bundle + count, one, 0)

    def prepare(t):
        for copy in near[t] + passed[t]:
            copy.wait_recv()
        at = slice(t % 2 * STEP, (t % 2 + 1) * STEP)
        total = jnp.zeros((LANES, STEP), F32)
        for q in range(4):
            value = xfull[q, t * STEP:(t + 1) * STEP, :].T
            total += value * value
            value = -2.0 * value
            high = value.astype(BF16)
            xh[t // 2, q * LANES:(q + 1) * LANES, at] = high
            xl[t // 2, q * LANES:(q + 1) * LANES, at] = (value - high.astype(F32)).astype(BF16)
        sq[t // 2, :, at] = jnp.sum(total.reshape(LANES // 8, 8, STEP), axis=0)

    def nearest(t, r, side):
        high, rows = ch[r, side], xh[t]
        value = jnp.dot(
            jnp.concatenate([high, cl[r, side], high], axis=1),
            jnp.concatenate([rows, rows, xl[t]], axis=0),
            preferred_element_type=F32,
        )
        value = value + jnp.concatenate([nrm[r, side]] * (WIDE // LANES), axis=1)
        low[t, r, side] = jnp.min(value.reshape(CORE_SLOTS // 8, 8, WIDE), axis=0)

    def finish(t):
        norm = jnp.sum(sq[t], axis=0, keepdims=True)
        best = [
            jnp.min(jnp.minimum(low[t, r, 0], low[t, r, 1]), axis=0, keepdims=True) for r in range(ROUNDS)
        ]
        for r in range(1, ROUNDS):
            best[r] = jnp.minimum(best[r], best[r - 1])
        done[:, t * WIDE:(t + 1) * WIDE] = jnp.concatenate(
            [jnp.maximum(value + norm, 0.0) for value in best], axis=0
        )

    def many(count, body):
        def one(k, carry):
            body(k)
            return carry

        lax.fori_loop(0, count, one, 0)

    def convert_swapped(r):
        for copy in swap[r]:
            copy.wait_recv()
        convert(r, 1, 0, 4)

    pick_send(0)
    pick_send(1)
    far_send(0)
    pick_send(2)
    first_send(0)
    far_send(1)
    first_send(1)
    near_send(0)
    first_send(2)
    second_send(0)
    far_pass(0)
    convert(0, 0, 0)
    second_send(1)
    far_send(2)
    convert(1, 0, 0)
    near_send(1)
    far_send(3)
    far_pass(1)
    own_rows.wait()
    prepare(0)
    second_pass(0)
    convert(0, 0, 1, 2)
    second_send(2)
    second_pass(1)
    convert(1, 0, 1, 2)
    near_send(2)
    far_pass(2)
    second_end(0)
    far_pass(3)
    convert(0, 0, 3)
    convert(2, 0, 0)
    near_send(3)
    prepare(1)
    nearest(0, 0, 0)
    second_pass(2)
    convert(2, 0, 1, 2)
    second_end(1)
    convert_swapped(0)
    convert(1, 0, 3)
    nearest(0, 0, 1)
    second_end(2)
    nearest(0, 1, 0)
    convert(2, 0, 3)
    convert_swapped(1)
    nearest(0, 2, 0)
    nearest(0, 1, 1)
    prepare(2)
    convert_swapped(2)
    nearest(0, 2, 1)
    finish(0)
    for r in range(ROUNDS):
        sent(cand[r].at[pl.ds(0, 3 * QUARTER)], PICK + r)
        sent(cand[r].at[pl.ds(0, 3 * BLOCK)], FIRST + r)
        sent(cand[r].at[pl.ds(0, 3 * BUNDLE)], SECOND + r)
        sent(cand[r].at[pl.ds(0, HALF)], SWAP + r)
    prepare(3)
    sent(xfull.at[pl.ds(0, 1)], RELAY)
    sent(xfull.at[pl.ds(0, 2)], NEAR)
    sent(xfull.at[pl.ds(0, 1)], PASSED)
    many(2 * ROUNDS, lambda k: nearest(1, k // 2, k % 2))
    finish(1)

    sums = sum([done[:, k * LANES:(k + 1) * LANES] for k in range(SHARE // LANES)])
    line = jnp.concatenate([sums, jnp.zeros((8 - ROUNDS, LANES), F32)], axis=0)
    for stage, (targets, landed) in enumerate(((line_devices, red_line), (plane_devices, red_plane))):
        part[stage] = line
        for k, target in enumerate(targets):
            pltpu.make_async_remote_copy(
                src_ref=part.at[stage], dst_ref=landed.at[k], send_sem=send_sem.at[COST + stage],
                recv_sem=cost_sem.at[stage], device_id=target, device_id_type=MESH,
            ).start()
        pltpu.make_async_copy(landed, landed, cost_sem.at[stage]).wait()
        line = line + jnp.sum(landed[...], axis=0)
    cost = jnp.sum(line, axis=1, keepdims=True)[:ROUNDS]
    out_ref[...] = jnp.minimum(CAP, TOTAL * done[...] / cost)
    sent(red_line, COST)
    sent(red_plane, COST + 1)


COPIES = ROUNDS * 13 + PIECES * 6
REDUCES = 22
PICK, FIRST, SECOND, SWAP, RELAY, NEAR, PASSED, COST = 0, 3, 6, 9, 12, 13, 14, 15
ANY = pl.BlockSpec(memory_space=pl.ANY)


def local(embeddings, cand_index, cand_count):
    return pl.pallas_call(
        kernel,
        out_shape=jax.ShapeDtypeStruct((ROUNDS, SHARE), F32),
        in_specs=[ANY, ANY, ANY],
        out_specs=pl.BlockSpec(memory_space=pltpu.VMEM),
        scratch_shapes=[
            pltpu.SMEM((ROUNDS, SLOTS), jnp.int32),
            pltpu.SMEM((ROUNDS, ITEMS), jnp.int32),
            pltpu.VMEM((ROWS, LANES), F32),
            pltpu.VMEM((4, SHARE, LANES), F32),
            pltpu.VMEM((2, PIECES, STEP // 2, LANES), F32),
            *[pltpu.VMEM((ITEMS * BLOCK, TILE, LANES), F32)] * ROUNDS,
            pltpu.VMEM((ROUNDS, 2, CORE_SLOTS, 512), BF16),
            pltpu.VMEM((ROUNDS, 2, CORE_SLOTS, 512), BF16),
            pltpu.VMEM((ROUNDS, 2, CORE_SLOTS, LANES), F32),
            pltpu.VMEM((PAIRS, 512, WIDE), BF16),
            pltpu.VMEM((PAIRS, 512, WIDE), BF16),
            pltpu.VMEM((PAIRS, 8, WIDE), F32),
            pltpu.VMEM((PAIRS, ROUNDS, 2, 8, WIDE), F32),
            pltpu.VMEM((ROUNDS, SHARE), F32),
            pltpu.VMEM((2, 8, LANES), F32),
            pltpu.VMEM((7, 8, LANES), F32),
            pltpu.VMEM((15, 8, LANES), F32),
            pltpu.SemaphoreType.DMA((4,)),
            pltpu.SemaphoreType.DMA((COST + 2,)),
            pltpu.SemaphoreType.DMA((COPIES,)),
            pltpu.SemaphoreType.DMA((2,)),
        ],
        compiler_params=pltpu.CompilerParams(
            collective_id=0, has_side_effects=True, vmem_limit_bytes=56 * 1024 * 1024
        ),
    )(cand_index, cand_count, embeddings)


def solution(mesh):
    in_specs = (P("item", "dim"), P(None, "item"), P())
    out_specs = P(None, ("item", "dim"))
    return jax.shard_map(local, mesh=mesh, in_specs=in_specs, out_specs=out_specs, check_vma=False)
```

```python
import itertools

import jax
import jax.numpy as jnp
from jax import lax
from jax.experimental import pallas as pl
from jax.experimental.pallas import tpu as pltpu
from jax.sharding import PartitionSpec as P

CAP = 4.0
MESH = pl.DeviceIdType.MESH
ROUNDS = 3
SLOTS = 32
LANES = 128
ITEMS = 32
ROWS = 4096
SHARE = 1024
STEP = 256
PIECES = SHARE // STEP
WIDE = 512
PAIRS = SHARE // WIDE
TOTAL = 131072
TILE = 8
QUARTER = SLOTS // TILE
BLOCK = 4 * QUARTER
BUNDLE = 4 * BLOCK
HALF = 4 * BUNDLE
CORE_SLOTS = 512
BF16 = jnp.bfloat16
F32 = jnp.float32


def kernel(
    index_hbm, count_hbm, x_ref, out_ref,
    index_ref, count_ref, xv, xfull, relay_buf, cand_0, cand_1, cand_2,
    ch, cl, nrm, xh, xl, sq, low, done, part, red_line, red_plane,
    load_sem, send_sem, recv_sem, cost_sem,
):
    cand = (cand_0, cand_1, cand_2)
    item, dim = lax.axis_index("item"), lax.axis_index("dim")
    z = lax.div(item, 8)
    x = lax.div(item - z * 8, 2)
    core = item - z * 8 - x * 2

    def ring(place):
        return [place] + [jnp.where(place + k > 3, place + k - 4, place + k) for k in range(1, 4)]

    xs, ys, zs = ring(x), ring(dim), ring(z)
    sibling = item + 1 - 2 * core

    def plane(dz, dx):
        return (zs[dz] * 8 + xs[dx] * 2 + core, dim)

    def axis(k, first):
        over_x, over_z = plane(0, k)[0], plane(k, 0)[0]
        lead = 1 - core if first else core
        return (over_z + lead * (over_x - over_z), dim)

    up_a, far_a, down_a = [axis(k, True) for k in range(1, 4)]
    up_b, far_b, down_b = [axis(k, False) for k in range(1, 4)]
    up_y, far_y, down_y = [(item, ys[k]) for k in range(1, 4)]
    _, y_up, y_far, y_down = ys
    line_devices = [(sibling, dim)]
    for k in range(1, 4):
        line_devices += [(item, ys[k]), (sibling, ys[k])]
    plane_devices = [plane(dz, dx) for dz in range(4) for dx in range(4) if dz or dx]

    loads = [
        pltpu.make_async_copy(index_hbm, index_ref, load_sem.at[0]),
        pltpu.make_async_copy(x_ref, xv, load_sem.at[1]),
        pltpu.make_async_copy(count_hbm, count_ref, load_sem.at[2]),
        pltpu.make_async_copy(x_ref.at[pl.ds(dim * SHARE, SHARE)], xfull.at[dim], load_sem.at[3]),
    ]
    for copy in loads:
        copy.start()
    index_load, x_load, count_load, own_rows = loads

    barrier = pltpu.get_barrier_semaphore()
    for target in line_devices + plane_devices:
        pl.semaphore_signal(barrier, inc=1, device_id=target, device_id_type=MESH)

    index_load.wait()
    count_load.wait()
    x_load.wait()
    pl.semaphore_wait(barrier, REDUCES)

    number = itertools.count()

    def send(src, dst, target, group, like):
        k = next(number)
        pltpu.make_async_remote_copy(
            src_ref=src, dst_ref=dst, send_sem=send_sem.at[group], recv_sem=recv_sem.at[k],
            device_id=target, device_id_type=MESH,
        ).start()
        return lambda: pltpu.make_async_copy(like, like, recv_sem.at[k]).wait()

    def send_tiles(r, start, to, count, target, group):
        like = cand[r].at[pl.ds(0, count)]
        return send(tiles(r, start, count), tiles(r, to, count), target, group + r, like)

    def send_rows(src, dst, target, group, count):
        return send(src, dst, target, group, xfull.at[0, pl.ds(0, count)])

    def sent(ref, group):
        pltpu.make_async_copy(ref, ref, send_sem.at[group]).wait()

    half = STEP // 2
    y_copies, first, second, passes, swap, relay, near, passed = [{} for _ in range(8)]

    def near_send(t):
        lands = xfull.at[dim, pl.ds(t * STEP, STEP)]
        near[t] = (
            send_rows(xv.at[pl.ds(y_up * SHARE + t * STEP, STEP)], lands, up_y, NEAR, STEP),
            send_rows(xv.at[pl.ds(y_down * SHARE + t * STEP, STEP)], lands, down_y, NEAR, STEP),
        )

    def far_send(t):
        far = y_far * SHARE + t * STEP
        relay[t] = (
            send_rows(xv.at[pl.ds(far, half)], relay_buf.at[0, t], up_y, RELAY, half),
            send_rows(xv.at[pl.ds(far + half, half)], relay_buf.at[1, t], down_y, RELAY, half),
        )

    def far_pass(t):
        relay[t][0]()
        up = send_rows(relay_buf.at[0, t], xfull.at[y_down, pl.ds(t * STEP, half)], up_y, PASSED, half)
        relay[t][1]()
        lands = xfull.at[y_up, pl.ds(t * STEP + half, half)]
        down = send_rows(relay_buf.at[1, t], lands, down_y, PASSED, half)
        passed[t] = (up, down)

    def tiles(r, start, count):
        return cand[r].at[pl.ds(core * HALF + start, count)]

    def pick_send(r):
        def pick(g, carry):
            slots = [g * TILE + k for k in range(TILE)]
            slots = [jnp.where(slot < count_ref[r, item], slot, 0) for slot in slots]
            rows = [xv[pl.ds(index_ref[r, slot], 1), :] for slot in slots]
            cand[r][core * HALF + dim * QUARTER + g] = jnp.concatenate(rows, axis=0)
            return carry

        lax.fori_loop(0, QUARTER, pick, 0, unroll=True)

        place = dim * QUARTER
        y_copies[r] = [send_tiles(r, place, place, QUARTER, target, PICK) for target in (up_y, down_y, far_y)]

    def first_send(r):
        for landed in y_copies[r]:
            landed()
        first[r] = [
            send_tiles(r, 0, k * BLOCK, BLOCK, target, FIRST)
            for k, target in ((3, far_a), (1, up_a), (2, down_a))
        ]

    def second_send(r):
        for landed in first[r]:
            landed()
        second[r] = (
            send_tiles(r, 0, BUNDLE, BUNDLE, up_b, SECOND),
            send_tiles(r, 0, 2 * BUNDLE, BUNDLE, down_b, SECOND),
        )
        swap[r] = [send_tiles(r, 0, 0, BUNDLE, (sibling, dim), SWAP)]

    def second_pass(r):
        part = 2 * BLOCK
        second[r][0]()
        up = send_tiles(r, BUNDLE, 3 * BUNDLE, part, up_b, SECOND)
        second[r][1]()
        down = send_tiles(r, 2 * BUNDLE + part, 3 * BUNDLE + part, part, down_b, SECOND)
        passes[r] = (up, down)
        swap[r].append(send_tiles(r, BUNDLE, BUNDLE, 2 * BUNDLE, (sibling, dim), SWAP))

    def second_end(r):
        for landed in passes[r]:
            landed()
        swap[r].append(send_tiles(r, 3 * BUNDLE, 3 * BUNDLE, BUNDLE, (sibling, dim), SWAP))

    def convert(r, side, bundle, count=1):
        start = (core * HALF if side == 0 else (1 - core) * HALF) + bundle * BUNDLE

        def one(step, carry):
            for k in range(4):
                at = pl.ds(pl.multiple_of(step * 4 * SLOTS + k * SLOTS, SLOTS), SLOTS)
                total = jnp.zeros((SLOTS, LANES), F32)
                for q in range(4):
                    place = start + (step - bundle) * BUNDLE + k * BLOCK + q * QUARTER
                    value = cand[r][pl.ds(place, QUARTER)].reshape(SLOTS, LANES)
                    total += value * value
                    high = value.astype(BF16)
                    ch[r, side, at, q * LANES:(q + 1) * LANES] = high
                    cl[r, side, at, q * LANES:(q + 1) * LANES] = (value - high.astype(F32)).astype(BF16)
                norm = jnp.sum(total, axis=1, keepdims=True)
                nrm[r, side, at, :] = jnp.broadcast_to(norm, (SLOTS, LANES))
            return carry

        lax.fori_loop(bundle, bundle + count, one, 0)

    def prepare(t):
        for landed in near[t] + passed[t]:
            landed()
        at = slice(t % 2 * STEP, (t % 2 + 1) * STEP)
        total = jnp.zeros((LANES, STEP), F32)
        for q in range(4):
            value = xfull[q, t * STEP:(t + 1) * STEP, :].T
            total += value * value
            value = -2.0 * value
            high = value.astype(BF16)
            xh[t // 2, q * LANES:(q + 1) * LANES, at] = high
            xl[t // 2, q * LANES:(q + 1) * LANES, at] = (value - high.astype(F32)).astype(BF16)
        sq[t // 2, :, at] = jnp.sum(total.reshape(LANES // 8, 8, STEP), axis=0)

    def nearest(t, r, side):
        high, rows = ch[r, side], xh[t]
        value = jnp.dot(
            jnp.concatenate([high, cl[r, side], high], axis=1),
            jnp.concatenate([rows, rows, xl[t]], axis=0),
            preferred_element_type=F32,
        )
        value = value + jnp.concatenate([nrm[r, side]] * (WIDE // LANES), axis=1)
        low[t, r, side] = jnp.min(value.reshape(CORE_SLOTS // 8, 8, WIDE), axis=0)

    def finish(t):
        norm = jnp.sum(sq[t], axis=0, keepdims=True)
        best = [
            jnp.min(jnp.minimum(low[t, r, 0], low[t, r, 1]), axis=0, keepdims=True) for r in range(ROUNDS)
        ]
        for r in range(1, ROUNDS):
            best[r] = jnp.minimum(best[r], best[r - 1])
        done[:, t * WIDE:(t + 1) * WIDE] = jnp.concatenate(
            [jnp.maximum(value + norm, 0.0) for value in best], axis=0
        )

    def convert_swapped(r):
        for landed in swap[r]:
            landed()
        convert(r, 1, 0, 4)

    pick_send(0)
    pick_send(1)
    far_send(0)
    pick_send(2)
    first_send(0)
    far_send(1)
    first_send(1)
    near_send(0)
    first_send(2)
    second_send(0)
    far_pass(0)
    convert(0, 0, 0)
    second_send(1)
    far_send(2)
    convert(1, 0, 0)
    near_send(1)
    far_send(3)
    far_pass(1)
    own_rows.wait()
    prepare(0)
    second_pass(0)
    convert(0, 0, 1, 2)
    second_send(2)
    second_pass(1)
    convert(1, 0, 1, 2)
    near_send(2)
    far_pass(2)
    second_end(0)
    far_pass(3)
    convert(0, 0, 3)
    convert(2, 0, 0)
    near_send(3)
    prepare(1)

    def product(k, carry):
        @pl.when(k == 1)
        def _():
            second_pass(2)
            convert(2, 0, 1, 2)
            second_end(1)
            convert_swapped(0)
            convert(1, 0, 3)

        @pl.when(k == 2)
        def _():
            second_end(2)

        @pl.when(k == 3)
        def _():
            convert(2, 0, 3)
            convert_swapped(1)

        @pl.when(k == 5)
        def _():
            prepare(2)
            convert_swapped(2)

        @pl.when(k == 6)
        def _():
            finish(0)
            for r in range(ROUNDS):
                sent(cand[r].at[pl.ds(0, 3 * QUARTER)], PICK + r)
                sent(cand[r].at[pl.ds(0, 3 * BLOCK)], FIRST + r)
                sent(cand[r].at[pl.ds(0, 3 * BUNDLE)], SECOND + r)
                sent(cand[r].at[pl.ds(0, HALF)], SWAP + r)
            prepare(3)
            sent(xfull.at[pl.ds(0, 1)], RELAY)
            sent(xfull.at[pl.ds(0, 2)], NEAR)
            sent(xfull.at[pl.ds(0, 1)], PASSED)

        pair = jnp.where(k > 5, 1, 0)
        m = k - 6 * pair
        r = jnp.where(m < 2, 0, jnp.where((m == 2) | (m == 4), 1, 2))
        side = jnp.where((m == 1) | (m > 3), 1, 0)
        nearest(pair, r, side)
        return carry

    lax.fori_loop(0, 2 * 2 * ROUNDS, product, 0)
    finish(1)

    sums = sum([done[:, k * LANES:(k + 1) * LANES] for k in range(SHARE // LANES)])
    line = jnp.concatenate([sums, jnp.zeros((8 - ROUNDS, LANES), F32)], axis=0)
    for stage, (targets, landed) in enumerate(((line_devices, red_line), (plane_devices, red_plane))):
        part[stage] = line
        for k, target in enumerate(targets):
            pltpu.make_async_remote_copy(
                src_ref=part.at[stage], dst_ref=landed.at[k], send_sem=send_sem.at[COST + stage],
                recv_sem=cost_sem.at[stage], device_id=target, device_id_type=MESH,
            ).start()
        pltpu.make_async_copy(landed, landed, cost_sem.at[stage]).wait()
        line = line + jnp.sum(landed[...], axis=0)
    cost = jnp.sum(line, axis=1, keepdims=True)[:ROUNDS]
    out_ref[...] = jnp.minimum(CAP, TOTAL * done[...] / cost)
    sent(red_line, COST)
    sent(red_plane, COST + 1)


COPIES = ROUNDS * 13 + PIECES * 6
REDUCES = 22
PICK, FIRST, SECOND, SWAP, RELAY, NEAR, PASSED, COST = 0, 3, 6, 9, 12, 13, 14, 15
ANY = pl.BlockSpec(memory_space=pl.ANY)


def local(embeddings, cand_index, cand_count):
    return pl.pallas_call(
        kernel,
        out_shape=jax.ShapeDtypeStruct((ROUNDS, SHARE), F32),
        in_specs=[ANY, ANY, ANY],
        out_specs=pl.BlockSpec(memory_space=pltpu.VMEM),
        scratch_shapes=[
            pltpu.SMEM((ROUNDS, SLOTS), jnp.int32),
            pltpu.SMEM((ROUNDS, ITEMS), jnp.int32),
            pltpu.VMEM((ROWS, LANES), F32),
            pltpu.VMEM((4, SHARE, LANES), F32),
            pltpu.VMEM((2, PIECES, STEP // 2, LANES), F32),
            *[pltpu.VMEM((ITEMS * BLOCK, TILE, LANES), F32)] * ROUNDS,
            pltpu.VMEM((ROUNDS, 2, CORE_SLOTS, 512), BF16),
            pltpu.VMEM((ROUNDS, 2, CORE_SLOTS, 512), BF16),
            pltpu.VMEM((ROUNDS, 2, CORE_SLOTS, LANES), F32),
            pltpu.VMEM((PAIRS, 512, WIDE), BF16),
            pltpu.VMEM((PAIRS, 512, WIDE), BF16),
            pltpu.VMEM((PAIRS, 8, WIDE), F32),
            pltpu.VMEM((PAIRS, ROUNDS, 2, 8, WIDE), F32),
            pltpu.VMEM((ROUNDS, SHARE), F32),
            pltpu.VMEM((2, 8, LANES), F32),
            pltpu.VMEM((7, 8, LANES), F32),
            pltpu.VMEM((15, 8, LANES), F32),
            pltpu.SemaphoreType.DMA((4,)),
            pltpu.SemaphoreType.DMA((COST + 2,)),
            pltpu.SemaphoreType.DMA((COPIES,)),
            pltpu.SemaphoreType.DMA((2,)),
        ],
        compiler_params=pltpu.CompilerParams(
            collective_id=0, has_side_effects=True, vmem_limit_bytes=56 * 1024 * 1024
        ),
    )(cand_index, cand_count, embeddings)


def solution(mesh):
    in_specs = (P("item", "dim"), P(None, "item"), P())
    out_specs = P(None, ("item", "dim"))
    return jax.shard_map(local, mesh=mesh, in_specs=in_specs, out_specs=out_specs, check_vma=False)
```

```python
import itertools

import jax
import jax.numpy as jnp
from jax import lax
from jax.experimental import pallas as pl
from jax.experimental.pallas import tpu as pltpu
from jax.sharding import PartitionSpec as P

CAP = 4.0
MESH = pl.DeviceIdType.MESH
ROUNDS = 3
SLOTS = 32
LANES = 128
ITEMS = 32
ROWS = 4096
SHARE = 1024
STEP = 256
PIECES = SHARE // STEP
WIDE = 512
PAIRS = SHARE // WIDE
TOTAL = 131072
TILE = 8
QUARTER = SLOTS // TILE
BLOCK = 4 * QUARTER
BUNDLE = 4 * BLOCK
HALF = 4 * BUNDLE
CORE_SLOTS = 512
BF16 = jnp.bfloat16
F32 = jnp.float32


def kernel(
    index_hbm, count_hbm, x_ref, out_ref,
    index_ref, count_ref, xv, xfull, relay_buf, cand_0, cand_1, cand_2,
    ch, cl, nrm, xh, xl, sq, low, done, part, red_line, red_plane,
    load_sem, send_sem, recv_sem, cost_sem,
):
    cand = (cand_0, cand_1, cand_2)
    item, dim = lax.axis_index("item"), lax.axis_index("dim")
    z = lax.div(item, 8)
    x = lax.div(item - z * 8, 2)
    core = item - z * 8 - x * 2

    def ring(place):
        return [place] + [jnp.where(place + k > 3, place + k - 4, place + k) for k in range(1, 4)]

    xs, ys, zs = ring(x), ring(dim), ring(z)
    sibling = item + 1 - 2 * core

    def plane(dz, dx):
        return (zs[dz] * 8 + xs[dx] * 2 + core, dim)

    def axis(k, first):
        over_x, over_z = plane(0, k)[0], plane(k, 0)[0]
        lead = 1 - core if first else core
        return (over_z + lead * (over_x - over_z), dim)

    up_a, far_a, down_a = [axis(k, True) for k in range(1, 4)]
    up_b, far_b, down_b = [axis(k, False) for k in range(1, 4)]
    up_y, far_y, down_y = [(item, ys[k]) for k in range(1, 4)]
    _, y_up, y_far, y_down = ys
    line_devices = [(sibling, dim)]
    for k in range(1, 4):
        line_devices += [(item, ys[k]), (sibling, ys[k])]
    plane_devices = [plane(dz, dx) for dz in range(4) for dx in range(4) if dz or dx]

    loads = [
        pltpu.make_async_copy(index_hbm, index_ref, load_sem.at[0]),
        pltpu.make_async_copy(x_ref, xv, load_sem.at[1]),
        pltpu.make_async_copy(count_hbm, count_ref, load_sem.at[2]),
        pltpu.make_async_copy(x_ref.at[pl.ds(dim * SHARE, SHARE)], xfull.at[dim], load_sem.at[3]),
    ]
    for copy in loads:
        copy.start()
    index_load, x_load, count_load, own_rows = loads

    barrier = pltpu.get_barrier_semaphore()
    for target in line_devices + plane_devices:
        pl.semaphore_signal(barrier, inc=1, device_id=target, device_id_type=MESH)

    pl.semaphore_wait(barrier, REDUCES)

    number = itertools.count()

    def send(src, dst, target, group):
        k = next(number)
        copy = pltpu.make_async_remote_copy(
            src_ref=src, dst_ref=dst, send_sem=send_sem.at[group], recv_sem=recv_sem.at[k],
            device_id=target, device_id_type=MESH,
        )
        copy.start()
        return copy

    def sent(ref, group):
        pltpu.make_async_copy(ref, ref, send_sem.at[group]).wait()

    half = STEP // 2
    y_copies, first, second, passes, swap, relay, near, passed = [{} for _ in range(8)]

    def near_send(t):
        lands = xfull.at[dim, pl.ds(t * STEP, STEP)]
        near[t] = (
            send(x_ref.at[pl.ds(y_up * SHARE + t * STEP, STEP)], lands, up_y, NEAR),
            send(x_ref.at[pl.ds(y_down * SHARE + t * STEP, STEP)], lands, down_y, NEAR),
        )

    def far_send(t):
        far = y_far * SHARE + t * STEP
        relay[t] = (
            send(x_ref.at[pl.ds(far, half)], relay_buf.at[0, t], up_y, RELAY),
            send(x_ref.at[pl.ds(far + half, half)], relay_buf.at[1, t], down_y, RELAY),
        )

    def far_pass(t):
        relay[t][0].wait_recv()
        up = send(relay_buf.at[0, t], xfull.at[y_down, pl.ds(t * STEP, half)], up_y, PASSED)
        relay[t][1].wait_recv()
        down = send(relay_buf.at[1, t], xfull.at[y_up, pl.ds(t * STEP + half, half)], down_y, PASSED)
        passed[t] = (up, down)

    def tiles(r, start, count):
        return cand[r].at[pl.ds(core * HALF + start, count)]

    def pick_send(r):
        def pick(g, carry):
            slots = [g * TILE + k for k in range(TILE)]
            slots = [jnp.where(slot < count_ref[r, item], slot, 0) for slot in slots]
            rows = [xv[pl.ds(index_ref[r, slot], 1), :] for slot in slots]
            cand[r][core * HALF + dim * QUARTER + g] = jnp.concatenate(rows, axis=0)
            return carry

        lax.fori_loop(0, QUARTER, pick, 0, unroll=True)

        ref = tiles(r, dim * QUARTER, QUARTER)
        y_copies[r] = [send(ref, ref, target, PICK + r) for target in (up_y, down_y, far_y)]

    def first_send(r):
        for copy in y_copies[r]:
            copy.wait_recv()
        block = tiles(r, 0, BLOCK)
        first[r] = [
            send(block, tiles(r, k * BLOCK, BLOCK), target, FIRST + r)
            for k, target in ((3, far_a), (1, up_a), (2, down_a))
        ]

    def second_send(r):
        for copy in first[r]:
            copy.wait_recv()
        bundle = tiles(r, 0, BUNDLE)
        second[r] = (
            send(bundle, tiles(r, BUNDLE, BUNDLE), up_b, SECOND + r),
            send(bundle, tiles(r, 2 * BUNDLE, BUNDLE), down_b, SECOND + r),
        )
        swap[r] = [send(bundle, bundle, (sibling, dim), SWAP + r)]

    def second_pass(r):
        part = 2 * BLOCK
        second[r][0].wait_recv()
        up = send(tiles(r, BUNDLE, part), tiles(r, 3 * BUNDLE, part), up_b, SECOND + r)
        second[r][1].wait_recv()
        down = send(tiles(r, 2 * BUNDLE + part, part), tiles(r, 3 * BUNDLE + part, part), down_b, SECOND + r)
        passes[r] = (up, down)
        ready = tiles(r, BUNDLE, 2 * BUNDLE)
        swap[r].append(send(ready, ready, (sibling, dim), SWAP + r))

    def second_end(r):
        for copy in passes[r]:
            copy.wait_recv()
        ready = tiles(r, 3 * BUNDLE, BUNDLE)
        swap[r].append(send(ready, ready, (sibling, dim), SWAP + r))

    def convert(r, side, bundle, count=1):
        start = (core * HALF if side == 0 else (1 - core) * HALF) + bundle * BUNDLE

        def one(step, carry):
            for k in range(4):
                at = pl.ds(pl.multiple_of(step * 4 * SLOTS + k * SLOTS, SLOTS), SLOTS)
                total = jnp.zeros((SLOTS, LANES), F32)
                for q in range(4):
                    place = start + (step - bundle) * BUNDLE + k * BLOCK + q * QUARTER
                    value = cand[r][pl.ds(place, QUARTER)].reshape(SLOTS, LANES)
                    total += value * value
                    high = value.astype(BF16)
                    ch[r, side, at, q * LANES:(q + 1) * LANES] = high
                    cl[r, side, at, q * LANES:(q + 1) * LANES] = (value - high.astype(F32)).astype(BF16)
                norm = jnp.sum(total, axis=1, keepdims=True)
                nrm[r, side, at, :] = jnp.broadcast_to(norm, (SLOTS, LANES))
            return carry

        lax.fori_loop(bundle, bundle + count, one, 0)

    def prepare(t):
        for copy in near[t] + passed[t]:
            copy.wait_recv()
        at = slice(t % 2 * STEP, (t % 2 + 1) * STEP)
        total = jnp.zeros((LANES, STEP), F32)
        for q in range(4):
            value = xfull[q, t * STEP:(t + 1) * STEP, :].T
            total += value * value
            value = -2.0 * value
            high = value.astype(BF16)
            xh[t // 2, q * LANES:(q + 1) * LANES, at] = high
            xl[t // 2, q * LANES:(q + 1) * LANES, at] = (value - high.astype(F32)).astype(BF16)
        sq[t // 2, :, at] = jnp.sum(total.reshape(LANES // 8, 8, STEP), axis=0)

    def products(pair, at, r, side):
        high, rows = ch[r, side], xh[pair, :, at]
        value = jnp.dot(
            jnp.concatenate([high, cl[r, side], high], axis=1),
            jnp.concatenate([rows, rows, xl[pair, :, at]], axis=0),
            preferred_element_type=F32,
        )
        width = value.shape[1]
        value = value + jnp.concatenate([nrm[r, side]] * (width // LANES), axis=1)
        low[pair, r, side, :, at] = jnp.min(value.reshape(CORE_SLOTS // 8, 8, width), axis=0)

    def nearest(pair, r, side):
        products(pair, slice(0, WIDE), r, side)

    def nearest_piece(t, r, side):
        products(t // 2, slice(t % 2 * STEP, (t % 2 + 1) * STEP), r, side)

    def finish(t):
        norm = jnp.sum(sq[t], axis=0, keepdims=True)
        best = [
            jnp.min(jnp.minimum(low[t, r, 0], low[t, r, 1]), axis=0, keepdims=True) for r in range(ROUNDS)
        ]
        for r in range(1, ROUNDS):
            best[r] = jnp.minimum(best[r], best[r - 1])
        done[:, t * WIDE:(t + 1) * WIDE] = jnp.concatenate(
            [jnp.maximum(value + norm, 0.0) for value in best], axis=0
        )

    def many(count, body):
        def one(k, carry):
            body(k)
            return carry

        lax.fori_loop(0, count, one, 0)

    def convert_swapped(r):
        for copy in swap[r]:
            copy.wait_recv()
        convert(r, 1, 0, 4)

    far_send(0)
    index_load.wait()
    count_load.wait()
    x_load.wait()
    pick_send(0)
    pick_send(1)
    near_send(0)
    pick_send(2)
    far_send(1)
    first_send(0)
    near_send(1)
    first_send(1)
    far_send(2)
    first_send(2)
    far_pass(0)
    second_send(0)
    near_send(2)
    far_send(3)
    convert(0, 0, 0)
    second_send(1)
    far_pass(1)
    near_send(3)
    convert(1, 0, 0)
    own_rows.wait()
    prepare(0)
    second_pass(0)
    convert(0, 0, 1, 2)
    second_send(2)
    far_pass(2)
    second_pass(1)
    far_pass(3)
    convert(1, 0, 1, 2)
    second_end(0)
    convert(0, 0, 3)
    convert(2, 0, 0)
    prepare(1)
    nearest(0, 0, 0)
    second_pass(2)
    convert(2, 0, 1, 2)
    second_end(1)
    convert_swapped(0)
    convert(1, 0, 3)
    nearest(0, 0, 1)
    second_end(2)
    nearest(0, 1, 0)
    convert(2, 0, 3)
    convert_swapped(1)
    nearest(0, 2, 0)
    nearest(0, 1, 1)
    prepare(2)
    many(4, lambda k: nearest_piece(2, k // 2, k % 2))
    convert_swapped(2)
    nearest(0, 2, 1)
    many(2, lambda k: nearest_piece(2, 2, k))
    finish(0)
    for r in range(ROUNDS):
        sent(cand[r].at[pl.ds(0, 3 * QUARTER)], PICK + r)
        sent(cand[r].at[pl.ds(0, 3 * BLOCK)], FIRST + r)
        sent(cand[r].at[pl.ds(0, 3 * BUNDLE)], SECOND + r)
        sent(cand[r].at[pl.ds(0, HALF)], SWAP + r)
    prepare(3)
    sent(xfull.at[pl.ds(0, 1)], RELAY)
    sent(xfull.at[pl.ds(0, 2)], NEAR)
    sent(xfull.at[pl.ds(0, 1)], PASSED)
    many(2 * ROUNDS, lambda k: nearest_piece(3, k // 2, k % 2))
    finish(1)

    sums = sum([done[:, k * LANES:(k + 1) * LANES] for k in range(SHARE // LANES)])
    line = jnp.concatenate([sums, jnp.zeros((8 - ROUNDS, LANES), F32)], axis=0)
    for stage, (targets, landed) in enumerate(((line_devices, red_line), (plane_devices, red_plane))):
        part[stage] = line
        for k, target in enumerate(targets):
            pltpu.make_async_remote_copy(
                src_ref=part.at[stage], dst_ref=landed.at[k], send_sem=send_sem.at[COST + stage],
                recv_sem=cost_sem.at[stage], device_id=target, device_id_type=MESH,
            ).start()
        pltpu.make_async_copy(landed, landed, cost_sem.at[stage]).wait()
        line = line + jnp.sum(landed[...], axis=0)
    cost = jnp.sum(line, axis=1, keepdims=True)[:ROUNDS]
    out_ref[...] = jnp.minimum(CAP, TOTAL * done[...] / cost)
    sent(red_line, COST)
    sent(red_plane, COST + 1)


COPIES = ROUNDS * 13 + PIECES * 6
REDUCES = 22
PICK, FIRST, SECOND, SWAP, RELAY, NEAR, PASSED, COST = 0, 3, 6, 9, 12, 13, 14, 15
ANY = pl.BlockSpec(memory_space=pl.ANY)


def local(embeddings, cand_index, cand_count):
    return pl.pallas_call(
        kernel,
        out_shape=jax.ShapeDtypeStruct((ROUNDS, SHARE), F32),
        in_specs=[ANY, ANY, ANY],
        out_specs=pl.BlockSpec(memory_space=pltpu.VMEM),
        scratch_shapes=[
            pltpu.SMEM((ROUNDS, SLOTS), jnp.int32),
            pltpu.SMEM((ROUNDS, ITEMS), jnp.int32),
            pltpu.VMEM((ROWS, LANES), F32),
            pltpu.VMEM((4, SHARE, LANES), F32),
            pltpu.VMEM((2, PIECES, STEP // 2, LANES), F32),
            *[pltpu.VMEM((ITEMS * BLOCK, TILE, LANES), F32)] * ROUNDS,
            pltpu.VMEM((ROUNDS, 2, CORE_SLOTS, 512), BF16),
            pltpu.VMEM((ROUNDS, 2, CORE_SLOTS, 512), BF16),
            pltpu.VMEM((ROUNDS, 2, CORE_SLOTS, LANES), F32),
            pltpu.VMEM((PAIRS, 512, WIDE), BF16),
            pltpu.VMEM((PAIRS, 512, WIDE), BF16),
            pltpu.VMEM((PAIRS, 8, WIDE), F32),
            pltpu.VMEM((PAIRS, ROUNDS, 2, 8, WIDE), F32),
            pltpu.VMEM((ROUNDS, SHARE), F32),
            pltpu.VMEM((2, 8, LANES), F32),
            pltpu.VMEM((7, 8, LANES), F32),
            pltpu.VMEM((15, 8, LANES), F32),
            pltpu.SemaphoreType.DMA((4,)),
            pltpu.SemaphoreType.DMA((COST + 2,)),
            pltpu.SemaphoreType.DMA((COPIES,)),
            pltpu.SemaphoreType.DMA((2,)),
        ],
        compiler_params=pltpu.CompilerParams(
            collective_id=0, has_side_effects=True, vmem_limit_bytes=56 * 1024 * 1024
        ),
    )(cand_index, cand_count, embeddings)


def solution(mesh):
    in_specs = (P("item", "dim"), P(None, "item"), P())
    out_specs = P(None, ("item", "dim"))
    return jax.shard_map(local, mesh=mesh, in_specs=in_specs, out_specs=out_specs, check_vma=False)
```

```python
import itertools

import jax
import jax.numpy as jnp
from jax import lax
from jax.experimental import pallas as pl
from jax.experimental.pallas import tpu as pltpu
from jax.sharding import PartitionSpec as P

CAP = 4.0
MESH = pl.DeviceIdType.MESH
ROUNDS = 3
SLOTS = 32
LANES = 128
ITEMS = 32
ROWS = 4096
SHARE = 1024
STEP = 256
PIECES = SHARE // STEP
WIDE = 512
PAIRS = SHARE // WIDE
TOTAL = 131072
TILE = 8
QUARTER = SLOTS // TILE
BLOCK = 4 * QUARTER
BUNDLE = 4 * BLOCK
HALF = 4 * BUNDLE
LOADS = 4
CORE_SLOTS = 512
BF16 = jnp.bfloat16
F32 = jnp.float32


def kernel(
    index_hbm, count_hbm, x_ref, out_ref,
    index_ref, count_ref, xv, xfull, relay_buf, cand_0, cand_1, cand_2,
    ch, cl, nrm, xh, xl, sq, low, done, part, red_line, red_plane,
    load_sem, send_sem, recv_sem, cost_sem,
):
    cand = (cand_0, cand_1, cand_2)
    item, dim = lax.axis_index("item"), lax.axis_index("dim")
    z = lax.div(item, 8)
    x = lax.div(item - z * 8, 2)
    core = item - z * 8 - x * 2

    def ring(place):
        return [place] + [jnp.where(place + k > 3, place + k - 4, place + k) for k in range(1, 4)]

    xs, ys, zs = ring(x), ring(dim), ring(z)
    sibling = item + 1 - 2 * core

    def plane(dz, dx):
        return (zs[dz] * 8 + xs[dx] * 2 + core, dim)

    def axis(k, first):
        over_x, over_z = plane(0, k)[0], plane(k, 0)[0]
        lead = 1 - core if first else core
        return (over_z + lead * (over_x - over_z), dim)

    up_a, far_a, down_a = [axis(k, True) for k in range(1, 4)]
    up_b, far_b, down_b = [axis(k, False) for k in range(1, 4)]
    up_y, far_y, down_y = [(item, ys[k]) for k in range(1, 4)]
    _, y_up, y_far, y_down = ys
    line_devices = [(sibling, dim)]
    for k in range(1, 4):
        line_devices += [(item, ys[k]), (sibling, ys[k])]
    plane_devices = [plane(dz, dx) for dz in range(4) for dx in range(4) if dz or dx]

    index_load = pltpu.make_async_copy(index_hbm, index_ref, load_sem.at[0])
    count_load = pltpu.make_async_copy(count_hbm, count_ref, load_sem.at[1])
    x_loads = []
    for k in range(LOADS):
        at = pl.ds(k * (ROWS // LOADS), ROWS // LOADS)
        x_loads.append(pltpu.make_async_copy(x_ref.at[at], xv.at[at], load_sem.at[3 + k]))
    for copy in [index_load, count_load] + x_loads:
        copy.start()
    own_rows = pltpu.make_async_copy(
        x_ref.at[pl.ds(dim * SHARE, SHARE)], xfull.at[dim], load_sem.at[2]
    )

    barrier = pltpu.get_barrier_semaphore()
    for target in line_devices + plane_devices:
        pl.semaphore_signal(barrier, inc=1, device_id=target, device_id_type=MESH)

    index_load.wait()
    count_load.wait()
    for copy in x_loads:
        copy.wait()
    pl.semaphore_wait(barrier, REDUCES)

    number = itertools.count()

    def send(src, dst, target, group):
        k = next(number)
        copy = pltpu.make_async_remote_copy(
            src_ref=src, dst_ref=dst, send_sem=send_sem.at[group], recv_sem=recv_sem.at[k],
            device_id=target, device_id_type=MESH,
        )
        copy.start()
        return copy

    def sent(ref, group):
        pltpu.make_async_copy(ref, ref, send_sem.at[group]).wait()

    half = STEP // 2
    y_copies, first, second, passes, swap, relay, near, passed = [{} for _ in range(8)]

    def near_send(t):
        lands = xfull.at[dim, pl.ds(t * STEP, STEP)]
        near[t] = (
            send(xv.at[pl.ds(y_up * SHARE + t * STEP, STEP)], lands, up_y, NEAR),
            send(xv.at[pl.ds(y_down * SHARE + t * STEP, STEP)], lands, down_y, NEAR),
        )

    def far_send(t):
        far = y_far * SHARE + t * STEP
        relay[t] = (
            send(xv.at[pl.ds(far, half)], relay_buf.at[0, t], up_y, RELAY),
            send(xv.at[pl.ds(far + half, half)], relay_buf.at[1, t], down_y, RELAY),
        )

    def far_pass(t):
        relay[t][0].wait_recv()
        up = send(relay_buf.at[0, t], xfull.at[y_down, pl.ds(t * STEP, half)], up_y, PASSED)
        relay[t][1].wait_recv()
        down = send(relay_buf.at[1, t], xfull.at[y_up, pl.ds(t * STEP + half, half)], down_y, PASSED)
        passed[t] = (up, down)

    def tiles(r, start, count):
        return cand[r].at[pl.ds(core * HALF + start, count)]

    def pick_send(r):
        def pick(g, carry):
            slots = [g * TILE + k for k in range(TILE)]
            slots = [jnp.where(slot < count_ref[r, item], slot, 0) for slot in slots]
            rows = [xv[pl.ds(index_ref[r, slot], 1), :] for slot in slots]
            cand[r][core * HALF + dim * QUARTER + g] = jnp.concatenate(rows, axis=0)
            return carry

        lax.fori_loop(0, QUARTER, pick, 0, unroll=True)

        ref = tiles(r, dim * QUARTER, QUARTER)
        y_copies[r] = [send(ref, ref, target, PICK + r) for target in (far_y, up_y, down_y)]

    def first_send(r):
        for copy in y_copies[r]:
            copy.wait_recv()
        block = tiles(r, 0, BLOCK)
        first[r] = [
            send(block, tiles(r, k * BLOCK, BLOCK), target, FIRST + r)
            for k, target in ((3, far_a), (1, up_a), (2, down_a))
        ]

    def second_send(r):
        for copy in first[r]:
            copy.wait_recv()
        part = 2 * BLOCK

        def send_part(start, to, target):
            return send(tiles(r, start, part), tiles(r, to + start, part), target, SECOND + r)

        second[r] = [send_part(0, BUNDLE, up_b), send_part(part, 2 * BUNDLE, down_b)]
        second[r] += [send_part(part, BUNDLE, up_b), send_part(0, 2 * BUNDLE, down_b)]
        swap[r] = [send(tiles(r, 0, BUNDLE), tiles(r, 0, BUNDLE), (sibling, dim), SWAP + r)]

    def second_pass(r):
        part = 2 * BLOCK
        second[r][0].wait_recv()
        up = send(tiles(r, BUNDLE, part), tiles(r, 3 * BUNDLE, part), up_b, SECOND + r)
        second[r][1].wait_recv()
        down = send(tiles(r, 2 * BUNDLE + part, part), tiles(r, 3 * BUNDLE + part, part), down_b, SECOND + r)
        passes[r] = (up, down)
        for copy in second[r][2:]:
            copy.wait_recv()
        ready = tiles(r, BUNDLE, 2 * BUNDLE)
        swap[r].append(send(ready, ready, (sibling, dim), SWAP + r))

    def second_end(r):
        for copy in passes[r]:
            copy.wait_recv()
        ready = tiles(r, 3 * BUNDLE, BUNDLE)
        swap[r].append(send(ready, ready, (sibling, dim), SWAP + r))

    def convert(r, side, bundle, count=1):
        start = (core * HALF if side == 0 else (1 - core) * HALF) + bundle * BUNDLE

        def one(step, carry):
            for k in range(4):
                at = pl.ds(pl.multiple_of(step * 4 * SLOTS + k * SLOTS, SLOTS), SLOTS)
                total = jnp.zeros((SLOTS, LANES), F32)
                for q in range(4):
                    place = start + (step - bundle) * BUNDLE + k * BLOCK + q * QUARTER
                    value = cand[r][pl.ds(place, QUARTER)].reshape(SLOTS, LANES)
                    total += value * value
                    high = value.astype(BF16)
                    ch[r, side, at, q * LANES:(q + 1) * LANES] = high
                    cl[r, side, at, q * LANES:(q + 1) * LANES] = (value - high.astype(F32)).astype(BF16)
                norm = jnp.sum(total, axis=1, keepdims=True)
                nrm[r, side, at, :] = jnp.broadcast_to(norm, (SLOTS, LANES))
            return carry

        lax.fori_loop(bundle, bundle + count, one, 0)

    def prepare(t):
        for copy in near[t] + passed[t]:
            copy.wait_recv()
        at = slice(t % 2 * STEP, (t % 2 + 1) * STEP)
        total = jnp.zeros((LANES, STEP), F32)
        for q in range(4):
            value = xfull[q, t * STEP:(t + 1) * STEP, :].T
            total += value * value
            value = -2.0 * value
            high = value.astype(BF16)
            xh[t // 2, q * LANES:(q + 1) * LANES, at] = high
            xl[t // 2, q * LANES:(q + 1) * LANES, at] = (value - high.astype(F32)).astype(BF16)
        sq[t // 2, :, at] = jnp.sum(total.reshape(LANES // 8, 8, STEP), axis=0)

    def nearest(t, r, side):
        high, rows = ch[r, side], xh[t]
        value = jnp.dot(
            jnp.concatenate([high, cl[r, side], high], axis=1),
            jnp.concatenate([rows, rows, xl[t]], axis=0),
            preferred_element_type=F32,
        )
        value = value + jnp.concatenate([nrm[r, side]] * (WIDE // LANES), axis=1)
        low[t, r, side] = jnp.min(value.reshape(CORE_SLOTS // 8, 8, WIDE), axis=0)

    def finish(t):
        norm = jnp.sum(sq[t], axis=0, keepdims=True)
        best = [
            jnp.min(jnp.minimum(low[t, r, 0], low[t, r, 1]), axis=0, keepdims=True) for r in range(ROUNDS)
        ]
        for r in range(1, ROUNDS):
            best[r] = jnp.minimum(best[r], best[r - 1])
        done[:, t * WIDE:(t + 1) * WIDE] = jnp.concatenate(
            [jnp.maximum(value + norm, 0.0) for value in best], axis=0
        )

    def many(count, body):
        def one(k, carry):
            body(k)
            return carry

        lax.fori_loop(0, count, one, 0)

    def convert_swapped(r):
        for copy in swap[r]:
            copy.wait_recv()
        convert(r, 1, 0, 4)

    pick_send(0)
    pick_send(1)
    own_rows.start()
    far_send(0)
    pick_send(2)
    first_send(0)
    far_send(1)
    first_send(1)
    near_send(0)
    first_send(2)
    second_send(0)
    far_pass(0)
    convert(0, 0, 0)
    second_send(1)
    far_send(2)
    convert(1, 0, 0)
    near_send(1)
    far_send(3)
    far_pass(1)
    own_rows.wait()
    prepare(0)
    second_pass(0)
    convert(0, 0, 1, 2)
    second_send(2)
    second_pass(1)
    convert(1, 0, 1, 2)
    near_send(2)
    far_pass(2)
    second_end(0)
    far_pass(3)
    convert(0, 0, 3)
    convert(2, 0, 0)
    near_send(3)
    prepare(1)
    nearest(0, 0, 0)
    second_pass(2)
    convert(2, 0, 1, 2)
    second_end(1)
    convert_swapped(0)
    convert(1, 0, 3)
    nearest(0, 0, 1)
    second_end(2)
    nearest(0, 1, 0)
    convert(2, 0, 3)
    convert_swapped(1)
    nearest(0, 2, 0)
    nearest(0, 1, 1)
    prepare(2)
    convert_swapped(2)
    nearest(0, 2, 1)
    finish(0)
    for r in range(ROUNDS):
        sent(cand[r].at[pl.ds(0, 3 * QUARTER)], PICK + r)
        sent(cand[r].at[pl.ds(0, 3 * BLOCK)], FIRST + r)
        sent(cand[r].at[pl.ds(0, 3 * BUNDLE)], SECOND + r)
        sent(cand[r].at[pl.ds(0, HALF)], SWAP + r)
    prepare(3)
    sent(xfull.at[pl.ds(0, 1)], RELAY)
    sent(xfull.at[pl.ds(0, 2)], NEAR)
    sent(xfull.at[pl.ds(0, 1)], PASSED)
    many(2 * ROUNDS, lambda k: nearest(1, k // 2, k % 2))
    finish(1)

    sums = sum([done[:, k * LANES:(k + 1) * LANES] for k in range(SHARE // LANES)])
    line = jnp.concatenate([sums, jnp.zeros((8 - ROUNDS, LANES), F32)], axis=0)
    for stage, (targets, landed) in enumerate(((line_devices, red_line), (plane_devices, red_plane))):
        part[stage] = line
        for k, target in enumerate(targets):
            pltpu.make_async_remote_copy(
                src_ref=part.at[stage], dst_ref=landed.at[k], send_sem=send_sem.at[COST + stage],
                recv_sem=cost_sem.at[stage], device_id=target, device_id_type=MESH,
            ).start()
        pltpu.make_async_copy(landed, landed, cost_sem.at[stage]).wait()
        line = line + jnp.sum(landed[...], axis=0)
    cost = jnp.sum(line, axis=1, keepdims=True)[:ROUNDS]
    out_ref[...] = jnp.minimum(CAP, TOTAL * done[...] / cost)
    sent(red_line, COST)
    sent(red_plane, COST + 1)


COPIES = ROUNDS * 15 + PIECES * 6
REDUCES = 22
PICK, FIRST, SECOND, SWAP, RELAY, NEAR, PASSED, COST = 0, 3, 6, 9, 12, 13, 14, 15
ANY = pl.BlockSpec(memory_space=pl.ANY)


def local(embeddings, cand_index, cand_count):
    return pl.pallas_call(
        kernel,
        out_shape=jax.ShapeDtypeStruct((ROUNDS, SHARE), F32),
        in_specs=[ANY, ANY, ANY],
        out_specs=pl.BlockSpec(memory_space=pltpu.VMEM),
        scratch_shapes=[
            pltpu.SMEM((ROUNDS, SLOTS), jnp.int32),
            pltpu.SMEM((ROUNDS, ITEMS), jnp.int32),
            pltpu.VMEM((ROWS, LANES), F32),
            pltpu.VMEM((4, SHARE, LANES), F32),
            pltpu.VMEM((2, PIECES, STEP // 2, LANES), F32),
            *[pltpu.VMEM((ITEMS * BLOCK, TILE, LANES), F32)] * ROUNDS,
            pltpu.VMEM((ROUNDS, 2, CORE_SLOTS, 512), BF16),
            pltpu.VMEM((ROUNDS, 2, CORE_SLOTS, 512), BF16),
            pltpu.VMEM((ROUNDS, 2, CORE_SLOTS, LANES), F32),
            pltpu.VMEM((PAIRS, 512, WIDE), BF16),
            pltpu.VMEM((PAIRS, 512, WIDE), BF16),
            pltpu.VMEM((PAIRS, 8, WIDE), F32),
            pltpu.VMEM((PAIRS, ROUNDS, 2, 8, WIDE), F32),
            pltpu.VMEM((ROUNDS, SHARE), F32),
            pltpu.VMEM((2, 8, LANES), F32),
            pltpu.VMEM((7, 8, LANES), F32),
            pltpu.VMEM((15, 8, LANES), F32),
            pltpu.SemaphoreType.DMA((3 + LOADS,)),
            pltpu.SemaphoreType.DMA((COST + 2,)),
            pltpu.SemaphoreType.DMA((COPIES,)),
            pltpu.SemaphoreType.DMA((2,)),
        ],
        compiler_params=pltpu.CompilerParams(
            collective_id=0, has_side_effects=True, vmem_limit_bytes=56 * 1024 * 1024
        ),
    )(cand_index, cand_count, embeddings)


def solution(mesh):
    in_specs = (P("item", "dim"), P(None, "item"), P())
    out_specs = P(None, ("item", "dim"))
    return jax.shard_map(local, mesh=mesh, in_specs=in_specs, out_specs=out_specs, check_vma=False)
```

```python
import itertools

import jax
import jax.numpy as jnp
from jax import lax
from jax.experimental import pallas as pl
from jax.experimental.pallas import tpu as pltpu
from jax.sharding import PartitionSpec as P

CAP = 4.0
MESH = pl.DeviceIdType.MESH
ROUNDS = 3
SLOTS = 32
LANES = 128
ITEMS = 32
ROWS = 4096
SHARE = 1024
STEP = 256
PIECES = SHARE // STEP
WIDE = 512
PAIRS = SHARE // WIDE
TOTAL = 131072
TILE = 8
QUARTER = SLOTS // TILE
BLOCK = 4 * QUARTER
BUNDLE = 4 * BLOCK
HALF = 4 * BUNDLE
LOADS = 4
CORE_SLOTS = 512
BF16 = jnp.bfloat16
F32 = jnp.float32


def kernel(
    index_hbm, count_hbm, x_ref, out_ref,
    index_ref, count_ref, xv, xfull, relay_buf, cand_0, cand_1, cand_2,
    ch, cl, nrm, xh, xl, sq, low, done, part, red_line, red_plane,
    load_sem, send_sem, recv_sem, cost_sem,
):
    cand = (cand_0, cand_1, cand_2)
    item, dim = lax.axis_index("item"), lax.axis_index("dim")
    z = lax.div(item, 8)
    x = lax.div(item - z * 8, 2)
    core = item - z * 8 - x * 2

    def ring(place):
        return [place] + [jnp.where(place + k > 3, place + k - 4, place + k) for k in range(1, 4)]

    xs, ys, zs = ring(x), ring(dim), ring(z)
    sibling = item + 1 - 2 * core

    def plane(dz, dx):
        return (zs[dz] * 8 + xs[dx] * 2 + core, dim)

    def axis(k, first):
        over_x, over_z = plane(0, k)[0], plane(k, 0)[0]
        lead = 1 - core if first else core
        return (over_z + lead * (over_x - over_z), dim)

    up_a, far_a, down_a = [axis(k, True) for k in range(1, 4)]
    up_b, far_b, down_b = [axis(k, False) for k in range(1, 4)]
    up_y, far_y, down_y = [(item, ys[k]) for k in range(1, 4)]
    _, y_up, y_far, y_down = ys
    line_devices = [(sibling, dim)]
    for k in range(1, 4):
        line_devices += [(item, ys[k]), (sibling, ys[k])]
    plane_devices = [plane(dz, dx) for dz in range(4) for dx in range(4) if dz or dx]

    index_load = pltpu.make_async_copy(index_hbm, index_ref, load_sem.at[0])
    count_load = pltpu.make_async_copy(count_hbm, count_ref, load_sem.at[1])
    x_loads = []
    for k in range(LOADS):
        at = pl.ds(k * (ROWS // LOADS), ROWS // LOADS)
        x_loads.append(pltpu.make_async_copy(x_ref.at[at], xv.at[at], load_sem.at[3 + k]))
    for copy in [index_load, count_load] + x_loads:
        copy.start()
    own_rows = pltpu.make_async_copy(
        x_ref.at[pl.ds(dim * SHARE, SHARE)], xfull.at[dim], load_sem.at[2]
    )

    barrier = pltpu.get_barrier_semaphore()
    for target in line_devices + plane_devices:
        pl.semaphore_signal(barrier, inc=1, device_id=target, device_id_type=MESH)

    index_load.wait()
    count_load.wait()
    for copy in x_loads:
        copy.wait()
    pl.semaphore_wait(barrier, REDUCES)

    number = itertools.count()

    def send(src, dst, target, group):
        k = next(number)
        copy = pltpu.make_async_remote_copy(
            src_ref=src, dst_ref=dst, send_sem=send_sem.at[group], recv_sem=recv_sem.at[k],
            device_id=target, device_id_type=MESH,
        )
        copy.start()
        return copy

    def sent(ref, group):
        pltpu.make_async_copy(ref, ref, send_sem.at[group]).wait()

    half = STEP // 2
    y_copies, first, second, passes, swap, relay, near, passed = [{} for _ in range(8)]

    def near_send(t):
        lands = xfull.at[dim, pl.ds(t * STEP, STEP)]
        near[t] = (
            send(xv.at[pl.ds(y_up * SHARE + t * STEP, STEP)], lands, up_y, NEAR),
            send(xv.at[pl.ds(y_down * SHARE + t * STEP, STEP)], lands, down_y, NEAR),
        )

    def far_send(t):
        far = y_far * SHARE + t * STEP
        relay[t] = (
            send(xv.at[pl.ds(far, half)], relay_buf.at[0, t], up_y, RELAY),
            send(xv.at[pl.ds(far + half, half)], relay_buf.at[1, t], down_y, RELAY),
        )

    def far_pass(t):
        relay[t][0].wait_recv()
        up = send(relay_buf.at[0, t], xfull.at[y_down, pl.ds(t * STEP, half)], up_y, PASSED)
        relay[t][1].wait_recv()
        down = send(relay_buf.at[1, t], xfull.at[y_up, pl.ds(t * STEP + half, half)], down_y, PASSED)
        passed[t] = (up, down)

    def tiles(r, start, count):
        return cand[r].at[pl.ds(core * HALF + start, count)]

    def pick_send(r):
        def pick(g, carry):
            slots = [g * TILE + k for k in range(TILE)]
            slots = [jnp.where(slot < count_ref[r, item], slot, 0) for slot in slots]
            rows = [xv[pl.ds(index_ref[r, slot], 1), :] for slot in slots]
            cand[r][core * HALF + dim * QUARTER + g] = jnp.concatenate(rows, axis=0)
            return carry

        lax.fori_loop(0, QUARTER, pick, 0, unroll=True)

        ref = tiles(r, dim * QUARTER, QUARTER)
        y_copies[r] = [send(ref, ref, target, PICK + r) for target in (far_y, up_y, down_y)]

    def first_send(r):
        for copy in y_copies[r]:
            copy.wait_recv()
        block = tiles(r, 0, BLOCK)
        first[r] = [
            send(block, tiles(r, k * BLOCK, BLOCK), target, FIRST + r)
            for k, target in ((3, far_a), (1, up_a), (2, down_a))
        ]

    def second_send(r):
        for copy in first[r]:
            copy.wait_recv()
        part = 2 * BLOCK

        def send_part(start, to, target):
            return send(tiles(r, start, part), tiles(r, to + start, part), target, SECOND + r)

        second[r] = [send_part(0, BUNDLE, up_b), send_part(part, 2 * BUNDLE, down_b)]
        second[r] += [send_part(part, BUNDLE, up_b), send_part(0, 2 * BUNDLE, down_b)]
        swap[r] = [send(tiles(r, 0, BUNDLE), tiles(r, 0, BUNDLE), (sibling, dim), SWAP + r)]

    def second_pass(r):
        part = 2 * BLOCK
        second[r][0].wait_recv()
        up = send(tiles(r, BUNDLE, part), tiles(r, 3 * BUNDLE, part), up_b, SECOND + r)
        second[r][1].wait_recv()
        down = send(tiles(r, 2 * BUNDLE + part, part), tiles(r, 3 * BUNDLE + part, part), down_b, SECOND + r)
        passes[r] = (up, down)
        for copy in second[r][2:]:
            copy.wait_recv()
        ready = tiles(r, BUNDLE, 2 * BUNDLE)
        swap[r].append(send(ready, ready, (sibling, dim), SWAP + r))

    def second_end(r):
        part = 2 * BLOCK
        for k, copy in enumerate(passes[r]):
            copy.wait_recv()
            ready = tiles(r, 3 * BUNDLE + k * part, part)
            swap[r].append(send(ready, ready, (sibling, dim), SWAP + r))

    def convert(r, side, bundle, count=1):
        start = (core * HALF if side == 0 else (1 - core) * HALF) + bundle * BUNDLE

        def one(step, carry):
            for k in range(4):
                at = pl.ds(pl.multiple_of(step * 4 * SLOTS + k * SLOTS, SLOTS), SLOTS)
                total = jnp.zeros((SLOTS, LANES), F32)
                for q in range(4):
                    place = start + (step - bundle) * BUNDLE + k * BLOCK + q * QUARTER
                    value = cand[r][pl.ds(place, QUARTER)].reshape(SLOTS, LANES)
                    total += value * value
                    high = value.astype(BF16)
                    ch[r, side, at, q * LANES:(q + 1) * LANES] = high
                    cl[r, side, at, q * LANES:(q + 1) * LANES] = (value - high.astype(F32)).astype(BF16)
                norm = jnp.sum(total, axis=1, keepdims=True)
                nrm[r, side, at, :] = jnp.broadcast_to(norm, (SLOTS, LANES))
            return carry

        lax.fori_loop(bundle, bundle + count, one, 0)

    def prepare(t):
        for copy in near[t] + passed[t]:
            copy.wait_recv()
        at = slice(t % 2 * STEP, (t % 2 + 1) * STEP)
        total = jnp.zeros((LANES, STEP), F32)
        for q in range(4):
            value = xfull[q, t * STEP:(t + 1) * STEP, :].T
            total += value * value
            value = -2.0 * value
            high = value.astype(BF16)
            xh[t // 2, q * LANES:(q + 1) * LANES, at] = high
            xl[t // 2, q * LANES:(q + 1) * LANES, at] = (value - high.astype(F32)).astype(BF16)
        sq[t // 2, :, at] = jnp.sum(total.reshape(LANES // 8, 8, STEP), axis=0)

    def nearest(t, r, side):
        high, rows = ch[r, side], xh[t]
        value = jnp.dot(
            jnp.concatenate([high, cl[r, side], high], axis=1),
            jnp.concatenate([rows, rows, xl[t]], axis=0),
            preferred_element_type=F32,
        )
        value = value + jnp.concatenate([nrm[r, side]] * (WIDE // LANES), axis=1)
        low[t, r, side] = jnp.min(value.reshape(CORE_SLOTS // 8, 8, WIDE), axis=0)

    def finish(t):
        norm = jnp.sum(sq[t], axis=0, keepdims=True)
        best = [
            jnp.min(jnp.minimum(low[t, r, 0], low[t, r, 1]), axis=0, keepdims=True) for r in range(ROUNDS)
        ]
        for r in range(1, ROUNDS):
            best[r] = jnp.minimum(best[r], best[r - 1])
        done[:, t * WIDE:(t + 1) * WIDE] = jnp.concatenate(
            [jnp.maximum(value + norm, 0.0) for value in best], axis=0
        )

    def many(count, body):
        def one(k, carry):
            body(k)
            return carry

        lax.fori_loop(0, count, one, 0)

    def other(r, step):
        for copy in (swap[r][0:1], swap[r][1:2], swap[r][2:4])[step]:
            copy.wait_recv()
        convert(r, 1, (0, 1, 3)[step], (1, 2, 1)[step])

    pick_send(0)
    pick_send(1)
    own_rows.start()
    far_send(0)
    pick_send(2)
    first_send(0)
    far_send(1)
    first_send(1)
    near_send(0)
    first_send(2)
    second_send(0)
    far_pass(0)
    convert(0, 0, 0)
    second_send(1)
    far_send(2)
    convert(1, 0, 0)
    near_send(1)
    far_send(3)
    far_pass(1)
    own_rows.wait()
    prepare(0)
    other(0, 0)
    second_pass(0)
    convert(0, 0, 1, 2)
    second_send(2)
    other(1, 0)
    second_pass(1)
    convert(1, 0, 1, 2)
    near_send(2)
    far_pass(2)
    second_end(0)
    far_pass(3)
    convert(0, 0, 3)
    convert(2, 0, 0)
    other(0, 1)
    near_send(3)
    prepare(1)
    nearest(0, 0, 0)
    second_pass(2)
    convert(2, 0, 1, 2)
    second_end(1)
    other(0, 2)
    nearest(0, 0, 1)
    convert(1, 0, 3)
    other(1, 1)
    nearest(0, 1, 0)
    second_end(2)
    convert(2, 0, 3)
    other(1, 2)
    other(2, 0)
    nearest(0, 2, 0)
    nearest(0, 1, 1)
    other(2, 1)
    prepare(2)
    other(2, 2)
    nearest(0, 2, 1)
    finish(0)
    for r in range(ROUNDS):
        sent(cand[r].at[pl.ds(0, 3 * QUARTER)], PICK + r)
        sent(cand[r].at[pl.ds(0, 3 * BLOCK)], FIRST + r)
        sent(cand[r].at[pl.ds(0, 3 * BUNDLE)], SECOND + r)
        sent(cand[r].at[pl.ds(0, HALF)], SWAP + r)
    prepare(3)
    sent(xfull.at[pl.ds(0, 1)], RELAY)
    sent(xfull.at[pl.ds(0, 2)], NEAR)
    sent(xfull.at[pl.ds(0, 1)], PASSED)
    many(2 * ROUNDS, lambda k: nearest(1, k // 2, k % 2))
    finish(1)

    sums = sum([done[:, k * LANES:(k + 1) * LANES] for k in range(SHARE // LANES)])
    line = jnp.concatenate([sums, jnp.zeros((8 - ROUNDS, LANES), F32)], axis=0)
    for stage, (targets, landed) in enumerate(((line_devices, red_line), (plane_devices, red_plane))):
        part[stage] = line
        for k, target in enumerate(targets):
            pltpu.make_async_remote_copy(
                src_ref=part.at[stage], dst_ref=landed.at[k], send_sem=send_sem.at[COST + stage],
                recv_sem=cost_sem.at[stage], device_id=target, device_id_type=MESH,
            ).start()
        pltpu.make_async_copy(landed, landed, cost_sem.at[stage]).wait()
        line = line + jnp.sum(landed[...], axis=0)
    cost = jnp.sum(line, axis=1, keepdims=True)[:ROUNDS]
    out_ref[...] = jnp.minimum(CAP, TOTAL * done[...] / cost)
    sent(red_line, COST)
    sent(red_plane, COST + 1)


COPIES = ROUNDS * 16 + PIECES * 6
REDUCES = 22
PICK, FIRST, SECOND, SWAP, RELAY, NEAR, PASSED, COST = 0, 3, 6, 9, 12, 13, 14, 15
ANY = pl.BlockSpec(memory_space=pl.ANY)


def local(embeddings, cand_index, cand_count):
    return pl.pallas_call(
        kernel,
        out_shape=jax.ShapeDtypeStruct((ROUNDS, SHARE), F32),
        in_specs=[ANY, ANY, ANY],
        out_specs=pl.BlockSpec(memory_space=pltpu.VMEM),
        scratch_shapes=[
            pltpu.SMEM((ROUNDS, SLOTS), jnp.int32),
            pltpu.SMEM((ROUNDS, ITEMS), jnp.int32),
            pltpu.VMEM((ROWS, LANES), F32),
            pltpu.VMEM((4, SHARE, LANES), F32),
            pltpu.VMEM((2, PIECES, STEP // 2, LANES), F32),
            *[pltpu.VMEM((ITEMS * BLOCK, TILE, LANES), F32)] * ROUNDS,
            pltpu.VMEM((ROUNDS, 2, CORE_SLOTS, 512), BF16),
            pltpu.VMEM((ROUNDS, 2, CORE_SLOTS, 512), BF16),
            pltpu.VMEM((ROUNDS, 2, CORE_SLOTS, LANES), F32),
            pltpu.VMEM((PAIRS, 512, WIDE), BF16),
            pltpu.VMEM((PAIRS, 512, WIDE), BF16),
            pltpu.VMEM((PAIRS, 8, WIDE), F32),
            pltpu.VMEM((PAIRS, ROUNDS, 2, 8, WIDE), F32),
            pltpu.VMEM((ROUNDS, SHARE), F32),
            pltpu.VMEM((2, 8, LANES), F32),
            pltpu.VMEM((7, 8, LANES), F32),
            pltpu.VMEM((15, 8, LANES), F32),
            pltpu.SemaphoreType.DMA((3 + LOADS,)),
            pltpu.SemaphoreType.DMA((COST + 2,)),
            pltpu.SemaphoreType.DMA((COPIES,)),
            pltpu.SemaphoreType.DMA((2,)),
        ],
        compiler_params=pltpu.CompilerParams(
            collective_id=0, has_side_effects=True, vmem_limit_bytes=56 * 1024 * 1024
        ),
    )(cand_index, cand_count, embeddings)


def solution(mesh):
    in_specs = (P("item", "dim"), P(None, "item"), P())
    out_specs = P(None, ("item", "dim"))
    return jax.shard_map(local, mesh=mesh, in_specs=in_specs, out_specs=out_specs, check_vma=False)
```

```python
import itertools

import jax
import jax.numpy as jnp
from jax import lax
from jax.experimental import pallas as pl
from jax.experimental.pallas import tpu as pltpu
from jax.sharding import PartitionSpec as P

CAP = 4.0
MESH = pl.DeviceIdType.MESH
ROUNDS = 3
SLOTS = 32
LANES = 128
ITEMS = 32
ROWS = 4096
SHARE = 1024
STEP = 256
PIECES = SHARE // STEP
WIDE = 512
PAIRS = SHARE // WIDE
TOTAL = 131072
TILE = 8
QUARTER = SLOTS // TILE
BLOCK = 4 * QUARTER
BUNDLE = 4 * BLOCK
HALF = 4 * BUNDLE
LOADS = 4
CORE_SLOTS = 512
BF16 = jnp.bfloat16
F32 = jnp.float32


def kernel(
    index_hbm, count_hbm, x_ref, out_ref,
    index_ref, count_ref, xv, xfull, relay_buf, cand_0, cand_1, cand_2,
    ch, cl, nrm, xh, xl, sq, low, done, part, red_line, red_plane,
    load_sem, send_sem, recv_sem, cost_sem,
):
    cand = (cand_0, cand_1, cand_2)
    item, dim = lax.axis_index("item"), lax.axis_index("dim")
    z = lax.div(item, 8)
    x = lax.div(item - z * 8, 2)
    core = item - z * 8 - x * 2

    def ring(place):
        return [place] + [jnp.where(place + k > 3, place + k - 4, place + k) for k in range(1, 4)]

    xs, ys, zs = ring(x), ring(dim), ring(z)
    sibling = item + 1 - 2 * core

    def plane(dz, dx):
        return (zs[dz] * 8 + xs[dx] * 2 + core, dim)

    def axis(k, first):
        over_x, over_z = plane(0, k)[0], plane(k, 0)[0]
        lead = 1 - core if first else core
        return (over_z + lead * (over_x - over_z), dim)

    up_a, far_a, down_a = [axis(k, True) for k in range(1, 4)]
    up_b, far_b, down_b = [axis(k, False) for k in range(1, 4)]
    up_y, far_y, down_y = [(item, ys[k]) for k in range(1, 4)]
    _, y_up, y_far, y_down = ys
    line_devices = [(sibling, dim)]
    for k in range(1, 4):
        line_devices += [(item, ys[k]), (sibling, ys[k])]
    plane_devices = [plane(dz, dx) for dz in range(4) for dx in range(4) if dz or dx]

    index_load = pltpu.make_async_copy(index_hbm, index_ref, load_sem.at[0])
    count_load = pltpu.make_async_copy(count_hbm, count_ref, load_sem.at[1])
    x_loads = []
    for k in range(LOADS):
        at = pl.ds(k * (ROWS // LOADS), ROWS // LOADS)
        x_loads.append(pltpu.make_async_copy(x_ref.at[at], xv.at[at], load_sem.at[3 + k]))
    for copy in [index_load, count_load] + x_loads:
        copy.start()
    own_rows = pltpu.make_async_copy(
        x_ref.at[pl.ds(dim * SHARE, SHARE)], xfull.at[dim], load_sem.at[2]
    )

    barrier = pltpu.get_barrier_semaphore()
    near_devices = [far_y, up_y, down_y, far_a, up_a, down_a, up_b, down_b, (sibling, dim)]
    for target in near_devices:
        pl.semaphore_signal(barrier, inc=1, device_id=target, device_id_type=MESH)

    index_load.wait()
    count_load.wait()
    for copy in x_loads:
        copy.wait()
    pl.semaphore_wait(barrier, len(near_devices))

    number = itertools.count()

    def send(src, dst, target, group):
        k = next(number)
        copy = pltpu.make_async_remote_copy(
            src_ref=src, dst_ref=dst, send_sem=send_sem.at[group], recv_sem=recv_sem.at[k],
            device_id=target, device_id_type=MESH,
        )
        copy.start()
        return copy

    def sent(ref, group):
        pltpu.make_async_copy(ref, ref, send_sem.at[group]).wait()

    half = STEP // 2
    y_copies, first, second, passes, swap, relay, near, passed = [{} for _ in range(8)]

    def near_send(t):
        lands = xfull.at[dim, pl.ds(t * STEP, STEP)]
        near[t] = (
            send(xv.at[pl.ds(y_up * SHARE + t * STEP, STEP)], lands, up_y, NEAR),
            send(xv.at[pl.ds(y_down * SHARE + t * STEP, STEP)], lands, down_y, NEAR),
        )

    def far_send(t):
        far = y_far * SHARE + t * STEP
        relay[t] = (
            send(xv.at[pl.ds(far, half)], relay_buf.at[0, t], up_y, RELAY),
            send(xv.at[pl.ds(far + half, half)], relay_buf.at[1, t], down_y, RELAY),
        )

    def far_pass(t):
        relay[t][0].wait_recv()
        up = send(relay_buf.at[0, t], xfull.at[y_down, pl.ds(t * STEP, half)], up_y, PASSED)
        relay[t][1].wait_recv()
        down = send(relay_buf.at[1, t], xfull.at[y_up, pl.ds(t * STEP + half, half)], down_y, PASSED)
        passed[t] = (up, down)

    def tiles(r, start, count):
        return cand[r].at[pl.ds(core * HALF + start, count)]

    def pick_send(r):
        def pick(g, carry):
            slots = [g * TILE + k for k in range(TILE)]
            slots = [jnp.where(slot < count_ref[r, item], slot, 0) for slot in slots]
            rows = [xv[pl.ds(index_ref[r, slot], 1), :] for slot in slots]
            cand[r][core * HALF + dim * QUARTER + g] = jnp.concatenate(rows, axis=0)
            return carry

        lax.fori_loop(0, QUARTER, pick, 0, unroll=True)

        ref = tiles(r, dim * QUARTER, QUARTER)
        y_copies[r] = [send(ref, ref, target, PICK + r) for target in (far_y, up_y, down_y)]

    def first_send(r):
        for copy in y_copies[r]:
            copy.wait_recv()
        block = tiles(r, 0, BLOCK)
        first[r] = [
            send(block, tiles(r, k * BLOCK, BLOCK), target, FIRST + r)
            for k, target in ((3, far_a), (1, up_a), (2, down_a))
        ]

    def second_send(r):
        for copy in first[r]:
            copy.wait_recv()
        part = 2 * BLOCK

        def send_part(start, to, target):
            return send(tiles(r, start, part), tiles(r, to + start, part), target, SECOND + r)

        second[r] = [send_part(0, BUNDLE, up_b), send_part(part, 2 * BUNDLE, down_b)]
        second[r] += [send_part(part, BUNDLE, up_b), send_part(0, 2 * BUNDLE, down_b)]
        swap[r] = [send(tiles(r, 0, BUNDLE), tiles(r, 0, BUNDLE), (sibling, dim), SWAP + r)]

    def second_pass(r):
        part = 2 * BLOCK
        second[r][0].wait_recv()
        up = send(tiles(r, BUNDLE, part), tiles(r, 3 * BUNDLE, part), up_b, SECOND + r)
        second[r][1].wait_recv()
        down = send(tiles(r, 2 * BUNDLE + part, part), tiles(r, 3 * BUNDLE + part, part), down_b, SECOND + r)
        passes[r] = (up, down)
        for copy in second[r][2:]:
            copy.wait_recv()
        ready = tiles(r, BUNDLE, 2 * BUNDLE)
        swap[r].append(send(ready, ready, (sibling, dim), SWAP + r))

    def second_end(r):
        part = 2 * BLOCK
        for k, copy in enumerate(passes[r]):
            copy.wait_recv()
            ready = tiles(r, 3 * BUNDLE + k * part, part)
            swap[r].append(send(ready, ready, (sibling, dim), SWAP + r))

    def convert(r, side, bundle, count=1):
        start = (core * HALF if side == 0 else (1 - core) * HALF) + bundle * BUNDLE

        def one(step, carry):
            for k in range(4):
                at = pl.ds(pl.multiple_of(step * 4 * SLOTS + k * SLOTS, SLOTS), SLOTS)
                total = jnp.zeros((SLOTS, LANES), F32)
                for q in range(4):
                    place = start + (step - bundle) * BUNDLE + k * BLOCK + q * QUARTER
                    value = cand[r][pl.ds(place, QUARTER)].reshape(SLOTS, LANES)
                    total += value * value
                    high = value.astype(BF16)
                    ch[r, side, at, q * LANES:(q + 1) * LANES] = high
                    cl[r, side, at, q * LANES:(q + 1) * LANES] = (value - high.astype(F32)).astype(BF16)
                norm = jnp.sum(total, axis=1, keepdims=True)
                nrm[r, side, at, :] = jnp.broadcast_to(norm, (SLOTS, LANES))
            return carry

        lax.fori_loop(bundle, bundle + count, one, 0)

    def prepare(t):
        for copy in near[t] + passed[t]:
            copy.wait_recv()
        at = slice(t % 2 * STEP, (t % 2 + 1) * STEP)
        total = jnp.zeros((LANES, STEP), F32)
        for q in range(4):
            value = xfull[q, t * STEP:(t + 1) * STEP, :].T
            total += value * value
            value = -2.0 * value
            high = value.astype(BF16)
            xh[t // 2, q * LANES:(q + 1) * LANES, at] = high
            xl[t // 2, q * LANES:(q + 1) * LANES, at] = (value - high.astype(F32)).astype(BF16)
        sq[t // 2, :, at] = jnp.sum(total.reshape(LANES // 8, 8, STEP), axis=0)

    def nearest(t, r, side):
        high, rows = ch[r, side], xh[t]
        value = jnp.dot(
            jnp.concatenate([high, cl[r, side], high], axis=1),
            jnp.concatenate([rows, rows, xl[t]], axis=0),
            preferred_element_type=F32,
        )
        value = value + jnp.concatenate([nrm[r, side]] * (WIDE // LANES), axis=1)
        low[t, r, side] = jnp.min(value.reshape(CORE_SLOTS // 8, 8, WIDE), axis=0)

    def finish(t):
        norm = jnp.sum(sq[t], axis=0, keepdims=True)
        best = [
            jnp.min(jnp.minimum(low[t, r, 0], low[t, r, 1]), axis=0, keepdims=True) for r in range(ROUNDS)
        ]
        for r in range(1, ROUNDS):
            best[r] = jnp.minimum(best[r], best[r - 1])
        done[:, t * WIDE:(t + 1) * WIDE] = jnp.concatenate(
            [jnp.maximum(value + norm, 0.0) for value in best], axis=0
        )

    def many(count, body):
        def one(k, carry):
            body(k)
            return carry

        lax.fori_loop(0, count, one, 0)

    def other(r, step):
        for copy in (swap[r][0:1], swap[r][1:2], swap[r][2:4])[step]:
            copy.wait_recv()
        convert(r, 1, (0, 1, 3)[step], (1, 2, 1)[step])

    pick_send(0)
    pick_send(1)
    own_rows.start()
    far_send(0)
    pick_send(2)
    first_send(0)
    far_send(1)
    first_send(1)
    near_send(0)
    first_send(2)
    second_send(0)
    far_pass(0)
    convert(0, 0, 0)
    second_send(1)
    far_send(2)
    convert(1, 0, 0)
    near_send(1)
    far_send(3)
    far_pass(1)
    own_rows.wait()
    prepare(0)
    other(0, 0)
    second_pass(0)
    convert(0, 0, 1, 2)
    second_send(2)
    other(1, 0)
    second_pass(1)
    convert(1, 0, 1, 2)
    near_send(2)
    far_pass(2)
    second_end(0)
    far_pass(3)
    convert(0, 0, 3)
    convert(2, 0, 0)
    other(0, 1)
    near_send(3)
    prepare(1)
    nearest(0, 0, 0)
    second_pass(2)
    convert(2, 0, 1, 2)
    second_end(1)
    other(0, 2)
    nearest(0, 0, 1)
    convert(1, 0, 3)
    other(1, 1)
    nearest(0, 1, 0)
    second_end(2)
    convert(2, 0, 3)
    other(1, 2)
    other(2, 0)
    nearest(0, 2, 0)
    nearest(0, 1, 1)
    other(2, 1)
    prepare(2)
    other(2, 2)
    nearest(0, 2, 1)
    finish(0)
    for r in range(ROUNDS):
        sent(cand[r].at[pl.ds(0, 3 * QUARTER)], PICK + r)
        sent(cand[r].at[pl.ds(0, 3 * BLOCK)], FIRST + r)
        sent(cand[r].at[pl.ds(0, 3 * BUNDLE)], SECOND + r)
        sent(cand[r].at[pl.ds(0, HALF)], SWAP + r)
    prepare(3)
    sent(xfull.at[pl.ds(0, 1)], RELAY)
    sent(xfull.at[pl.ds(0, 2)], NEAR)
    sent(xfull.at[pl.ds(0, 1)], PASSED)
    many(2 * ROUNDS, lambda k: nearest(1, k // 2, k % 2))
    finish(1)

    sums = sum([done[:, k * LANES:(k + 1) * LANES] for k in range(SHARE // LANES)])
    line = jnp.concatenate([sums, jnp.zeros((8 - ROUNDS, LANES), F32)], axis=0)
    for stage, (targets, landed) in enumerate(((line_devices, red_line), (plane_devices, red_plane))):
        part[stage] = line
        for k, target in enumerate(targets):
            pltpu.make_async_remote_copy(
                src_ref=part.at[stage], dst_ref=landed.at[k], send_sem=send_sem.at[COST + stage],
                recv_sem=cost_sem.at[stage], device_id=target, device_id_type=MESH,
            ).start()
        pltpu.make_async_copy(landed, landed, cost_sem.at[stage]).wait()
        line = line + jnp.sum(landed[...], axis=0)
    cost = jnp.sum(line, axis=1, keepdims=True)[:ROUNDS]
    out_ref[...] = jnp.minimum(CAP, TOTAL * done[...] / cost)
    sent(red_line, COST)
    sent(red_plane, COST + 1)


COPIES = ROUNDS * 16 + PIECES * 6
PICK, FIRST, SECOND, SWAP, RELAY, NEAR, PASSED, COST = 0, 3, 6, 9, 12, 13, 14, 15
ANY = pl.BlockSpec(memory_space=pl.ANY)


def local(embeddings, cand_index, cand_count):
    return pl.pallas_call(
        kernel,
        out_shape=jax.ShapeDtypeStruct((ROUNDS, SHARE), F32),
        in_specs=[ANY, ANY, ANY],
        out_specs=pl.BlockSpec(memory_space=pltpu.VMEM),
        scratch_shapes=[
            pltpu.SMEM((ROUNDS, SLOTS), jnp.int32),
            pltpu.SMEM((ROUNDS, ITEMS), jnp.int32),
            pltpu.VMEM((ROWS, LANES), F32),
            pltpu.VMEM((4, SHARE, LANES), F32),
            pltpu.VMEM((2, PIECES, STEP // 2, LANES), F32),
            *[pltpu.VMEM((ITEMS * BLOCK, TILE, LANES), F32)] * ROUNDS,
            pltpu.VMEM((ROUNDS, 2, CORE_SLOTS, 512), BF16),
            pltpu.VMEM((ROUNDS, 2, CORE_SLOTS, 512), BF16),
            pltpu.VMEM((ROUNDS, 2, CORE_SLOTS, LANES), F32),
            pltpu.VMEM((PAIRS, 512, WIDE), BF16),
            pltpu.VMEM((PAIRS, 512, WIDE), BF16),
            pltpu.VMEM((PAIRS, 8, WIDE), F32),
            pltpu.VMEM((PAIRS, ROUNDS, 2, 8, WIDE), F32),
            pltpu.VMEM((ROUNDS, SHARE), F32),
            pltpu.VMEM((2, 8, LANES), F32),
            pltpu.VMEM((7, 8, LANES), F32),
            pltpu.VMEM((15, 8, LANES), F32),
            pltpu.SemaphoreType.DMA((3 + LOADS,)),
            pltpu.SemaphoreType.DMA((COST + 2,)),
            pltpu.SemaphoreType.DMA((COPIES,)),
            pltpu.SemaphoreType.DMA((2,)),
        ],
        compiler_params=pltpu.CompilerParams(
            collective_id=0, has_side_effects=True, vmem_limit_bytes=56 * 1024 * 1024
        ),
    )(cand_index, cand_count, embeddings)


def solution(mesh):
    in_specs = (P("item", "dim"), P(None, "item"), P())
    out_specs = P(None, ("item", "dim"))
    return jax.shard_map(local, mesh=mesh, in_specs=in_specs, out_specs=out_specs, check_vma=False)
```

```python
import itertools

import jax
import jax.numpy as jnp
from jax import lax
from jax.experimental import pallas as pl
from jax.experimental.pallas import tpu as pltpu
from jax.sharding import PartitionSpec as P

CAP = 4.0
MESH = pl.DeviceIdType.MESH
ROUNDS = 3
SLOTS = 32
LANES = 128
ITEMS = 32
ROWS = 4096
SHARE = 1024
STEP = 256
PIECES = SHARE // STEP
WIDE = 512
PAIRS = SHARE // WIDE
TOTAL = 131072
TILE = 8
QUARTER = SLOTS // TILE
BLOCK = 4 * QUARTER
BUNDLE = 4 * BLOCK
HALF = 4 * BUNDLE
LOADS = 4
CORE_SLOTS = 512
BF16 = jnp.bfloat16
F32 = jnp.float32


def kernel(
    index_hbm, count_hbm, x_ref, out_ref,
    index_ref, count_ref, xv, xfull, relay_buf, cand_0, cand_1, cand_2,
    ch, cl, nrm, xh, xl, sq, low, done, part, red_line, red_plane,
    load_sem, send_sem, recv_sem, cost_sem,
):
    cand = (cand_0, cand_1, cand_2)
    item, dim = lax.axis_index("item"), lax.axis_index("dim")
    z = lax.div(item, 8)
    x = lax.div(item - z * 8, 2)
    core = item - z * 8 - x * 2

    def ring(place):
        return [place] + [jnp.where(place + k > 3, place + k - 4, place + k) for k in range(1, 4)]

    xs, ys, zs = ring(x), ring(dim), ring(z)
    sibling = item + 1 - 2 * core

    def plane(dz, dx):
        return (zs[dz] * 8 + xs[dx] * 2 + core, dim)

    def axis(k, first):
        over_x, over_z = plane(0, k)[0], plane(k, 0)[0]
        lead = 1 - core if first else core
        return (over_z + lead * (over_x - over_z), dim)

    up_a, far_a, down_a = [axis(k, True) for k in range(1, 4)]
    up_b, far_b, down_b = [axis(k, False) for k in range(1, 4)]
    up_y, far_y, down_y = [(item, ys[k]) for k in range(1, 4)]
    _, y_up, y_far, y_down = ys
    line_devices = [(sibling, dim)]
    for k in range(1, 4):
        line_devices += [(item, ys[k]), (sibling, ys[k])]
    plane_devices = [plane(dz, dx) for dz in range(4) for dx in range(4) if dz or dx]

    index_load = pltpu.make_async_copy(index_hbm, index_ref, load_sem.at[0])
    count_load = pltpu.make_async_copy(count_hbm, count_ref, load_sem.at[1])
    x_loads = []
    for k in range(LOADS):
        at = pl.ds(k * (ROWS // LOADS), ROWS // LOADS)
        x_loads.append(pltpu.make_async_copy(x_ref.at[at], xv.at[at], load_sem.at[3 + k]))
    for copy in [index_load, count_load] + x_loads:
        copy.start()
    own_rows = pltpu.make_async_copy(
        x_ref.at[pl.ds(dim * SHARE, SHARE)], xfull.at[dim], load_sem.at[2]
    )

    barrier = pltpu.get_barrier_semaphore()
    near_devices = [far_y, up_y, down_y, far_a, up_a, down_a, up_b, down_b, (sibling, dim)]
    for target in near_devices:
        pl.semaphore_signal(barrier, inc=1, device_id=target, device_id_type=MESH)

    index_load.wait()
    count_load.wait()
    for copy in x_loads:
        copy.wait()
    pl.semaphore_wait(barrier, len(near_devices))

    number = itertools.count()

    def send(src, dst, target, group):
        k = next(number)
        copy = pltpu.make_async_remote_copy(
            src_ref=src, dst_ref=dst, send_sem=send_sem.at[group], recv_sem=recv_sem.at[k],
            device_id=target, device_id_type=MESH,
        )
        copy.start()
        return copy

    def sent(ref, group):
        pltpu.make_async_copy(ref, ref, send_sem.at[group]).wait()

    half = STEP // 2
    y_copies, first, second, passes, swap, relay, near, passed = [{} for _ in range(8)]

    def near_send(t):
        lands = xfull.at[dim, pl.ds(t * STEP, STEP)]
        near[t] = (
            send(xv.at[pl.ds(y_up * SHARE + t * STEP, STEP)], lands, up_y, NEAR),
            send(xv.at[pl.ds(y_down * SHARE + t * STEP, STEP)], lands, down_y, NEAR),
        )

    def far_send(t):
        far = y_far * SHARE + t * STEP
        relay[t] = (
            send(xv.at[pl.ds(far, half)], relay_buf.at[0, t], up_y, RELAY),
            send(xv.at[pl.ds(far + half, half)], relay_buf.at[1, t], down_y, RELAY),
        )

    def far_pass(t):
        relay[t][0].wait_recv()
        up = send(relay_buf.at[0, t], xfull.at[y_down, pl.ds(t * STEP, half)], up_y, PASSED)
        relay[t][1].wait_recv()
        down = send(relay_buf.at[1, t], xfull.at[y_up, pl.ds(t * STEP + half, half)], down_y, PASSED)
        passed[t] = (up, down)

    def tiles(r, start, count):
        return cand[r].at[pl.ds(core * HALF + start, count)]

    def pick_send(r):
        def pick(g, carry):
            slots = [g * TILE + k for k in range(TILE)]
            slots = [jnp.where(slot < count_ref[r, item], slot, 0) for slot in slots]
            rows = [xv[pl.ds(index_ref[r, slot], 1), :] for slot in slots]
            cand[r][core * HALF + dim * QUARTER + g] = jnp.concatenate(rows, axis=0)
            return carry

        lax.fori_loop(0, QUARTER, pick, 0, unroll=True)

        ref = tiles(r, dim * QUARTER, QUARTER)
        y_copies[r] = [send(ref, ref, target, PICK + r) for target in (far_y, up_y, down_y)]

    def first_send(r):
        for copy in y_copies[r]:
            copy.wait_recv()
        block = tiles(r, 0, BLOCK)
        first[r] = [
            send(block, tiles(r, k * BLOCK, BLOCK), target, FIRST + r)
            for k, target in ((3, far_a), (1, up_a), (2, down_a))
        ]

    def second_send(r):
        for copy in first[r]:
            copy.wait_recv()
        part = 2 * BLOCK

        def send_part(start, to, target):
            return send(tiles(r, start, part), tiles(r, to + start, part), target, SECOND + r)

        second[r] = [send_part(0, BUNDLE, up_b), send_part(part, 2 * BUNDLE, down_b)]
        second[r] += [send_part(part, BUNDLE, up_b), send_part(0, 2 * BUNDLE, down_b)]
        swap[r] = [send(tiles(r, 0, BUNDLE), tiles(r, 0, BUNDLE), (sibling, dim), SWAP + r)]

    def second_pass(r):
        part = 2 * BLOCK
        second[r][0].wait_recv()
        up = send(tiles(r, BUNDLE, part), tiles(r, 3 * BUNDLE, part), up_b, SECOND + r)
        second[r][1].wait_recv()
        down = send(tiles(r, 2 * BUNDLE + part, part), tiles(r, 3 * BUNDLE + part, part), down_b, SECOND + r)
        passes[r] = (up, down)
        for copy in second[r][2:]:
            copy.wait_recv()
        ready = tiles(r, BUNDLE, 2 * BUNDLE)
        swap[r].append(send(ready, ready, (sibling, dim), SWAP + r))

    def second_end(r):
        part = 2 * BLOCK
        for k, copy in enumerate(passes[r]):
            copy.wait_recv()
            ready = tiles(r, 3 * BUNDLE + k * part, part)
            swap[r].append(send(ready, ready, (sibling, dim), SWAP + r))

    def convert(r, side, bundle, count=1):
        start = (core * HALF if side == 0 else (1 - core) * HALF) + bundle * BUNDLE

        def one(step, carry):
            for k in range(4):
                at = pl.ds(pl.multiple_of(step * 4 * SLOTS + k * SLOTS, SLOTS), SLOTS)
                total = jnp.zeros((SLOTS, LANES), F32)
                for q in range(4):
                    place = start + (step - bundle) * BUNDLE + k * BLOCK + q * QUARTER
                    value = cand[r][pl.ds(place, QUARTER)].reshape(SLOTS, LANES)
                    total += value * value
                    high = value.astype(BF16)
                    ch[r, side, at, q * LANES:(q + 1) * LANES] = high
                    cl[r, side, at, q * LANES:(q + 1) * LANES] = (value - high.astype(F32)).astype(BF16)
                norm = jnp.sum(total, axis=1, keepdims=True)
                nrm[r, side, at, :] = jnp.broadcast_to(norm, (SLOTS, LANES))
            return carry

        lax.fori_loop(bundle, bundle + count, one, 0)

    def prepare(t):
        for copy in near[t] + passed[t]:
            copy.wait_recv()
        at = slice(t % 2 * STEP, (t % 2 + 1) * STEP)
        total = jnp.zeros((LANES, STEP), F32)
        for q in range(4):
            value = xfull[q, t * STEP:(t + 1) * STEP, :].T
            total += value * value
            value = -2.0 * value
            high = value.astype(BF16)
            xh[t // 2, q * LANES:(q + 1) * LANES, at] = high
            xl[t // 2, q * LANES:(q + 1) * LANES, at] = (value - high.astype(F32)).astype(BF16)
        sq[t // 2, :, at] = jnp.sum(total.reshape(LANES // 8, 8, STEP), axis=0)

    def nearest(t, r, side):
        high, rows = ch[r, side], xh[t]
        value = jnp.dot(
            jnp.concatenate([high, cl[r, side], high], axis=1),
            jnp.concatenate([rows, rows, xl[t]], axis=0),
            preferred_element_type=F32,
        )
        value = value + jnp.concatenate([nrm[r, side]] * (WIDE // LANES), axis=1)
        low[t, r, side] = jnp.min(value.reshape(CORE_SLOTS // 8, 8, WIDE), axis=0)

    def nearest_both(t, r):
        high, rows = ch[r].reshape(2 * CORE_SLOTS, 512), xh[t]
        value = jnp.dot(
            jnp.concatenate([high, cl[r].reshape(2 * CORE_SLOTS, 512), high], axis=1),
            jnp.concatenate([rows, rows, xl[t]], axis=0),
            preferred_element_type=F32,
        )
        norm = nrm[r].reshape(2 * CORE_SLOTS, LANES)
        value = value + jnp.concatenate([norm] * (WIDE // LANES), axis=1)
        value = jnp.min(value.reshape(2 * CORE_SLOTS // 8, 8, WIDE), axis=0)
        low[t, r, 0] = value
        low[t, r, 1] = value

    def finish(t):
        norm = jnp.sum(sq[t], axis=0, keepdims=True)
        best = [
            jnp.min(jnp.minimum(low[t, r, 0], low[t, r, 1]), axis=0, keepdims=True) for r in range(ROUNDS)
        ]
        for r in range(1, ROUNDS):
            best[r] = jnp.minimum(best[r], best[r - 1])
        done[:, t * WIDE:(t + 1) * WIDE] = jnp.concatenate(
            [jnp.maximum(value + norm, 0.0) for value in best], axis=0
        )

    def many(count, body):
        def one(k, carry):
            body(k)
            return carry

        lax.fori_loop(0, count, one, 0)

    def other(r, step):
        for copy in (swap[r][0:1], swap[r][1:2], swap[r][2:4])[step]:
            copy.wait_recv()
        convert(r, 1, (0, 1, 3)[step], (1, 2, 1)[step])

    pick_send(0)
    pick_send(1)
    own_rows.start()
    far_send(0)
    pick_send(2)
    first_send(0)
    far_send(1)
    first_send(1)
    near_send(0)
    first_send(2)
    second_send(0)
    far_pass(0)
    convert(0, 0, 0)
    second_send(1)
    far_send(2)
    convert(1, 0, 0)
    near_send(1)
    far_send(3)
    far_pass(1)
    own_rows.wait()
    prepare(0)
    other(0, 0)
    second_pass(0)
    convert(0, 0, 1, 2)
    second_send(2)
    other(1, 0)
    second_pass(1)
    convert(1, 0, 1, 2)
    near_send(2)
    far_pass(2)
    second_end(0)
    far_pass(3)
    convert(0, 0, 3)
    convert(2, 0, 0)
    other(0, 1)
    near_send(3)
    prepare(1)
    nearest(0, 0, 0)
    second_pass(2)
    convert(2, 0, 1, 2)
    second_end(1)
    other(0, 2)
    nearest(0, 0, 1)
    convert(1, 0, 3)
    other(1, 1)
    nearest(0, 1, 0)
    second_end(2)
    convert(2, 0, 3)
    other(1, 2)
    other(2, 0)
    nearest(0, 1, 1)
    other(2, 1)
    prepare(2)
    other(2, 2)
    nearest_both(0, 2)
    finish(0)
    for r in range(ROUNDS):
        sent(cand[r].at[pl.ds(0, 3 * QUARTER)], PICK + r)
        sent(cand[r].at[pl.ds(0, 3 * BLOCK)], FIRST + r)
        sent(cand[r].at[pl.ds(0, 3 * BUNDLE)], SECOND + r)
        sent(cand[r].at[pl.ds(0, HALF)], SWAP + r)
    prepare(3)
    sent(xfull.at[pl.ds(0, 1)], RELAY)
    sent(xfull.at[pl.ds(0, 2)], NEAR)
    sent(xfull.at[pl.ds(0, 1)], PASSED)
    many(ROUNDS, lambda r: nearest_both(1, r))
    finish(1)

    sums = sum([done[:, k * LANES:(k + 1) * LANES] for k in range(SHARE // LANES)])
    line = jnp.concatenate([sums, jnp.zeros((8 - ROUNDS, LANES), F32)], axis=0)
    for stage, (targets, landed) in enumerate(((line_devices, red_line), (plane_devices, red_plane))):
        part[stage] = line
        for k, target in enumerate(targets):
            pltpu.make_async_remote_copy(
                src_ref=part.at[stage], dst_ref=landed.at[k], send_sem=send_sem.at[COST + stage],
                recv_sem=cost_sem.at[stage], device_id=target, device_id_type=MESH,
            ).start()
        pltpu.make_async_copy(landed, landed, cost_sem.at[stage]).wait()
        line = line + jnp.sum(landed[...], axis=0)
    cost = jnp.sum(line, axis=1, keepdims=True)[:ROUNDS]
    out_ref[...] = jnp.minimum(CAP, TOTAL * done[...] / cost)
    sent(red_line, COST)
    sent(red_plane, COST + 1)


COPIES = ROUNDS * 16 + PIECES * 6
PICK, FIRST, SECOND, SWAP, RELAY, NEAR, PASSED, COST = 0, 3, 6, 9, 12, 13, 14, 15
ANY = pl.BlockSpec(memory_space=pl.ANY)


def local(embeddings, cand_index, cand_count):
    return pl.pallas_call(
        kernel,
        out_shape=jax.ShapeDtypeStruct((ROUNDS, SHARE), F32),
        in_specs=[ANY, ANY, ANY],
        out_specs=pl.BlockSpec(memory_space=pltpu.VMEM),
        scratch_shapes=[
            pltpu.SMEM((ROUNDS, SLOTS), jnp.int32),
            pltpu.SMEM((ROUNDS, ITEMS), jnp.int32),
            pltpu.VMEM((ROWS, LANES), F32),
            pltpu.VMEM((4, SHARE, LANES), F32),
            pltpu.VMEM((2, PIECES, STEP // 2, LANES), F32),
            *[pltpu.VMEM((ITEMS * BLOCK, TILE, LANES), F32)] * ROUNDS,
            pltpu.VMEM((ROUNDS, 2, CORE_SLOTS, 512), BF16),
            pltpu.VMEM((ROUNDS, 2, CORE_SLOTS, 512), BF16),
            pltpu.VMEM((ROUNDS, 2, CORE_SLOTS, LANES), F32),
            pltpu.VMEM((PAIRS, 512, WIDE), BF16),
            pltpu.VMEM((PAIRS, 512, WIDE), BF16),
            pltpu.VMEM((PAIRS, 8, WIDE), F32),
            pltpu.VMEM((PAIRS, ROUNDS, 2, 8, WIDE), F32),
            pltpu.VMEM((ROUNDS, SHARE), F32),
            pltpu.VMEM((2, 8, LANES), F32),
            pltpu.VMEM((7, 8, LANES), F32),
            pltpu.VMEM((15, 8, LANES), F32),
            pltpu.SemaphoreType.DMA((3 + LOADS,)),
            pltpu.SemaphoreType.DMA((COST + 2,)),
            pltpu.SemaphoreType.DMA((COPIES,)),
            pltpu.SemaphoreType.DMA((2,)),
        ],
        compiler_params=pltpu.CompilerParams(
            collective_id=0, has_side_effects=True, vmem_limit_bytes=56 * 1024 * 1024
        ),
    )(cand_index, cand_count, embeddings)


def solution(mesh):
    in_specs = (P("item", "dim"), P(None, "item"), P())
    out_specs = P(None, ("item", "dim"))
    return jax.shard_map(local, mesh=mesh, in_specs=in_specs, out_specs=out_specs, check_vma=False)
```

```python
import itertools

import jax
import jax.numpy as jnp
from jax import lax
from jax.experimental import pallas as pl
from jax.experimental.pallas import tpu as pltpu
from jax.sharding import PartitionSpec as P

CAP = 4.0
MESH = pl.DeviceIdType.MESH
ROUNDS = 3
SLOTS = 32
LANES = 128
ITEMS = 32
ROWS = 4096
SHARE = 1024
STEP = 256
PIECES = SHARE // STEP
WIDE = 512
PAIRS = SHARE // WIDE
TOTAL = 131072
TILE = 8
QUARTER = SLOTS // TILE
BLOCK = 4 * QUARTER
BUNDLE = 4 * BLOCK
HALF = 4 * BUNDLE
LOADS = 4
CORE_SLOTS = 512
BF16 = jnp.bfloat16
F32 = jnp.float32


def kernel(
    index_hbm, count_hbm, x_ref, out_ref,
    index_ref, count_ref, xv, xfull, relay_buf, cand_0, cand_1, cand_2,
    ch, cl, nrm, xh, xl, sq, low, done, part, red_line, red_plane,
    load_sem, send_sem, recv_sem, cost_sem,
):
    cand = (cand_0, cand_1, cand_2)
    item, dim = lax.axis_index("item"), lax.axis_index("dim")
    z = lax.div(item, 8)
    x = lax.div(item - z * 8, 2)
    core = item - z * 8 - x * 2

    def ring(place):
        return [place] + [jnp.where(place + k > 3, place + k - 4, place + k) for k in range(1, 4)]

    xs, ys, zs = ring(x), ring(dim), ring(z)
    sibling = item + 1 - 2 * core

    def plane(dz, dx):
        return (zs[dz] * 8 + xs[dx] * 2 + core, dim)

    def axis(k, first):
        over_x, over_z = plane(0, k)[0], plane(k, 0)[0]
        lead = 1 - core if first else core
        return (over_z + lead * (over_x - over_z), dim)

    up_a, far_a, down_a = [axis(k, True) for k in range(1, 4)]
    up_b, far_b, down_b = [axis(k, False) for k in range(1, 4)]
    up_y, far_y, down_y = [(item, ys[k]) for k in range(1, 4)]
    _, y_up, y_far, y_down = ys
    line_devices = [(sibling, dim)]
    for k in range(1, 4):
        line_devices += [(item, ys[k]), (sibling, ys[k])]
    plane_devices = [plane(dz, dx) for dz in range(4) for dx in range(4) if dz or dx]

    index_load = pltpu.make_async_copy(index_hbm, index_ref, load_sem.at[0])
    count_load = pltpu.make_async_copy(count_hbm, count_ref, load_sem.at[1])
    x_loads = []
    for k in range(LOADS):
        at = pl.ds(k * (ROWS // LOADS), ROWS // LOADS)
        x_loads.append(pltpu.make_async_copy(x_ref.at[at], xv.at[at], load_sem.at[3 + k]))
    for copy in [index_load, count_load] + x_loads:
        copy.start()
    own_rows = pltpu.make_async_copy(
        x_ref.at[pl.ds(dim * SHARE, SHARE)], xfull.at[dim], load_sem.at[2]
    )

    barrier = pltpu.get_barrier_semaphore()
    near_devices = [far_y, up_y, down_y, far_a, up_a, down_a, up_b, down_b, (sibling, dim)]
    for target in near_devices:
        pl.semaphore_signal(barrier, inc=1, device_id=target, device_id_type=MESH)

    index_load.wait()
    count_load.wait()
    for copy in x_loads:
        copy.wait()
    pl.semaphore_wait(barrier, len(near_devices))

    number = itertools.count()

    def send(src, dst, target, group):
        k = next(number)
        copy = pltpu.make_async_remote_copy(
            src_ref=src, dst_ref=dst, send_sem=send_sem.at[group], recv_sem=recv_sem.at[k],
            device_id=target, device_id_type=MESH,
        )
        copy.start()
        return copy

    def sent(ref, group):
        pltpu.make_async_copy(ref, ref, send_sem.at[group]).wait()

    half = STEP // 2
    y_copies, first, second, passes, swap, relay, near, passed = [{} for _ in range(8)]

    def near_send(t):
        lands = xfull.at[dim, pl.ds(t * STEP, STEP)]
        near[t] = (
            send(xv.at[pl.ds(y_up * SHARE + t * STEP, STEP)], lands, up_y, NEAR),
            send(xv.at[pl.ds(y_down * SHARE + t * STEP, STEP)], lands, down_y, NEAR),
        )

    def far_send(t):
        far = y_far * SHARE + t * STEP
        relay[t] = (
            send(xv.at[pl.ds(far, half)], relay_buf.at[0, t], up_y, RELAY),
            send(xv.at[pl.ds(far + half, half)], relay_buf.at[1, t], down_y, RELAY),
        )

    def far_pass(t):
        relay[t][0].wait_recv()
        up = send(relay_buf.at[0, t], xfull.at[y_down, pl.ds(t * STEP, half)], up_y, PASSED)
        relay[t][1].wait_recv()
        down = send(relay_buf.at[1, t], xfull.at[y_up, pl.ds(t * STEP + half, half)], down_y, PASSED)
        passed[t] = (up, down)

    def tiles(r, start, count):
        return cand[r].at[pl.ds(core * HALF + start, count)]

    def pick_send(r):
        def pick(g, carry):
            slots = [g * TILE + k for k in range(TILE)]
            slots = [jnp.where(slot < count_ref[r, item], slot, 0) for slot in slots]
            rows = [xv[pl.ds(index_ref[r, slot], 1), :] for slot in slots]
            cand[r][core * HALF + dim * QUARTER + g] = jnp.concatenate(rows, axis=0)
            return carry

        lax.fori_loop(0, QUARTER, pick, 0, unroll=True)

        ref = tiles(r, dim * QUARTER, QUARTER)
        y_copies[r] = [send(ref, ref, target, PICK + r) for target in (far_y, up_y, down_y)]

    def first_send(r):
        for copy in y_copies[r]:
            copy.wait_recv()
        block = tiles(r, 0, BLOCK)
        first[r] = [
            send(block, tiles(r, k * BLOCK, BLOCK), target, FIRST + r)
            for k, target in ((3, far_a), (1, up_a), (2, down_a))
        ]

    def second_send(r):
        for copy in first[r]:
            copy.wait_recv()
        part = 2 * BLOCK

        def send_part(start, to, target):
            return send(tiles(r, start, part), tiles(r, to + start, part), target, SECOND + r)

        second[r] = [send_part(0, BUNDLE, up_b), send_part(part, 2 * BUNDLE, down_b)]
        second[r] += [send_part(part, BUNDLE, up_b), send_part(0, 2 * BUNDLE, down_b)]
        swap[r] = [send(tiles(r, 0, BUNDLE), tiles(r, 0, BUNDLE), (sibling, dim), SWAP + r)]

    def second_pass(r):
        part = 2 * BLOCK
        second[r][0].wait_recv()
        up = send(tiles(r, BUNDLE, part), tiles(r, 3 * BUNDLE, part), up_b, SECOND + r)
        second[r][1].wait_recv()
        down = send(tiles(r, 2 * BUNDLE + part, part), tiles(r, 3 * BUNDLE + part, part), down_b, SECOND + r)
        passes[r] = (up, down)
        for copy in second[r][2:]:
            copy.wait_recv()
        ready = tiles(r, BUNDLE, 2 * BUNDLE)
        swap[r].append(send(ready, ready, (sibling, dim), SWAP + r))

    def second_end(r):
        part = 2 * BLOCK
        for k, copy in enumerate(passes[r]):
            copy.wait_recv()
            ready = tiles(r, 3 * BUNDLE + k * part, part)
            swap[r].append(send(ready, ready, (sibling, dim), SWAP + r))

    def convert(r, side, bundle, count=1):
        start = (core * HALF if side == 0 else (1 - core) * HALF) + bundle * BUNDLE

        def one(step, carry):
            for k in range(4):
                at = pl.ds(pl.multiple_of(step * 4 * SLOTS + k * SLOTS, SLOTS), SLOTS)
                total = jnp.zeros((SLOTS, LANES), F32)
                for q in range(4):
                    place = start + (step - bundle) * BUNDLE + k * BLOCK + q * QUARTER
                    value = cand[r][pl.ds(place, QUARTER)].reshape(SLOTS, LANES)
                    total += value * value
                    high = value.astype(BF16)
                    ch[r, side, at, q * LANES:(q + 1) * LANES] = high
                    cl[r, side, at, q * LANES:(q + 1) * LANES] = (value - high.astype(F32)).astype(BF16)
                norm = jnp.sum(total, axis=1, keepdims=True)
                nrm[r, side, at, :] = jnp.broadcast_to(norm, (SLOTS, LANES))
            return carry

        lax.fori_loop(bundle, bundle + count, one, 0)

    def prepare(t):
        for copy in near[t] + passed[t]:
            copy.wait_recv()
        at = slice(t % 2 * STEP, (t % 2 + 1) * STEP)
        total = jnp.zeros((LANES, STEP), F32)
        for q in range(4):
            value = xfull[q, t * STEP:(t + 1) * STEP, :].T
            total += value * value
            value = -2.0 * value
            high = value.astype(BF16)
            xh[t // 2, q * LANES:(q + 1) * LANES, at] = high
            xl[t // 2, q * LANES:(q + 1) * LANES, at] = (value - high.astype(F32)).astype(BF16)
        sq[t // 2, :, at] = jnp.sum(total.reshape(LANES // 8, 8, STEP), axis=0)

    def nearest(t, r, side):
        high, rows = ch[r, side], xh[t]
        value = jnp.dot(
            jnp.concatenate([high, cl[r, side], high], axis=1),
            jnp.concatenate([rows, rows, xl[t]], axis=0),
            preferred_element_type=F32,
        )
        value = value + jnp.concatenate([nrm[r, side]] * (WIDE // LANES), axis=1)
        low[t, r, side] = jnp.min(value.reshape(CORE_SLOTS // 8, 8, WIDE), axis=0)

    def nearest_both(t, r):
        high, rows = ch[r].reshape(2 * CORE_SLOTS, 512), xh[t]
        value = jnp.dot(
            jnp.concatenate([high, cl[r].reshape(2 * CORE_SLOTS, 512), high], axis=1),
            jnp.concatenate([rows, rows, xl[t]], axis=0),
            preferred_element_type=F32,
        )
        norm = nrm[r].reshape(2 * CORE_SLOTS, LANES)
        value = value + jnp.concatenate([norm] * (WIDE // LANES), axis=1)
        value = jnp.min(value.reshape(2 * CORE_SLOTS // 8, 8, WIDE), axis=0)
        low[t, r, 0] = value
        low[t, r, 1] = value

    def finish(t):
        norm = jnp.sum(sq[t], axis=0, keepdims=True)
        best = [
            jnp.min(jnp.minimum(low[t, r, 0], low[t, r, 1]), axis=0, keepdims=True) for r in range(ROUNDS)
        ]
        for r in range(1, ROUNDS):
            best[r] = jnp.minimum(best[r], best[r - 1])
        done[:, t * WIDE:(t + 1) * WIDE] = jnp.concatenate(
            [jnp.maximum(value + norm, 0.0) for value in best], axis=0
        )

    def many(count, body):
        def one(k, carry):
            body(k)
            return carry

        lax.fori_loop(0, count, one, 0)

    def other(r, step):
        for copy in (swap[r][0:1], swap[r][1:2], swap[r][2:4])[step]:
            copy.wait_recv()
        convert(r, 1, (0, 1, 3)[step], (1, 2, 1)[step])

    def all_sent():
        for r in range(ROUNDS):
            sent(cand[r].at[pl.ds(0, 3 * QUARTER)], PICK + r)
            sent(cand[r].at[pl.ds(0, 3 * BLOCK)], FIRST + r)
            sent(cand[r].at[pl.ds(0, 3 * BUNDLE)], SECOND + r)
            sent(cand[r].at[pl.ds(0, HALF)], SWAP + r)
        sent(xfull.at[pl.ds(0, 1)], RELAY)
        sent(xfull.at[pl.ds(0, 2)], NEAR)
        sent(xfull.at[pl.ds(0, 1)], PASSED)

    pick_send(0)
    pick_send(1)
    own_rows.start()
    far_send(0)
    pick_send(2)
    first_send(0)
    far_send(1)
    first_send(1)
    near_send(0)
    first_send(2)
    second_send(0)
    far_pass(0)
    convert(0, 0, 0)
    second_send(1)
    far_send(2)
    convert(1, 0, 0)
    near_send(1)
    far_send(3)
    far_pass(1)
    own_rows.wait()
    prepare(0)
    other(0, 0)
    second_pass(0)
    convert(0, 0, 1, 2)
    second_send(2)
    other(1, 0)
    second_pass(1)
    convert(1, 0, 1, 2)
    near_send(2)
    far_pass(2)
    second_end(0)
    far_pass(3)
    convert(0, 0, 3)
    convert(2, 0, 0)
    other(0, 1)
    near_send(3)
    prepare(1)
    nearest(0, 0, 0)
    second_pass(2)
    convert(2, 0, 1, 2)
    second_end(1)
    other(0, 2)
    nearest(0, 0, 1)
    convert(1, 0, 3)
    other(1, 1)
    nearest(0, 1, 0)
    second_end(2)
    convert(2, 0, 3)
    other(1, 2)
    other(2, 0)
    nearest(0, 1, 1)
    other(2, 1)
    prepare(2)
    other(2, 2)
    nearest_both(0, 2)
    finish(0)
    prepare(3)
    many(ROUNDS, lambda r: nearest_both(1, r))
    finish(1)

    sums = sum([done[:, k * LANES:(k + 1) * LANES] for k in range(SHARE // LANES)])
    line = jnp.concatenate([sums, jnp.zeros((8 - ROUNDS, LANES), F32)], axis=0)
    for stage, (targets, landed) in enumerate(((line_devices, red_line), (plane_devices, red_plane))):
        part[stage] = line
        for k, target in enumerate(targets):
            pltpu.make_async_remote_copy(
                src_ref=part.at[stage], dst_ref=landed.at[k], send_sem=send_sem.at[COST + stage],
                recv_sem=cost_sem.at[stage], device_id=target, device_id_type=MESH,
            ).start()
        if stage == 0:
            all_sent()
        pltpu.make_async_copy(landed, landed, cost_sem.at[stage]).wait()
        line = line + jnp.sum(landed[...], axis=0)
    cost = jnp.sum(line, axis=1, keepdims=True)[:ROUNDS]
    out_ref[...] = jnp.minimum(CAP, TOTAL * done[...] / cost)
    sent(red_line, COST)
    sent(red_plane, COST + 1)


COPIES = ROUNDS * 16 + PIECES * 6
PICK, FIRST, SECOND, SWAP, RELAY, NEAR, PASSED, COST = 0, 3, 6, 9, 12, 13, 14, 15
ANY = pl.BlockSpec(memory_space=pl.ANY)


def local(embeddings, cand_index, cand_count):
    return pl.pallas_call(
        kernel,
        out_shape=jax.ShapeDtypeStruct((ROUNDS, SHARE), F32),
        in_specs=[ANY, ANY, ANY],
        out_specs=pl.BlockSpec(memory_space=pltpu.VMEM),
        scratch_shapes=[
            pltpu.SMEM((ROUNDS, SLOTS), jnp.int32),
            pltpu.SMEM((ROUNDS, ITEMS), jnp.int32),
            pltpu.VMEM((ROWS, LANES), F32),
            pltpu.VMEM((4, SHARE, LANES), F32),
            pltpu.VMEM((2, PIECES, STEP // 2, LANES), F32),
            *[pltpu.VMEM((ITEMS * BLOCK, TILE, LANES), F32)] * ROUNDS,
            pltpu.VMEM((ROUNDS, 2, CORE_SLOTS, 512), BF16),
            pltpu.VMEM((ROUNDS, 2, CORE_SLOTS, 512), BF16),
            pltpu.VMEM((ROUNDS, 2, CORE_SLOTS, LANES), F32),
            pltpu.VMEM((PAIRS, 512, WIDE), BF16),
            pltpu.VMEM((PAIRS, 512, WIDE), BF16),
            pltpu.VMEM((PAIRS, 8, WIDE), F32),
            pltpu.VMEM((PAIRS, ROUNDS, 2, 8, WIDE), F32),
            pltpu.VMEM((ROUNDS, SHARE), F32),
            pltpu.VMEM((2, 8, LANES), F32),
            pltpu.VMEM((7, 8, LANES), F32),
            pltpu.VMEM((15, 8, LANES), F32),
            pltpu.SemaphoreType.DMA((3 + LOADS,)),
            pltpu.SemaphoreType.DMA((COST + 2,)),
            pltpu.SemaphoreType.DMA((COPIES,)),
            pltpu.SemaphoreType.DMA((2,)),
        ],
        compiler_params=pltpu.CompilerParams(
            collective_id=0, has_side_effects=True, vmem_limit_bytes=56 * 1024 * 1024
        ),
    )(cand_index, cand_count, embeddings)


def solution(mesh):
    in_specs = (P("item", "dim"), P(None, "item"), P())
    out_specs = P(None, ("item", "dim"))
    return jax.shard_map(local, mesh=mesh, in_specs=in_specs, out_specs=out_specs, check_vma=False)
```

```python
import itertools

import jax
import jax.numpy as jnp
from jax import lax
from jax.experimental import pallas as pl
from jax.experimental.pallas import tpu as pltpu
from jax.sharding import PartitionSpec as P

CAP = 4.0
MESH = pl.DeviceIdType.MESH
ROUNDS = 3
SLOTS = 32
LANES = 128
ITEMS = 32
ROWS = 4096
SHARE = 1024
STEP = 256
PIECES = SHARE // STEP
WIDE = 512
PAIRS = SHARE // WIDE
TOTAL = 131072
TILE = 8
QUARTER = SLOTS // TILE
BLOCK = 4 * QUARTER
BUNDLE = 4 * BLOCK
HALF = 4 * BUNDLE
LOADS = 4
CORE_SLOTS = 512
BF16 = jnp.bfloat16
F32 = jnp.float32


def kernel(
    index_hbm, count_hbm, x_ref, out_ref,
    index_ref, count_ref, xv, xfull, relay_buf, cand_0, cand_1, cand_2,
    ch, cl, nrm, xh, xl, sq, low, done, part, red_line, red_plane,
    load_sem, send_sem, recv_sem, cost_sem,
):
    cand = (cand_0, cand_1, cand_2)
    item, dim = lax.axis_index("item"), lax.axis_index("dim")
    z = lax.div(item, 8)
    x = lax.div(item - z * 8, 2)
    core = item - z * 8 - x * 2

    def ring(place):
        return [place] + [jnp.where(place + k > 3, place + k - 4, place + k) for k in range(1, 4)]

    xs, ys, zs = ring(x), ring(dim), ring(z)
    sibling = item + 1 - 2 * core

    def plane(dz, dx):
        return (zs[dz] * 8 + xs[dx] * 2 + core, dim)

    def axis(k, first):
        over_x, over_z = plane(0, k)[0], plane(k, 0)[0]
        lead = 1 - core if first else core
        return (over_z + lead * (over_x - over_z), dim)

    up_a, far_a, down_a = [axis(k, True) for k in range(1, 4)]
    up_b, far_b, down_b = [axis(k, False) for k in range(1, 4)]
    up_y, far_y, down_y = [(item, ys[k]) for k in range(1, 4)]
    _, y_up, y_far, y_down = ys
    line_devices = [(sibling, dim)]
    for k in range(1, 4):
        line_devices += [(item, ys[k]), (sibling, ys[k])]
    plane_devices = [plane(dz, dx) for dz in range(4) for dx in range(4) if dz or dx]

    index_load = pltpu.make_async_copy(index_hbm, index_ref, load_sem.at[0])
    count_load = pltpu.make_async_copy(count_hbm, count_ref, load_sem.at[1])
    x_loads = []
    for k in range(LOADS):
        at = pl.ds(k * (ROWS // LOADS), ROWS // LOADS)
        x_loads.append(pltpu.make_async_copy(x_ref.at[at], xv.at[at], load_sem.at[3 + k]))
    for copy in [index_load, count_load] + x_loads:
        copy.start()
    own_rows = pltpu.make_async_copy(
        x_ref.at[pl.ds(dim * SHARE, SHARE)], xfull.at[dim], load_sem.at[2]
    )

    barrier = pltpu.get_barrier_semaphore()
    near_devices = [far_y, up_y, down_y, far_a, up_a, down_a, up_b, down_b, (sibling, dim)]
    for target in near_devices:
        pl.semaphore_signal(barrier, inc=1, device_id=target, device_id_type=MESH)

    index_load.wait()
    count_load.wait()
    for copy in x_loads:
        copy.wait()
    pl.semaphore_wait(barrier, len(near_devices))

    number = itertools.count()

    def send(src, dst, target, group):
        k = next(number)
        copy = pltpu.make_async_remote_copy(
            src_ref=src, dst_ref=dst, send_sem=send_sem.at[group], recv_sem=recv_sem.at[k],
            device_id=target, device_id_type=MESH,
        )
        copy.start()
        return copy

    def sent(ref, group):
        pltpu.make_async_copy(ref, ref, send_sem.at[group]).wait()

    half = STEP // 2
    y_copies, first, second, passes, swap, relay, near, passed = [{} for _ in range(8)]

    def near_send(t):
        lands = xfull.at[dim, pl.ds(t * STEP, STEP)]
        near[t] = (
            send(xv.at[pl.ds(y_up * SHARE + t * STEP, STEP)], lands, up_y, NEAR),
            send(xv.at[pl.ds(y_down * SHARE + t * STEP, STEP)], lands, down_y, NEAR),
        )

    def far_send(t):
        far = y_far * SHARE + t * STEP
        relay[t] = (
            send(xv.at[pl.ds(far, half)], relay_buf.at[0, t], up_y, RELAY),
            send(xv.at[pl.ds(far + half, half)], relay_buf.at[1, t], down_y, RELAY),
        )

    def far_pass(t):
        relay[t][0].wait_recv()
        up = send(relay_buf.at[0, t], xfull.at[y_down, pl.ds(t * STEP, half)], up_y, PASSED)
        relay[t][1].wait_recv()
        down = send(relay_buf.at[1, t], xfull.at[y_up, pl.ds(t * STEP + half, half)], down_y, PASSED)
        passed[t] = (up, down)

    def tiles(r, start, count):
        return cand[r].at[pl.ds(core * HALF + start, count)]

    def pick_send(r):
        def pick(g, carry):
            slots = [g * TILE + k for k in range(TILE)]
            slots = [jnp.where(slot < count_ref[r, item], slot, 0) for slot in slots]
            rows = [xv[pl.ds(index_ref[r, slot], 1), :] for slot in slots]
            cand[r][core * HALF + dim * QUARTER + g] = jnp.concatenate(rows, axis=0)
            return carry

        lax.fori_loop(0, QUARTER, pick, 0, unroll=True)

        ref = tiles(r, dim * QUARTER, QUARTER)
        y_copies[r] = [send(ref, ref, target, PICK + r) for target in (far_y, up_y, down_y)]

    def first_send(r):
        for copy in y_copies[r]:
            copy.wait_recv()
        block = tiles(r, 0, BLOCK)
        first[r] = [
            send(block, tiles(r, k * BLOCK, BLOCK), target, FIRST + r)
            for k, target in ((3, far_a), (1, up_a), (2, down_a))
        ]

    def second_send(r):
        for copy in first[r]:
            copy.wait_recv()
        part = 2 * BLOCK

        def send_part(start, to, target):
            return send(tiles(r, start, part), tiles(r, to + start, part), target, SECOND + r)

        second[r] = [send_part(0, BUNDLE, up_b), send_part(part, 2 * BUNDLE, down_b)]
        second[r] += [send_part(part, BUNDLE, up_b), send_part(0, 2 * BUNDLE, down_b)]
        swap[r] = [send(tiles(r, 0, BUNDLE), tiles(r, 0, BUNDLE), (sibling, dim), SWAP + r)]

    def second_pass(r):
        part = 2 * BLOCK
        second[r][0].wait_recv()
        up = send(tiles(r, BUNDLE, part), tiles(r, 3 * BUNDLE, part), up_b, SECOND + r)
        second[r][1].wait_recv()
        down = send(tiles(r, 2 * BUNDLE + part, part), tiles(r, 3 * BUNDLE + part, part), down_b, SECOND + r)
        passes[r] = (up, down)
        for copy in second[r][2:]:
            copy.wait_recv()
        ready = tiles(r, BUNDLE, 2 * BUNDLE)
        swap[r].append(send(ready, ready, (sibling, dim), SWAP + r))

    def second_end(r):
        part = 2 * BLOCK
        for k, copy in enumerate(passes[r]):
            copy.wait_recv()
            ready = tiles(r, 3 * BUNDLE + k * part, part)
            swap[r].append(send(ready, ready, (sibling, dim), SWAP + r))

    def convert(r, side, bundle, count=1):
        start = (core * HALF if side == 0 else (1 - core) * HALF) + bundle * BUNDLE

        def one(step, carry):
            for k in range(4):
                at = pl.ds(pl.multiple_of(step * 4 * SLOTS + k * SLOTS, SLOTS), SLOTS)
                total = jnp.zeros((SLOTS, LANES), F32)
                for q in range(4):
                    place = start + (step - bundle) * BUNDLE + k * BLOCK + q * QUARTER
                    value = cand[r][pl.ds(place, QUARTER)].reshape(SLOTS, LANES)
                    total += value * value
                    high = value.astype(BF16)
                    ch[r, side, at, q * LANES:(q + 1) * LANES] = high
                    cl[r, side, at, q * LANES:(q + 1) * LANES] = (value - high.astype(F32)).astype(BF16)
                norm = jnp.sum(total, axis=1, keepdims=True)
                nrm[r, side, at, :] = jnp.broadcast_to(norm, (SLOTS, LANES))
            return carry

        lax.fori_loop(bundle, bundle + count, one, 0)

    def prepare(t):
        for copy in near[t] + passed[t]:
            copy.wait_recv()
        at = slice(t % 2 * STEP, (t % 2 + 1) * STEP)
        total = jnp.zeros((LANES, STEP), F32)
        for q in range(4):
            value = xfull[q, t * STEP:(t + 1) * STEP, :].T
            total += value * value
            value = -2.0 * value
            high = value.astype(BF16)
            xh[t // 2, q * LANES:(q + 1) * LANES, at] = high
            xl[t // 2, q * LANES:(q + 1) * LANES, at] = (value - high.astype(F32)).astype(BF16)
        sq[t // 2, :, at] = jnp.sum(total.reshape(LANES // 8, 8, STEP), axis=0)

    def nearest(t, r, side):
        high, rows = ch[r, side], xh[t]
        value = jnp.dot(
            jnp.concatenate([high, cl[r, side], high], axis=1),
            jnp.concatenate([rows, rows, xl[t]], axis=0),
            preferred_element_type=F32,
        )
        value = value + jnp.concatenate([nrm[r, side]] * (WIDE // LANES), axis=1)
        low[t, r, side] = jnp.min(value.reshape(CORE_SLOTS // 8, 8, WIDE), axis=0)

    def nearest_both(t, r):
        high, rows = ch[r].reshape(2 * CORE_SLOTS, 512), xh[t]
        value = jnp.dot(
            jnp.concatenate([high, cl[r].reshape(2 * CORE_SLOTS, 512), high], axis=1),
            jnp.concatenate([rows, rows, xl[t]], axis=0),
            preferred_element_type=F32,
        )
        norm = nrm[r].reshape(2 * CORE_SLOTS, LANES)
        value = value + jnp.concatenate([norm] * (WIDE // LANES), axis=1)
        value = jnp.min(value.reshape(2 * CORE_SLOTS // 8, 8, WIDE), axis=0)
        low[t, r, 0] = value
        low[t, r, 1] = value

    def finish(t):
        norm = jnp.sum(sq[t], axis=0, keepdims=True)
        best = [
            jnp.min(jnp.minimum(low[t, r, 0], low[t, r, 1]), axis=0, keepdims=True) for r in range(ROUNDS)
        ]
        for r in range(1, ROUNDS):
            best[r] = jnp.minimum(best[r], best[r - 1])
        done[:, t * WIDE:(t + 1) * WIDE] = jnp.concatenate(
            [jnp.maximum(value + norm, 0.0) for value in best], axis=0
        )

    def many(count, body):
        def one(k, carry):
            body(k)
            return carry

        lax.fori_loop(0, count, one, 0)

    def other(r, step):
        for copy in (swap[r][0:1], swap[r][1:2], swap[r][2:4])[step]:
            copy.wait_recv()
        convert(r, 1, (0, 1, 3)[step], (1, 2, 1)[step])

    def all_sent():
        for r in range(ROUNDS):
            sent(cand[r].at[pl.ds(0, 3 * QUARTER)], PICK + r)
            sent(cand[r].at[pl.ds(0, 3 * BLOCK)], FIRST + r)
            sent(cand[r].at[pl.ds(0, 3 * BUNDLE)], SECOND + r)
            sent(cand[r].at[pl.ds(0, HALF)], SWAP + r)
        sent(xfull.at[pl.ds(0, 1)], RELAY)
        sent(xfull.at[pl.ds(0, 2)], NEAR)
        sent(xfull.at[pl.ds(0, 1)], PASSED)

    pick_send(0)
    far_send(0)
    pick_send(1)
    own_rows.start()
    near_send(0)
    first_send(0)
    far_send(1)
    far_send(2)
    first_send(1)
    second_send(0)
    pick_send(2)
    far_pass(0)
    second_send(1)
    convert(1, 0, 0)
    near_send(1)
    convert(0, 0, 0)
    first_send(2)
    other(0, 0)
    second_pass(0)
    far_pass(1)
    convert(0, 0, 1, 2)
    own_rows.wait()
    prepare(0)
    far_pass(2)
    far_send(3)
    near_send(2)
    other(1, 0)
    second_pass(1)
    second_send(2)
    convert(1, 0, 1, 2)
    convert(2, 0, 0)
    second_end(0)
    convert(0, 0, 3)
    other(0, 1)
    near_send(3)
    prepare(1)
    nearest(0, 0, 0)
    second_end(1)
    other(0, 2)
    nearest(0, 0, 1)
    second_pass(2)
    far_pass(3)
    convert(2, 0, 1, 2)
    convert(1, 0, 3)
    other(1, 1)
    other(2, 0)
    nearest(0, 1, 0)
    other(1, 2)
    nearest(0, 1, 1)
    second_end(2)
    convert(2, 0, 3)
    other(2, 1)
    prepare(2)
    other(2, 2)
    nearest_both(0, 2)
    finish(0)
    prepare(3)
    many(ROUNDS, lambda r: nearest_both(1, r))
    finish(1)

    sums = sum([done[:, k * LANES:(k + 1) * LANES] for k in range(SHARE // LANES)])
    line = jnp.concatenate([sums, jnp.zeros((8 - ROUNDS, LANES), F32)], axis=0)
    for stage, (targets, landed) in enumerate(((line_devices, red_line), (plane_devices, red_plane))):
        part[stage] = line
        for k, target in enumerate(targets):
            pltpu.make_async_remote_copy(
                src_ref=part.at[stage], dst_ref=landed.at[k], send_sem=send_sem.at[COST + stage],
                recv_sem=cost_sem.at[stage], device_id=target, device_id_type=MESH,
            ).start()
        if stage == 0:
            all_sent()
        pltpu.make_async_copy(landed, landed, cost_sem.at[stage]).wait()
        line = line + jnp.sum(landed[...], axis=0)
    cost = jnp.sum(line, axis=1, keepdims=True)[:ROUNDS]
    out_ref[...] = jnp.minimum(CAP, TOTAL * done[...] / cost)
    sent(red_line, COST)
    sent(red_plane, COST + 1)


COPIES = ROUNDS * 16 + PIECES * 6
PICK, FIRST, SECOND, SWAP, RELAY, NEAR, PASSED, COST = 0, 3, 6, 9, 12, 13, 14, 15
ANY = pl.BlockSpec(memory_space=pl.ANY)


def local(embeddings, cand_index, cand_count):
    return pl.pallas_call(
        kernel,
        out_shape=jax.ShapeDtypeStruct((ROUNDS, SHARE), F32),
        in_specs=[ANY, ANY, ANY],
        out_specs=pl.BlockSpec(memory_space=pltpu.VMEM),
        scratch_shapes=[
            pltpu.SMEM((ROUNDS, SLOTS), jnp.int32),
            pltpu.SMEM((ROUNDS, ITEMS), jnp.int32),
            pltpu.VMEM((ROWS, LANES), F32),
            pltpu.VMEM((4, SHARE, LANES), F32),
            pltpu.VMEM((2, PIECES, STEP // 2, LANES), F32),
            *[pltpu.VMEM((ITEMS * BLOCK, TILE, LANES), F32)] * ROUNDS,
            pltpu.VMEM((ROUNDS, 2, CORE_SLOTS, 512), BF16),
            pltpu.VMEM((ROUNDS, 2, CORE_SLOTS, 512), BF16),
            pltpu.VMEM((ROUNDS, 2, CORE_SLOTS, LANES), F32),
            pltpu.VMEM((PAIRS, 512, WIDE), BF16),
            pltpu.VMEM((PAIRS, 512, WIDE), BF16),
            pltpu.VMEM((PAIRS, 8, WIDE), F32),
            pltpu.VMEM((PAIRS, ROUNDS, 2, 8, WIDE), F32),
            pltpu.VMEM((ROUNDS, SHARE), F32),
            pltpu.VMEM((2, 8, LANES), F32),
            pltpu.VMEM((7, 8, LANES), F32),
            pltpu.VMEM((15, 8, LANES), F32),
            pltpu.SemaphoreType.DMA((3 + LOADS,)),
            pltpu.SemaphoreType.DMA((COST + 2,)),
            pltpu.SemaphoreType.DMA((COPIES,)),
            pltpu.SemaphoreType.DMA((2,)),
        ],
        compiler_params=pltpu.CompilerParams(
            collective_id=0, has_side_effects=True, vmem_limit_bytes=56 * 1024 * 1024
        ),
    )(cand_index, cand_count, embeddings)


def solution(mesh):
    in_specs = (P("item", "dim"), P(None, "item"), P())
    out_specs = P(None, ("item", "dim"))
    return jax.shard_map(local, mesh=mesh, in_specs=in_specs, out_specs=out_specs, check_vma=False)
```

```python
import itertools

import jax
import jax.numpy as jnp
from jax import lax
from jax.experimental import pallas as pl
from jax.experimental.pallas import tpu as pltpu
from jax.sharding import PartitionSpec as P

CAP = 4.0
MESH = pl.DeviceIdType.MESH
ROUNDS = 3
SLOTS = 32
LANES = 128
ITEMS = 32
ROWS = 4096
SHARE = 1024
STEP = 256
PIECES = SHARE // STEP
WIDE = 512
PAIRS = SHARE // WIDE
TOTAL = 131072
TILE = 8
QUARTER = SLOTS // TILE
BLOCK = 4 * QUARTER
BUNDLE = 4 * BLOCK
HALF = 4 * BUNDLE
LOADS = 4
CORE_SLOTS = 512
BF16 = jnp.bfloat16
F32 = jnp.float32


def kernel(
    index_hbm, count_hbm, x_ref, out_ref,
    index_ref, count_ref, xv, xfull, relay_buf, cand_0, cand_1, cand_2,
    ch, cl, nrm, xh, xl, sq, low, done, part, red_line, red_plane,
    load_sem, send_sem, recv_sem, cost_sem,
):
    cand = (cand_0, cand_1, cand_2)
    item, dim = lax.axis_index("item"), lax.axis_index("dim")
    z = lax.div(item, 8)
    x = lax.div(item - z * 8, 2)
    core = item - z * 8 - x * 2

    def ring(place):
        return [place] + [jnp.where(place + k > 3, place + k - 4, place + k) for k in range(1, 4)]

    xs, ys, zs = ring(x), ring(dim), ring(z)
    sibling = item + 1 - 2 * core

    def plane(dz, dx):
        return (zs[dz] * 8 + xs[dx] * 2 + core, dim)

    def axis(k, first):
        over_x, over_z = plane(0, k)[0], plane(k, 0)[0]
        lead = 1 - core if first else core
        return (over_z + lead * (over_x - over_z), dim)

    up_a, far_a, down_a = [axis(k, True) for k in range(1, 4)]
    up_b, far_b, down_b = [axis(k, False) for k in range(1, 4)]
    up_y, far_y, down_y = [(item, ys[k]) for k in range(1, 4)]
    _, y_up, y_far, y_down = ys
    line_devices = [(sibling, dim)]
    for k in range(1, 4):
        line_devices += [(item, ys[k]), (sibling, ys[k])]
    plane_devices = [plane(dz, dx) for dz in range(4) for dx in range(4) if dz or dx]

    index_load = pltpu.make_async_copy(index_hbm, index_ref, load_sem.at[0])
    count_load = pltpu.make_async_copy(count_hbm, count_ref, load_sem.at[1])
    x_loads = []
    for k in range(LOADS):
        at = pl.ds(k * (ROWS // LOADS), ROWS // LOADS)
        x_loads.append(pltpu.make_async_copy(x_ref.at[at], xv.at[at], load_sem.at[3 + k]))
    for copy in [index_load, count_load] + x_loads:
        copy.start()
    own_rows = pltpu.make_async_copy(
        x_ref.at[pl.ds(dim * SHARE, SHARE)], xfull.at[dim], load_sem.at[2]
    )

    barrier = pltpu.get_barrier_semaphore()
    near_devices = [far_y, up_y, down_y, far_a, up_a, down_a, up_b, down_b, (sibling, dim)]
    for target in near_devices:
        pl.semaphore_signal(barrier, inc=1, device_id=target, device_id_type=MESH)

    index_load.wait()
    count_load.wait()
    for copy in x_loads:
        copy.wait()
    pl.semaphore_wait(barrier, len(near_devices))

    number = itertools.count()

    def send(src, dst, target, group):
        k = next(number)
        copy = pltpu.make_async_remote_copy(
            src_ref=src, dst_ref=dst, send_sem=send_sem.at[group], recv_sem=recv_sem.at[k],
            device_id=target, device_id_type=MESH,
        )
        copy.start()
        return copy

    def sent(ref, group):
        pltpu.make_async_copy(ref, ref, send_sem.at[group]).wait()

    half = STEP // 2
    y_copies, first, second, passes, swap, relay, near, passed = [{} for _ in range(8)]

    def near_send(t):
        lands = xfull.at[dim, pl.ds(t * STEP, STEP)]
        near[t] = (
            send(xv.at[pl.ds(y_up * SHARE + t * STEP, STEP)], lands, up_y, NEAR),
            send(xv.at[pl.ds(y_down * SHARE + t * STEP, STEP)], lands, down_y, NEAR),
        )

    def far_send(t):
        far = y_far * SHARE + t * STEP
        relay[t] = (
            send(xv.at[pl.ds(far, half)], relay_buf.at[0, t], up_y, RELAY),
            send(xv.at[pl.ds(far + half, half)], relay_buf.at[1, t], down_y, RELAY),
        )

    def far_pass(t):
        relay[t][0].wait_recv()
        up = send(relay_buf.at[0, t], xfull.at[y_down, pl.ds(t * STEP, half)], up_y, PASSED)
        relay[t][1].wait_recv()
        down = send(relay_buf.at[1, t], xfull.at[y_up, pl.ds(t * STEP + half, half)], down_y, PASSED)
        passed[t] = (up, down)

    def tiles(r, start, count):
        return cand[r].at[pl.ds(core * HALF + start, count)]

    def pick_send(r):
        def pick(g, carry):
            slots = [g * TILE + k for k in range(TILE)]
            slots = [jnp.where(slot < count_ref[r, item], slot, 0) for slot in slots]
            rows = [xv[pl.ds(index_ref[r, slot], 1), :] for slot in slots]
            cand[r][core * HALF + dim * QUARTER + g] = jnp.concatenate(rows, axis=0)
            return carry

        lax.fori_loop(0, QUARTER, pick, 0, unroll=True)

        ref = tiles(r, dim * QUARTER, QUARTER)
        y_copies[r] = [send(ref, ref, target, PICK + r) for target in (far_y, up_y, down_y)]

    def first_send(r):
        for copy in y_copies[r]:
            copy.wait_recv()
        block = tiles(r, 0, BLOCK)
        first[r] = [
            send(block, tiles(r, k * BLOCK, BLOCK), target, FIRST + r)
            for k, target in ((3, far_a), (1, up_a), (2, down_a))
        ]

    def second_send(r):
        for copy in first[r]:
            copy.wait_recv()
        part = 2 * BLOCK

        def send_part(start, to, target):
            return send(tiles(r, start, part), tiles(r, to + start, part), target, SECOND + r)

        second[r] = [send_part(0, BUNDLE, up_b), send_part(part, 2 * BUNDLE, down_b)]
        second[r] += [send_part(part, BUNDLE, up_b), send_part(0, 2 * BUNDLE, down_b)]
        swap[r] = [send(tiles(r, 0, BUNDLE), tiles(r, 0, BUNDLE), (sibling, dim), SWAP + r)]

    def second_pass(r):
        part = 2 * BLOCK
        second[r][0].wait_recv()
        up = send(tiles(r, BUNDLE, part), tiles(r, 3 * BUNDLE, part), up_b, SECOND + r)
        second[r][1].wait_recv()
        down = send(tiles(r, 2 * BUNDLE + part, part), tiles(r, 3 * BUNDLE + part, part), down_b, SECOND + r)
        passes[r] = (up, down)
        for copy in second[r][2:]:
            copy.wait_recv()
        ready = tiles(r, BUNDLE, 2 * BUNDLE)
        swap[r].append(send(ready, ready, (sibling, dim), SWAP + r))

    def second_end(r):
        part = 2 * BLOCK
        for k, copy in enumerate(passes[r]):
            copy.wait_recv()
            ready = tiles(r, 3 * BUNDLE + k * part, part)
            swap[r].append(send(ready, ready, (sibling, dim), SWAP + r))

    def convert(r, side, bundle, count=1):
        start = (core * HALF if side == 0 else (1 - core) * HALF) + bundle * BUNDLE

        def one(step, carry):
            for k in range(4):
                at = pl.ds(pl.multiple_of(step * 4 * SLOTS + k * SLOTS, SLOTS), SLOTS)
                total = jnp.zeros((SLOTS, LANES), F32)
                for q in range(4):
                    place = start + (step - bundle) * BUNDLE + k * BLOCK + q * QUARTER
                    value = cand[r][pl.ds(place, QUARTER)].reshape(SLOTS, LANES)
                    total += value * value
                    high = value.astype(BF16)
                    ch[r, side, at, q * LANES:(q + 1) * LANES] = high
                    cl[r, side, at, q * LANES:(q + 1) * LANES] = (value - high.astype(F32)).astype(BF16)
                norm = jnp.sum(total, axis=1, keepdims=True)
                nrm[r, side, at, :] = jnp.broadcast_to(norm, (SLOTS, LANES))
            return carry

        lax.fori_loop(bundle, bundle + count, one, 0)

    def prepare(t):
        for copy in near[t] + passed[t]:
            copy.wait_recv()
        at = slice(t % 2 * STEP, (t % 2 + 1) * STEP)
        total = jnp.zeros((LANES, STEP), F32)
        for q in range(4):
            value = xfull[q, t * STEP:(t + 1) * STEP, :].T
            total += value * value
            value = -2.0 * value
            high = value.astype(BF16)
            xh[t // 2, q * LANES:(q + 1) * LANES, at] = high
            xl[t // 2, q * LANES:(q + 1) * LANES, at] = (value - high.astype(F32)).astype(BF16)
        sq[t // 2, :, at] = jnp.sum(total.reshape(LANES // 8, 8, STEP), axis=0)

    def nearest(t, r, side):
        high, rows = ch[r, side], xh[t]
        value = jnp.dot(
            jnp.concatenate([high, cl[r, side], high], axis=1),
            jnp.concatenate([rows, rows, xl[t]], axis=0),
            preferred_element_type=F32,
        )
        value = value + jnp.concatenate([nrm[r, side]] * (WIDE // LANES), axis=1)
        low[t, r, side] = jnp.min(value.reshape(CORE_SLOTS // 8, 8, WIDE), axis=0)

    def nearest_both(t, r):
        high, rows = ch[r].reshape(2 * CORE_SLOTS, 512), xh[t]
        value = jnp.dot(
            jnp.concatenate([high, cl[r].reshape(2 * CORE_SLOTS, 512), high], axis=1),
            jnp.concatenate([rows, rows, xl[t]], axis=0),
            preferred_element_type=F32,
        )
        norm = nrm[r].reshape(2 * CORE_SLOTS, LANES)
        value = value + jnp.concatenate([norm] * (WIDE // LANES), axis=1)
        value = jnp.min(value.reshape(2 * CORE_SLOTS // 8, 8, WIDE), axis=0)
        low[t, r, 0] = value
        low[t, r, 1] = value

    def finish(t):
        norm = jnp.sum(sq[t], axis=0, keepdims=True)
        best = [
            jnp.min(jnp.minimum(low[t, r, 0], low[t, r, 1]), axis=0, keepdims=True) for r in range(ROUNDS)
        ]
        for r in range(1, ROUNDS):
            best[r] = jnp.minimum(best[r], best[r - 1])
        done[:, t * WIDE:(t + 1) * WIDE] = jnp.concatenate(
            [jnp.maximum(value + norm, 0.0) for value in best], axis=0
        )

    def many(count, body):
        def one(k, carry):
            body(k)
            return carry

        lax.fori_loop(0, count, one, 0)

    def other(r, step):
        for copy in (swap[r][0:1], swap[r][1:2], swap[r][2:4])[step]:
            copy.wait_recv()
        convert(r, 1, (0, 1, 3)[step], (1, 2, 1)[step])

    def all_sent():
        for r in range(ROUNDS):
            sent(cand[r].at[pl.ds(0, 3 * QUARTER)], PICK + r)
            sent(cand[r].at[pl.ds(0, 3 * BLOCK)], FIRST + r)
            sent(cand[r].at[pl.ds(0, 3 * BUNDLE)], SECOND + r)
            sent(cand[r].at[pl.ds(0, HALF)], SWAP + r)
        sent(xfull.at[pl.ds(0, 1)], RELAY)
        sent(xfull.at[pl.ds(0, 2)], NEAR)
        sent(xfull.at[pl.ds(0, 1)], PASSED)

    pick_send(0)
    pick_send(1)
    own_rows.start()
    far_send(0)
    pick_send(2)
    first_send(0)
    far_send(1)
    first_send(1)
    near_send(0)
    first_send(2)
    second_send(0)
    far_pass(0)
    convert(0, 0, 0)
    second_send(1)
    far_send(2)
    convert(1, 0, 0)
    near_send(1)
    far_send(3)
    far_pass(1)
    own_rows.wait()
    prepare(0)
    other(0, 0)
    second_pass(0)
    second_send(2)
    convert(0, 0, 1, 2)
    other(1, 0)
    second_pass(1)
    convert(1, 0, 1, 2)
    near_send(2)
    far_pass(2)
    second_end(0)
    far_pass(3)
    convert(0, 0, 3)
    convert(2, 0, 0)
    other(0, 1)
    near_send(3)
    prepare(1)
    second_pass(2)
    nearest(0, 0, 0)
    convert(2, 0, 1, 2)
    second_end(1)
    other(0, 2)
    nearest(0, 0, 1)
    convert(1, 0, 3)
    other(1, 1)
    nearest(0, 1, 0)
    second_end(2)
    convert(2, 0, 3)
    other(1, 2)
    other(2, 0)
    nearest(0, 1, 1)
    other(2, 1)
    prepare(2)
    other(2, 2)
    nearest_both(0, 2)
    finish(0)
    prepare(3)
    many(ROUNDS, lambda r: nearest_both(1, r))
    finish(1)

    sums = sum([done[:, k * LANES:(k + 1) * LANES] for k in range(SHARE // LANES)])
    line = jnp.concatenate([sums, jnp.zeros((8 - ROUNDS, LANES), F32)], axis=0)
    for stage, (targets, landed) in enumerate(((line_devices, red_line), (plane_devices, red_plane))):
        part[stage] = line
        for k, target in enumerate(targets):
            pltpu.make_async_remote_copy(
                src_ref=part.at[stage], dst_ref=landed.at[k], send_sem=send_sem.at[COST + stage],
                recv_sem=cost_sem.at[stage], device_id=target, device_id_type=MESH,
            ).start()
        if stage == 0:
            all_sent()
        pltpu.make_async_copy(landed, landed, cost_sem.at[stage]).wait()
        line = line + jnp.sum(landed[...], axis=0)
    cost = jnp.sum(line, axis=1, keepdims=True)[:ROUNDS]
    out_ref[...] = jnp.minimum(CAP, TOTAL * done[...] / cost)
    sent(red_line, COST)
    sent(red_plane, COST + 1)


COPIES = ROUNDS * 16 + PIECES * 6
PICK, FIRST, SECOND, SWAP, RELAY, NEAR, PASSED, COST = 0, 3, 6, 9, 12, 13, 14, 15
ANY = pl.BlockSpec(memory_space=pl.ANY)


def local(embeddings, cand_index, cand_count):
    return pl.pallas_call(
        kernel,
        out_shape=jax.ShapeDtypeStruct((ROUNDS, SHARE), F32),
        in_specs=[ANY, ANY, ANY],
        out_specs=pl.BlockSpec(memory_space=pltpu.VMEM),
        scratch_shapes=[
            pltpu.SMEM((ROUNDS, SLOTS), jnp.int32),
            pltpu.SMEM((ROUNDS, ITEMS), jnp.int32),
            pltpu.VMEM((ROWS, LANES), F32),
            pltpu.VMEM((4, SHARE, LANES), F32),
            pltpu.VMEM((2, PIECES, STEP // 2, LANES), F32),
            *[pltpu.VMEM((ITEMS * BLOCK, TILE, LANES), F32)] * ROUNDS,
            pltpu.VMEM((ROUNDS, 2, CORE_SLOTS, 512), BF16),
            pltpu.VMEM((ROUNDS, 2, CORE_SLOTS, 512), BF16),
            pltpu.VMEM((ROUNDS, 2, CORE_SLOTS, LANES), F32),
            pltpu.VMEM((PAIRS, 512, WIDE), BF16),
            pltpu.VMEM((PAIRS, 512, WIDE), BF16),
            pltpu.VMEM((PAIRS, 8, WIDE), F32),
            pltpu.VMEM((PAIRS, ROUNDS, 2, 8, WIDE), F32),
            pltpu.VMEM((ROUNDS, SHARE), F32),
            pltpu.VMEM((2, 8, LANES), F32),
            pltpu.VMEM((7, 8, LANES), F32),
            pltpu.VMEM((15, 8, LANES), F32),
            pltpu.SemaphoreType.DMA((3 + LOADS,)),
            pltpu.SemaphoreType.DMA((COST + 2,)),
            pltpu.SemaphoreType.DMA((COPIES,)),
            pltpu.SemaphoreType.DMA((2,)),
        ],
        compiler_params=pltpu.CompilerParams(
            collective_id=0, has_side_effects=True, vmem_limit_bytes=56 * 1024 * 1024
        ),
    )(cand_index, cand_count, embeddings)


def solution(mesh):
    in_specs = (P("item", "dim"), P(None, "item"), P())
    out_specs = P(None, ("item", "dim"))
    return jax.shard_map(local, mesh=mesh, in_specs=in_specs, out_specs=out_specs, check_vma=False)
```

```python
import itertools

import jax
import jax.numpy as jnp
from jax import lax
from jax.experimental import pallas as pl
from jax.experimental.pallas import tpu as pltpu
from jax.sharding import PartitionSpec as P

CAP = 4.0
MESH = pl.DeviceIdType.MESH
ROUNDS = 3
SLOTS = 32
LANES = 128
ITEMS = 32
ROWS = 4096
SHARE = 1024
STEP = 256
PIECES = SHARE // STEP
WIDE = 512
PAIRS = SHARE // WIDE
TOTAL = 131072
TILE = 8
QUARTER = SLOTS // TILE
BLOCK = 4 * QUARTER
BUNDLE = 4 * BLOCK
HALF = 4 * BUNDLE
LOADS = 4
CORE_SLOTS = 512
BF16 = jnp.bfloat16
F32 = jnp.float32


def kernel(
    index_hbm, count_hbm, x_ref, out_ref,
    index_ref, count_ref, xv, xfull, relay_buf, cand_0, cand_1, cand_2,
    ch, cl, nrm, xh, xl, sq, low, done, part, red_line, red_plane,
    load_sem, send_sem, recv_sem, cost_sem,
):
    cand = (cand_0, cand_1, cand_2)
    item, dim = lax.axis_index("item"), lax.axis_index("dim")
    z = lax.div(item, 8)
    x = lax.div(item - z * 8, 2)
    core = item - z * 8 - x * 2

    def ring(place):
        return [place] + [jnp.where(place + k > 3, place + k - 4, place + k) for k in range(1, 4)]

    xs, ys, zs = ring(x), ring(dim), ring(z)
    sibling = item + 1 - 2 * core

    def plane(dz, dx):
        return (zs[dz] * 8 + xs[dx] * 2 + core, dim)

    def axis(k, first):
        over_x, over_z = plane(0, k)[0], plane(k, 0)[0]
        lead = 1 - core if first else core
        return (over_z + lead * (over_x - over_z), dim)

    up_a, far_a, down_a = [axis(k, True) for k in range(1, 4)]
    up_b, far_b, down_b = [axis(k, False) for k in range(1, 4)]
    up_y, far_y, down_y = [(item, ys[k]) for k in range(1, 4)]
    _, y_up, y_far, y_down = ys
    line_devices = [(sibling, dim)]
    for k in range(1, 4):
        line_devices += [(item, ys[k]), (sibling, ys[k])]
    plane_devices = [plane(dz, dx) for dz in range(4) for dx in range(4) if dz or dx]

    index_load = pltpu.make_async_copy(index_hbm, index_ref, load_sem.at[0])
    count_load = pltpu.make_async_copy(count_hbm, count_ref, load_sem.at[1])
    x_loads = []
    for k in range(LOADS):
        at = pl.ds(k * (ROWS // LOADS), ROWS // LOADS)
        x_loads.append(pltpu.make_async_copy(x_ref.at[at], xv.at[at], load_sem.at[3 + k]))
    for copy in [index_load, count_load] + x_loads:
        copy.start()
    own_rows = pltpu.make_async_copy(
        x_ref.at[pl.ds(dim * SHARE, SHARE)], xfull.at[dim], load_sem.at[2]
    )

    barrier = pltpu.get_barrier_semaphore()
    near_devices = [far_y, up_y, down_y, far_a, up_a, down_a, up_b, down_b, (sibling, dim)]
    for target in near_devices:
        pl.semaphore_signal(barrier, inc=1, device_id=target, device_id_type=MESH)

    index_load.wait()
    count_load.wait()
    for copy in x_loads:
        copy.wait()
    pl.semaphore_wait(barrier, len(near_devices))

    number = itertools.count()

    def send(src, dst, target, group):
        k = next(number)
        copy = pltpu.make_async_remote_copy(
            src_ref=src, dst_ref=dst, send_sem=send_sem.at[group], recv_sem=recv_sem.at[k],
            device_id=target, device_id_type=MESH,
        )
        copy.start()
        return copy

    def sent(ref, group):
        pltpu.make_async_copy(ref, ref, send_sem.at[group]).wait()

    half = STEP // 2
    y_copies, first, second, passes, swap, relay, near, passed = [{} for _ in range(8)]

    def near_send(t):
        lands = xfull.at[dim, pl.ds(t * STEP, STEP)]
        near[t] = (
            send(xv.at[pl.ds(y_up * SHARE + t * STEP, STEP)], lands, up_y, NEAR),
            send(xv.at[pl.ds(y_down * SHARE + t * STEP, STEP)], lands, down_y, NEAR),
        )

    def far_send(t):
        far = y_far * SHARE + t * STEP
        relay[t] = (
            send(xv.at[pl.ds(far, half)], relay_buf.at[0, t], up_y, RELAY),
            send(xv.at[pl.ds(far + half, half)], relay_buf.at[1, t], down_y, RELAY),
        )

    def far_pass(t):
        relay[t][0].wait_recv()
        up = send(relay_buf.at[0, t], xfull.at[y_down, pl.ds(t * STEP, half)], up_y, PASSED)
        relay[t][1].wait_recv()
        down = send(relay_buf.at[1, t], xfull.at[y_up, pl.ds(t * STEP + half, half)], down_y, PASSED)
        passed[t] = (up, down)

    def tiles(r, start, count):
        return cand[r].at[pl.ds(core * HALF + start, count)]

    def pick_send(r):
        def pick(g, carry):
            slots = [g * TILE + k for k in range(TILE)]
            slots = [jnp.where(slot < count_ref[r, item], slot, 0) for slot in slots]
            rows = [xv[pl.ds(index_ref[r, slot], 1), :] for slot in slots]
            cand[r][core * HALF + dim * QUARTER + g] = jnp.concatenate(rows, axis=0)
            return carry

        lax.fori_loop(0, QUARTER, pick, 0, unroll=True)

        ref = tiles(r, dim * QUARTER, QUARTER)
        y_copies[r] = [send(ref, ref, target, PICK + r) for target in (far_y, up_y, down_y)]

    def first_send(r):
        for copy in y_copies[r]:
            copy.wait_recv()
        block = tiles(r, 0, BLOCK)
        first[r] = [
            send(block, tiles(r, k * BLOCK, BLOCK), target, FIRST + r)
            for k, target in ((3, far_a), (1, up_a), (2, down_a))
        ]

    def second_send(r):
        for copy in first[r]:
            copy.wait_recv()
        part = 2 * BLOCK

        def send_part(start, to, target):
            return send(tiles(r, start, part), tiles(r, to + start, part), target, SECOND + r)

        second[r] = [send_part(0, BUNDLE, up_b), send_part(part, 2 * BUNDLE, down_b)]
        second[r] += [send_part(part, BUNDLE, up_b), send_part(0, 2 * BUNDLE, down_b)]
        swap[r] = [send(tiles(r, 0, BUNDLE), tiles(r, 0, BUNDLE), (sibling, dim), SWAP + r)]

    def second_pass(r):
        part = 2 * BLOCK
        second[r][0].wait_recv()
        up = send(tiles(r, BUNDLE, part), tiles(r, 3 * BUNDLE, part), up_b, SECOND + r)
        second[r][1].wait_recv()
        down = send(tiles(r, 2 * BUNDLE + part, part), tiles(r, 3 * BUNDLE + part, part), down_b, SECOND + r)
        passes[r] = (up, down)
        for copy in second[r][2:]:
            copy.wait_recv()
        ready = tiles(r, BUNDLE, 2 * BUNDLE)
        swap[r].append(send(ready, ready, (sibling, dim), SWAP + r))

    def second_end(r):
        part = 2 * BLOCK
        for k, copy in enumerate(passes[r]):
            copy.wait_recv()
            ready = tiles(r, 3 * BUNDLE + k * part, part)
            swap[r].append(send(ready, ready, (sibling, dim), SWAP + r))

    def convert(r, side, bundle, count=1):
        start = (core * HALF if side == 0 else (1 - core) * HALF) + bundle * BUNDLE

        def one(step, carry):
            for k in range(4):
                at = pl.ds(pl.multiple_of(step * 4 * SLOTS + k * SLOTS, SLOTS), SLOTS)
                total = jnp.zeros((SLOTS, LANES), F32)
                for q in range(4):
                    place = start + (step - bundle) * BUNDLE + k * BLOCK + q * QUARTER
                    value = cand[r][pl.ds(place, QUARTER)].reshape(SLOTS, LANES)
                    total += value * value
                    high = value.astype(BF16)
                    ch[r, side, at, q * LANES:(q + 1) * LANES] = high
                    cl[r, side, at, q * LANES:(q + 1) * LANES] = (value - high.astype(F32)).astype(BF16)
                norm = jnp.sum(total, axis=1, keepdims=True)
                nrm[r, side, at, :] = jnp.broadcast_to(norm, (SLOTS, LANES))
            return carry

        lax.fori_loop(bundle, bundle + count, one, 0)

    def prepare(t):
        for copy in near[t] + passed[t]:
            copy.wait_recv()
        at = slice(t % 2 * STEP, (t % 2 + 1) * STEP)
        total = jnp.zeros((LANES, STEP), F32)
        for q in range(4):
            value = xfull[q, t * STEP:(t + 1) * STEP, :].T
            total += value * value
            value = -2.0 * value
            high = value.astype(BF16)
            xh[t // 2, q * LANES:(q + 1) * LANES, at] = high
            xl[t // 2, q * LANES:(q + 1) * LANES, at] = (value - high.astype(F32)).astype(BF16)
        sq[t // 2, :, at] = jnp.sum(total.reshape(LANES // 8, 8, STEP), axis=0)

    def nearest(t, r, side):
        high, rows = ch[r, side], xh[t]
        value = jnp.dot(
            jnp.concatenate([high, cl[r, side], high], axis=1),
            jnp.concatenate([rows, rows, xl[t]], axis=0),
            preferred_element_type=F32,
        )
        value = value + jnp.concatenate([nrm[r, side]] * (WIDE // LANES), axis=1)
        low[t, r, side] = jnp.min(value.reshape(CORE_SLOTS // 8, 8, WIDE), axis=0)

    def nearest_both(t, r):
        high, rows = ch[r].reshape(2 * CORE_SLOTS, 512), xh[t]
        value = jnp.dot(
            jnp.concatenate([high, cl[r].reshape(2 * CORE_SLOTS, 512), high], axis=1),
            jnp.concatenate([rows, rows, xl[t]], axis=0),
            preferred_element_type=F32,
        )
        norm = nrm[r].reshape(2 * CORE_SLOTS, LANES)
        value = value + jnp.concatenate([norm] * (WIDE // LANES), axis=1)
        value = jnp.min(value.reshape(2 * CORE_SLOTS // 8, 8, WIDE), axis=0)
        low[t, r, 0] = value
        low[t, r, 1] = value

    def finish(t):
        norm = jnp.sum(sq[t], axis=0, keepdims=True)
        best = [
            jnp.min(jnp.minimum(low[t, r, 0], low[t, r, 1]), axis=0, keepdims=True) for r in range(ROUNDS)
        ]
        for r in range(1, ROUNDS):
            best[r] = jnp.minimum(best[r], best[r - 1])
        done[:, t * WIDE:(t + 1) * WIDE] = jnp.concatenate(
            [jnp.maximum(value + norm, 0.0) for value in best], axis=0
        )

    def many(count, body):
        def one(k, carry):
            body(k)
            return carry

        lax.fori_loop(0, count, one, 0)

    def other(r, step):
        for copy in (swap[r][0:1], swap[r][1:2], swap[r][2:4])[step]:
            copy.wait_recv()
        convert(r, 1, (0, 1, 3)[step], (1, 2, 1)[step])

    def all_sent():
        for r in range(ROUNDS):
            sent(cand[r].at[pl.ds(0, 3 * QUARTER)], PICK + r)
            sent(cand[r].at[pl.ds(0, 3 * BLOCK)], FIRST + r)
            sent(cand[r].at[pl.ds(0, 3 * BUNDLE)], SECOND + r)
            sent(cand[r].at[pl.ds(0, HALF)], SWAP + r)
        sent(xfull.at[pl.ds(0, 1)], RELAY)
        sent(xfull.at[pl.ds(0, 2)], NEAR)
        sent(xfull.at[pl.ds(0, 1)], PASSED)

    pick_send(0)
    pick_send(1)
    own_rows.start()
    far_send(0)
    pick_send(2)
    first_send(0)
    far_send(1)
    first_send(1)
    near_send(0)
    first_send(2)
    second_send(0)
    far_pass(0)
    convert(0, 0, 0)
    second_send(1)
    far_send(2)
    convert(1, 0, 0)
    near_send(1)
    far_send(3)
    far_pass(1)
    own_rows.wait()
    prepare(0)
    other(0, 0)
    second_pass(0)
    second_send(2)
    convert(0, 0, 1, 2)
    other(1, 0)
    second_pass(1)
    convert(1, 0, 1, 2)
    near_send(2)
    far_pass(2)
    second_end(0)
    far_pass(3)
    convert(0, 0, 3)
    convert(2, 0, 0)
    other(0, 1)
    near_send(3)
    prepare(1)
    second_pass(2)
    nearest(0, 0, 0)
    convert(2, 0, 1, 2)
    second_end(1)
    other(0, 2)
    nearest(0, 0, 1)
    convert(1, 0, 3)
    other(1, 1)
    other(2, 0)
    prepare(2)
    second_end(2)
    convert(2, 0, 3)
    other(1, 2)
    nearest_both(0, 1)
    other(2, 1)
    other(2, 2)
    nearest_both(0, 2)
    finish(0)
    prepare(3)
    many(ROUNDS, lambda r: nearest_both(1, r))
    finish(1)

    sums = sum([done[:, k * LANES:(k + 1) * LANES] for k in range(SHARE // LANES)])
    line = jnp.concatenate([sums, jnp.zeros((8 - ROUNDS, LANES), F32)], axis=0)
    for stage, (targets, landed) in enumerate(((line_devices, red_line), (plane_devices, red_plane))):
        part[stage] = line
        for k, target in enumerate(targets):
            pltpu.make_async_remote_copy(
                src_ref=part.at[stage], dst_ref=landed.at[k], send_sem=send_sem.at[COST + stage],
                recv_sem=cost_sem.at[stage], device_id=target, device_id_type=MESH,
            ).start()
        if stage == 0:
            all_sent()
        pltpu.make_async_copy(landed, landed, cost_sem.at[stage]).wait()
        line = line + jnp.sum(landed[...], axis=0)
    cost = jnp.sum(line, axis=1, keepdims=True)[:ROUNDS]
    out_ref[...] = jnp.minimum(CAP, TOTAL * done[...] / cost)
    sent(red_line, COST)
    sent(red_plane, COST + 1)


COPIES = ROUNDS * 16 + PIECES * 6
PICK, FIRST, SECOND, SWAP, RELAY, NEAR, PASSED, COST = 0, 3, 6, 9, 12, 13, 14, 15
ANY = pl.BlockSpec(memory_space=pl.ANY)


def local(embeddings, cand_index, cand_count):
    return pl.pallas_call(
        kernel,
        out_shape=jax.ShapeDtypeStruct((ROUNDS, SHARE), F32),
        in_specs=[ANY, ANY, ANY],
        out_specs=pl.BlockSpec(memory_space=pltpu.VMEM),
        scratch_shapes=[
            pltpu.SMEM((ROUNDS, SLOTS), jnp.int32),
            pltpu.SMEM((ROUNDS, ITEMS), jnp.int32),
            pltpu.VMEM((ROWS, LANES), F32),
            pltpu.VMEM((4, SHARE, LANES), F32),
            pltpu.VMEM((2, PIECES, STEP // 2, LANES), F32),
            *[pltpu.VMEM((ITEMS * BLOCK, TILE, LANES), F32)] * ROUNDS,
            pltpu.VMEM((ROUNDS, 2, CORE_SLOTS, 512), BF16),
            pltpu.VMEM((ROUNDS, 2, CORE_SLOTS, 512), BF16),
            pltpu.VMEM((ROUNDS, 2, CORE_SLOTS, LANES), F32),
            pltpu.VMEM((PAIRS, 512, WIDE), BF16),
            pltpu.VMEM((PAIRS, 512, WIDE), BF16),
            pltpu.VMEM((PAIRS, 8, WIDE), F32),
            pltpu.VMEM((PAIRS, ROUNDS, 2, 8, WIDE), F32),
            pltpu.VMEM((ROUNDS, SHARE), F32),
            pltpu.VMEM((2, 8, LANES), F32),
            pltpu.VMEM((7, 8, LANES), F32),
            pltpu.VMEM((15, 8, LANES), F32),
            pltpu.SemaphoreType.DMA((3 + LOADS,)),
            pltpu.SemaphoreType.DMA((COST + 2,)),
            pltpu.SemaphoreType.DMA((COPIES,)),
            pltpu.SemaphoreType.DMA((2,)),
        ],
        compiler_params=pltpu.CompilerParams(
            collective_id=0, has_side_effects=True, vmem_limit_bytes=56 * 1024 * 1024
        ),
    )(cand_index, cand_count, embeddings)


def solution(mesh):
    in_specs = (P("item", "dim"), P(None, "item"), P())
    out_specs = P(None, ("item", "dim"))
    return jax.shard_map(local, mesh=mesh, in_specs=in_specs, out_specs=out_specs, check_vma=False)
```
